32 devices in a mesh: section: 4 (over y, x), seq: 4 (over z), mp: 2 (over core).
Axes of the slice: x: 2, y: 2, z: 4, core: 2. Of those that a mesh axis runs over, the one named last changes fastest.
Arguments:
- query_rows: bfloat16 [4, 512, 2048], P('section', 'seq', 'mp'), may hold values from -150 to 150
- key_row_matrix: bfloat16 [4, 512, 1024], P('section', 'seq', 'mp'), may hold values from -13 to 13
- value_row_matrix: bfloat16 [4, 512, 1024], P('section', 'seq', 'mp'), may hold values from -6 to 6
- out_grad: bfloat16 [4, 512, 2048], P('section', 'seq', 'mp'), may hold values from -24 to 24
- w_query: bfloat16 [4, 5376, 2048], P('section', 'seq', 'mp'), may hold values from -0.078125 to 0.078125
- key_weight: bfloat16 [4, 5376, 1024], P('section', 'seq', 'mp'), may hold values from -0.078125 to 0.078125
- value_weight: bfloat16 [4, 5376, 1024], P('section', 'seq', 'mp'), may hold values from -0.078125 to 0.078125
- doc_ids: int32 [4, 512], P('section'), may hold values from 0 to 5, never falling along the last dimension, each value on 1 to 170 neighbouring positions
Outputs:
- upstream: bfloat16 [4, 512, 5376], P('section', None, ('seq', 'mp'))
The draws below stay inside these ranges and needn't reach their ends.
All inputs are finite; a program needn't handle non-finite values.
Results may differ from the reference program's by a relative error of at most 0.0071.
Values may be sent and summed in bfloat16 or wider, within the bound.
No kernel may reach another device: no remote copies, remote signals or barrier semaphores. Data moves between devices by JAX's collectives and lax.ppermute only.
A program may use at most 64 MiB of HBM per device.

```python
import math
import jax
import jax.numpy as jnp
import numpy as np
from jax import lax

MODEL_WIDTH = 5376
QUERY_HEADS = 16
KEY_VALUE_HEADS = 8
HEAD_WIDTH = 128
WINDOW = 512
DOCS = 6
CASCADE_PARTS = 4
BATCH_TOKENS = 512
DOC_MOST = 170


def make_pair(key):
    key_base = jax.random.fold_in(key, 101)
    key_scale = jax.random.fold_in(key, 102)
    query_base = jax.random.fold_in(key, 103)
    query_scale = jax.random.fold_in(key, 104)
    key_rows_shaped = (CASCADE_PARTS, BATCH_TOKENS, KEY_VALUE_HEADS * HEAD_WIDTH)
    base_keys = jnp.clip(jax.random.normal(key_base, key_rows_shaped, jnp.float32), -4.0, 4.0)
    row_scale = jnp.exp(jax.random.uniform(key_scale, (CASCADE_PARTS, BATCH_TOKENS, 1), jnp.float32, -1.15, 1.15))
    base_queries = jnp.clip(jax.random.normal(query_base, (CASCADE_PARTS, BATCH_TOKENS, QUERY_HEADS * HEAD_WIDTH), jnp.float32), -4.0, 4.0)
    base_queries = base_queries * jnp.exp(jax.random.uniform(query_scale, (CASCADE_PARTS, BATCH_TOKENS, 1), jnp.float32, -1.15, 1.15))
    key_rows_scaled = base_keys * row_scale
    queries = base_queries
    return (queries, key_rows_scaled)


def draw_query_rows(key, part):
    return make_pair(key)[0].astype(jnp.bfloat16)


def draw_key_row_matrix(key, part):
    return make_pair(key)[1].astype(jnp.bfloat16)


def shard_levels(key, extent, split, low, top_value):
    def one(dim, shards_of):
        steps = jax.random.uniform(jax.random.fold_in(jax.random.fold_in(key, 6), dim), (shards_of,), jnp.float32, low / len(split), top_value / len(split))
        return jnp.repeat(jnp.exp(steps), extent[dim] // shards_of).reshape((-1,) + (1,) * (len(extent) - dim - 1))

    gain = one(*split[0])
    for cut in split[1:]:
        gain = gain * one(*cut)
    return gain


def length_profile(count, total, bound, skew):
    portions = [(1 << 20) // math.isqrt(standing ** skew) + 1 for standing in range(2, count + 1)]
    surplus, given = total - bound - (count - 1), [1] * (count - 1)
    while surplus > 0:
        candidates = [i for i in range(count - 1) if given[i] < bound]
        mass, budget = sum([portions[i] for i in candidates]), surplus
        for i in candidates:
            more = min(bound - given[i], max(1, budget * portions[i] // mass), surplus)
            given[i] = given[i] + more
            surplus = surplus - more
    return np.array([bound] + given)


def ragged(rng, count, total, reach, slope):
    if count == 2:
        one = jax.random.randint(rng, (), max(1, total - reach), min(reach, total - 1) + 1)
        return jnp.stack([one, total - one])
    sizes = jnp.asarray(length_profile(count, total, reach, slope), jnp.int32)
    pairs = (count - 1) // 2
    giver, receiver = sizes[1:1 + 2 * pairs:2], sizes[2:2 + 2 * pairs:2]
    room = jnp.minimum(giver - 1, reach - receiver)
    shifted = jax.random.randint(jax.random.fold_in(rng, 1), (pairs,), 0, 1 << 20) % (room + 1)
    sizes = sizes.at[1:1 + 2 * pairs:2].set(giver - shifted).at[2:2 + 2 * pairs:2].set(receiver + shifted)
    return sizes[jax.random.permutation(jax.random.fold_in(rng, 2), count)]


def noise(own_key, extent, spread, bound, split=(), held_as=jnp.bfloat16):
    values = jax.random.normal(own_key, extent, jnp.float32) * spread
    if len(split) > 0:
        values = shard_levels(own_key, extent, split, -0.22, 0.18) * values
    return jnp.clip(values, min=-bound, max=bound).astype(held_as)


def setup_inputs(seed: int = 0) -> dict:
    key_list = jax.random.split(jax.random.key(seed), 9)
    query_rows = draw_query_rows(jax.random.fold_in(key_list[8], 71), 0)
    key_row_matrix = draw_key_row_matrix(jax.random.fold_in(key_list[8], 71), 0)
    value_row_matrix = noise(key_list[2], (CASCADE_PARTS, BATCH_TOKENS, KEY_VALUE_HEADS * HEAD_WIDTH), 1.0, 6.0, ((0, 4), (1, 4), (2, 2)))
    out_grad = noise(key_list[3], (CASCADE_PARTS, BATCH_TOKENS, QUERY_HEADS * HEAD_WIDTH), 4.0, 24.0, ((0, 4), (1, 4), (2, 2)))
    w_query = noise(key_list[4], (CASCADE_PARTS, MODEL_WIDTH, QUERY_HEADS * HEAD_WIDTH), MODEL_WIDTH ** -0.5, 0.078125, ((0, 4), (1, 4), (2, 2)))
    key_weight = noise(key_list[5], (CASCADE_PARTS, MODEL_WIDTH, KEY_VALUE_HEADS * HEAD_WIDTH), MODEL_WIDTH ** -0.5, 0.078125, ((0, 4), (1, 4), (2, 2)))
    value_weight = noise(key_list[6], (CASCADE_PARTS, MODEL_WIDTH, KEY_VALUE_HEADS * HEAD_WIDTH), MODEL_WIDTH ** -0.5, 0.078125, ((0, 4), (1, 4), (2, 2)))
    doc_ids = jax.vmap(lambda own: jnp.searchsorted(jnp.cumsum(ragged(own, DOCS, BATCH_TOKENS, DOC_MOST, 1)), jnp.arange(BATCH_TOKENS), side="right"))(jax.random.split(key_list[7], CASCADE_PARTS)).reshape((CASCADE_PARTS, BATCH_TOKENS)).astype(jnp.int32)
    return dict(query_rows=query_rows, key_row_matrix=key_row_matrix, value_row_matrix=value_row_matrix, out_grad=out_grad, w_query=w_query, key_weight=key_weight, value_weight=value_weight, doc_ids=doc_ids)


def section_backward(query_rows, key_row_matrix, value_row_matrix, out_grad, w_query, key_weight, value_weight, doc_ids):
    group_width = QUERY_HEADS // KEY_VALUE_HEADS
    scaling = 1.0 / math.sqrt(HEAD_WIDTH)
    position = jnp.arange(BATCH_TOKENS, dtype=jnp.int32)
    offset = position[:, None] - position[None, :]
    allowed = (doc_ids[:, None] == doc_ids[None, :]) & (offset >= 0) & (offset < WINDOW)
    query_heads = query_rows.reshape(BATCH_TOKENS, QUERY_HEADS, HEAD_WIDTH).transpose(1, 0, 2)
    key_head_rows = key_row_matrix.reshape(BATCH_TOKENS, KEY_VALUE_HEADS, HEAD_WIDTH).transpose(1, 0, 2)
    value_head_rows = value_row_matrix.reshape(BATCH_TOKENS, KEY_VALUE_HEADS, HEAD_WIDTH).transpose(1, 0, 2)
    grad_heads = out_grad.reshape(BATCH_TOKENS, QUERY_HEADS, HEAD_WIDTH).transpose(1, 0, 2)

    def one_head(head_index):
        query_now = query_heads[head_index]
        key_now = key_head_rows[head_index // group_width]
        value_now = value_head_rows[head_index // group_width]
        grad_now = grad_heads[head_index]
        scores = jnp.dot(query_now, key_now.T, preferred_element_type=jnp.float32) * scaling
        scores = jnp.where(allowed, scores, -jnp.inf)
        row_max = lax.optimization_barrier(jnp.max(scores, axis=1, keepdims=True))
        raised = jnp.exp(scores - row_max)
        weights_full = raised / lax.optimization_barrier(jnp.sum(raised, axis=1, keepdims=True))
        weights_half = weights_full.astype(jnp.bfloat16)
        attended = jnp.dot(weights_half, value_now, preferred_element_type=jnp.float32)
        delta_row = lax.optimization_barrier(jnp.sum(grad_now.astype(jnp.float32) * attended, axis=1))
        grad_weights = jnp.dot(grad_now, value_now.T, preferred_element_type=jnp.float32)
        grad_scores = (weights_full * (grad_weights - delta_row[:, None])).astype(jnp.bfloat16)
        grad_query = (jnp.dot(grad_scores, key_now, preferred_element_type=jnp.float32) * scaling).astype(jnp.bfloat16)
        key_gradient = jnp.dot(grad_scores.T, query_now, preferred_element_type=jnp.float32) * scaling
        value_gradient = jnp.dot(weights_half.T, grad_now, preferred_element_type=jnp.float32)
        return (grad_query, key_gradient, value_gradient)
    grad_query, key_gradient, value_gradient = lax.map(one_head, jnp.arange(QUERY_HEADS, dtype=jnp.int32))
    key_gradient = key_gradient.reshape(KEY_VALUE_HEADS, group_width, BATCH_TOKENS, HEAD_WIDTH).sum(axis=1).astype(jnp.bfloat16)
    value_gradient = value_gradient.reshape(KEY_VALUE_HEADS, group_width, BATCH_TOKENS, HEAD_WIDTH).sum(axis=1).astype(jnp.bfloat16)
    query_cols = grad_query.transpose(1, 0, 2).reshape(BATCH_TOKENS, QUERY_HEADS * HEAD_WIDTH)
    key_columns = key_gradient.transpose(1, 0, 2).reshape(BATCH_TOKENS, KEY_VALUE_HEADS * HEAD_WIDTH)
    value_columns = value_gradient.transpose(1, 0, 2).reshape(BATCH_TOKENS, KEY_VALUE_HEADS * HEAD_WIDTH)
    grad_matrix = jnp.concatenate([query_cols, key_columns, value_columns], axis=1)
    weights_all = jnp.concatenate([w_query, key_weight, value_weight], axis=1)
    product = lax.dot_general(grad_matrix, weights_all, (((1,), (1,)), ((), ())), preferred_element_type=jnp.float32)
    return product.astype(jnp.bfloat16)

def reference(query_rows, key_row_matrix, value_row_matrix, out_grad, w_query, key_weight, value_weight, doc_ids):

    def per_section(section_inputs):
        return section_backward(section_inputs[0], section_inputs[1], section_inputs[2], section_inputs[3], section_inputs[4], section_inputs[5], section_inputs[6], section_inputs[7])
    grad_input = lax.map(per_section, (query_rows, key_row_matrix, value_row_matrix, out_grad, w_query, key_weight, value_weight, doc_ids))
    return jnp.roll(grad_input, -1, axis=0)
```

```python
import functools
import math

import jax
import jax.numpy as jnp
from jax import lax
from jax.experimental import pallas as pl
from jax.experimental.pallas import tpu as pltpu
from jax.sharding import PartitionSpec as P

HEAD_WIDTH = 128
WINDOW = 512
MASKED = -1e30


def dot(left, right, left_dim, right_dim):
    return lax.dot_general(
        left,
        right,
        (((left_dim,), (right_dim,)), ((), ())),
        preferred_element_type=jnp.float32,
    )


def attention_kernel(kv_heads, group_width, halo_rows, *refs):
    halo_count = len(halo_rows)
    query_ref, grad_ref, kv_ref, bias_ref = refs[:4]
    halo_refs = refs[4 : 4 + halo_count]
    grad_query_ref, grad_kv_ref = refs[4 + halo_count : 6 + halo_count]
    grad_halo_refs = refs[6 + halo_count :]
    rows = query_ref.shape[0]
    kv_cols = kv_heads * HEAD_WIDTH
    scaling = 1.0 / math.sqrt(HEAD_WIDTH)
    bias = jnp.concatenate([bias_ref[...]] * group_width, axis=1)
    for group in range(kv_heads):
        heads = [group * group_width + member for member in range(group_width)]
        query = jnp.concatenate(
            [query_ref[:, h * HEAD_WIDTH : (h + 1) * HEAD_WIDTH] for h in heads], axis=0
        )
        grad = jnp.concatenate(
            [grad_ref[:, h * HEAD_WIDTH : (h + 1) * HEAD_WIDTH] for h in heads], axis=0
        )
        key_cols = slice(group * HEAD_WIDTH, (group + 1) * HEAD_WIDTH)
        value_cols = slice(kv_cols + group * HEAD_WIDTH, kv_cols + (group + 1) * HEAD_WIDTH)
        blocks = [*halo_refs, kv_ref]
        key = jnp.concatenate([block[:, key_cols] for block in blocks], axis=0)
        value = jnp.concatenate([block[:, value_cols] for block in blocks], axis=0)
        scores = dot(key, query, 1, 1) * scaling + bias
        raised = jnp.exp(scores - jnp.max(scores, axis=0, keepdims=True))
        weights = raised * (1.0 / jnp.sum(raised, axis=0, keepdims=True))
        weights_half = weights.astype(jnp.bfloat16)
        grad_weights = dot(value, grad, 1, 1)
        delta = jnp.sum(weights_half.astype(jnp.float32) * grad_weights, axis=0, keepdims=True)
        grad_scores = (weights * (grad_weights - delta)).astype(jnp.bfloat16)
        grad_query = (dot(grad_scores, key, 0, 0) * scaling).astype(jnp.bfloat16)
        for member, h in enumerate(heads):
            grad_query_ref[:, h * HEAD_WIDTH : (h + 1) * HEAD_WIDTH] = grad_query[
                member * rows : (member + 1) * rows
            ]
        grad_key = dot(grad_scores, query, 1, 0) * scaling
        grad_value = dot(weights_half, grad, 1, 0)
        start = 0
        for size, out_ref in zip([*halo_rows, rows], [*grad_halo_refs, grad_kv_ref]):
            out_ref[:, key_cols] = grad_key[start : start + size].astype(out_ref.dtype)
            out_ref[:, value_cols] = grad_value[start : start + size].astype(out_ref.dtype)
            start += size


def attention_backward(query, grad, kv, bias, halos):
    rows, query_cols = query.shape
    kv_cols = kv.shape[1] // 2
    kv_heads = kv_cols // HEAD_WIDTH
    group_width = query_cols // kv_cols
    halo_rows = [halo.shape[0] for halo in halos]
    span = bias.shape[0]
    whole = pl.BlockSpec(memory_space=pltpu.VMEM)
    outs = [
        jax.ShapeDtypeStruct((rows, query_cols), jnp.bfloat16),
        jax.ShapeDtypeStruct((rows, 2 * kv_cols), jnp.float32),
        *[jax.ShapeDtypeStruct((size, 2 * kv_cols), jnp.bfloat16) for size in halo_rows],
    ]
    return pl.pallas_call(
        functools.partial(attention_kernel, kv_heads, group_width, halo_rows),
        out_shape=outs,
        in_specs=[whole] * (4 + len(halos)),
        out_specs=[whole] * len(outs),
        compiler_params=pltpu.CompilerParams(vmem_limit_bytes=32 * 1024 * 1024),
        cost_estimate=pl.CostEstimate(
            flops=12 * rows * span * query_cols,
            bytes_accessed=4 * rows * query_cols * 2,
            transcendentals=rows * span * kv_heads * group_width,
        ),
    )(query, grad, kv, bias, *halos)


def moved(block, axis, by, first=0):
    size = lax.axis_size(axis)
    if by > 0:
        sources = range(first, size - by)
    else:
        sources = range(-by, size - first)
    return lax.ppermute(block, axis, [(i, i + by) for i in sources])


def passed_along(block, axis, distance):
    devices = range(lax.axis_size(axis))
    return lax.ppermute(block, axis, [((i - distance) % len(devices), i) for i in devices])


def per_device(
    query_rows,
    key_row_matrix,
    value_row_matrix,
    out_grad,
    w_query,
    key_weight,
    value_weight,
    doc_ids,
):
    documents = doc_ids[0]
    tokens = documents.shape[0]
    rows = query_rows.shape[1]
    kv_cols = key_row_matrix.shape[2]
    shards = lax.axis_size("seq")
    place = lax.axis_index("seq")
    core = lax.axis_index("mp")
    back = min(WINDOW, tokens // 3) - 1
    halo_rows = []
    while sum(halo_rows) < back and len(halo_rows) < shards - 1:
        halo_rows.append(min(rows, -(-(back - sum(halo_rows)) // 16) * 16))
    kv = jnp.concatenate([key_row_matrix[0], value_row_matrix[0]], axis=1)
    halos = [moved(kv[rows - size :], "seq", d) for d, size in enumerate(halo_rows, 1)]
    reach = sum(halo_rows)
    first_row = place * rows
    key_docs = lax.dynamic_slice_in_dim(
        jnp.concatenate([jnp.full((reach,), -1, jnp.int32), documents]), first_row, reach + rows, 0
    )
    query_docs = lax.dynamic_slice_in_dim(documents, first_row, rows, 0)
    offset = (
        jnp.arange(rows, dtype=jnp.int32)[None, :]
        + reach
        - jnp.arange(reach + rows, dtype=jnp.int32)[:, None]
    )
    allowed = (query_docs[None, :] == key_docs[:, None]) & (offset >= 0) & (offset < WINDOW)
    bias = jnp.where(allowed, 0.0, MASKED).astype(jnp.float32)
    grad_query, grad_kv, *grad_halos = attention_backward(
        query_rows[0], out_grad[0], kv, bias, halos[::-1]
    )
    for d, part in enumerate(grad_halos[::-1], 1):
        part = moved(part, "seq", -d).astype(jnp.float32)
        grad_kv = grad_kv + jnp.pad(part, ((rows - part.shape[0], 0), (0, 0)))
    grad_kv = grad_kv.astype(jnp.bfloat16)

    def chain(piece):
        up, down = piece, piece
        arrived = []
        for step in range(1, shards):
            if 2 * step > shards + 1:
                both = [(i, i + 1) for i in range(step - 1, shards - 1)]
                both += [(i, i - 1) for i in range(1, shards - step + 1)]
                up = down = lax.ppermute(up, "seq", both)
                arrived.append([up])
                continue
            up = moved(up, "seq", 1, step - 1)
            down = moved(down, "seq", -1, step - 1)
            if 2 * step >= shards:
                up = down = jnp.where(place >= step, up, down)
                arrived.append([up])
            else:
                arrived.append([up, down])
        return arrived

    def finished(query_part, kv_part):
        partial = (
            dot(query_part, w_query[0], 1, 1)
            + dot(kv_part[:, :kv_cols], key_weight[0], 1, 1)
            + dot(kv_part[:, kv_cols:], value_weight[0], 1, 1)
        )
        half = partial.shape[1] // 2
        low, high = partial[:, :half], partial[:, half:]
        keep = jnp.where(core == 0, low, high)
        give = jnp.where(core == 0, high, low).astype(jnp.bfloat16)
        got = passed_along(give, "mp", 1)
        total = (keep + got.astype(jnp.float32)).astype(jnp.bfloat16)
        return passed_along(total, "section", -1)

    query_steps, kv_steps = chain(grad_query), chain(grad_kv)
    results = [[finished(grad_query, grad_kv)]]
    for query_parts, kv_parts in zip(query_steps, kv_steps):
        if len(query_parts) == 1:
            results.append([finished(query_parts[0], kv_parts[0])])
        else:
            joined = finished(
                jnp.concatenate(query_parts, axis=0), jnp.concatenate(kv_parts, axis=0)
            )
            results.append([joined[:rows], joined[rows:]])
    upstream = jnp.zeros((tokens, results[0][0].shape[1]), jnp.bfloat16)
    for s in range(shards):
        behind = results[s][0]
        ahead = results[(shards - s) % shards][-1]
        block = jnp.where(place >= s, behind, ahead)
        upstream = lax.dynamic_update_slice_in_dim(
            upstream, block, ((place - s) % shards) * rows, 0
        )
    return upstream[None]


def solution(mesh):
    placed = P("section", "seq", "mp")
    return jax.shard_map(
        per_device,
        mesh=mesh,
        in_specs=(placed,) * 7 + (P("section", None),),
        out_specs=P("section", None, ("seq", "mp")),
        check_vma=False,
    )
```

```python
import functools
import math

import jax
import jax.numpy as jnp
from jax import lax
from jax.experimental import pallas as pl
from jax.experimental.pallas import tpu as pltpu
from jax.sharding import PartitionSpec as P

HEAD_WIDTH = 128
WINDOW = 512
MASKED = -1e30


def dot(left, right, left_dim, right_dim):
    return lax.dot_general(
        left,
        right,
        (((left_dim,), (right_dim,)), ((), ())),
        preferred_element_type=jnp.float32,
    )


def attention_kernel(kv_heads, group_width, halo_rows, *refs):
    halo_count = len(halo_rows)
    query_ref, grad_ref, kv_ref, bias_ref = refs[:4]
    halo_refs = refs[4 : 4 + halo_count]
    grad_query_ref, grad_kv_ref = refs[4 + halo_count : 6 + halo_count]
    grad_halo_refs = refs[6 + halo_count :]
    rows = query_ref.shape[0]
    kv_cols = kv_heads * HEAD_WIDTH
    scaling = 1.0 / math.sqrt(HEAD_WIDTH)
    bias = jnp.concatenate([bias_ref[...]] * group_width, axis=1)
    for group in range(kv_heads):
        heads = [group * group_width + member for member in range(group_width)]
        query = jnp.concatenate(
            [query_ref[:, h * HEAD_WIDTH : (h + 1) * HEAD_WIDTH] for h in heads], axis=0
        )
        grad = jnp.concatenate(
            [grad_ref[:, h * HEAD_WIDTH : (h + 1) * HEAD_WIDTH] for h in heads], axis=0
        )
        key_cols = slice(group * HEAD_WIDTH, (group + 1) * HEAD_WIDTH)
        value_cols = slice(kv_cols + group * HEAD_WIDTH, kv_cols + (group + 1) * HEAD_WIDTH)
        blocks = [*halo_refs, kv_ref]
        key = jnp.concatenate([block[:, key_cols] for block in blocks], axis=0)
        value = jnp.concatenate([block[:, value_cols] for block in blocks], axis=0)
        scores = dot(key, query, 1, 1) * scaling + bias
        raised = jnp.exp(scores - jnp.max(scores, axis=0, keepdims=True))
        weights = raised * (1.0 / jnp.sum(raised, axis=0, keepdims=True))
        weights_half = weights.astype(jnp.bfloat16)
        grad_weights = dot(value, grad, 1, 1)
        delta = jnp.sum(weights_half.astype(jnp.float32) * grad_weights, axis=0, keepdims=True)
        grad_scores = (weights * (grad_weights - delta)).astype(jnp.bfloat16)
        grad_query = (dot(grad_scores, key, 0, 0) * scaling).astype(jnp.bfloat16)
        for member, h in enumerate(heads):
            grad_query_ref[:, h * HEAD_WIDTH : (h + 1) * HEAD_WIDTH] = grad_query[
                member * rows : (member + 1) * rows
            ]
        grad_key = dot(grad_scores, query, 1, 0) * scaling
        grad_value = dot(weights_half, grad, 1, 0)
        start = 0
        for size, out_ref in zip([*halo_rows, rows], [*grad_halo_refs, grad_kv_ref]):
            out_ref[:, key_cols] = grad_key[start : start + size].astype(out_ref.dtype)
            out_ref[:, value_cols] = grad_value[start : start + size].astype(out_ref.dtype)
            start += size


def attention_backward(query, grad, kv, bias, halos):
    rows, query_cols = query.shape
    kv_cols = kv.shape[1] // 2
    kv_heads = kv_cols // HEAD_WIDTH
    group_width = query_cols // kv_cols
    halo_rows = [halo.shape[0] for halo in halos]
    span = bias.shape[0]
    whole = pl.BlockSpec(memory_space=pltpu.VMEM)
    outs = [
        jax.ShapeDtypeStruct((rows, query_cols), jnp.bfloat16),
        jax.ShapeDtypeStruct((rows, 2 * kv_cols), jnp.float32),
        *[jax.ShapeDtypeStruct((size, 2 * kv_cols), jnp.bfloat16) for size in halo_rows],
    ]
    return pl.pallas_call(
        functools.partial(attention_kernel, kv_heads, group_width, halo_rows),
        out_shape=outs,
        in_specs=[pl.BlockSpec()] * 2 + [whole] * (2 + len(halos)),
        out_specs=[whole] * len(outs),
        compiler_params=pltpu.CompilerParams(vmem_limit_bytes=8 * 1024 * 1024),
        cost_estimate=pl.CostEstimate(
            flops=12 * rows * span * query_cols,
            bytes_accessed=4 * rows * query_cols * 2,
            transcendentals=rows * span * kv_heads * group_width,
        ),
    )(query, grad, kv, bias, *halos)


def join_kernel(query_ref, kv_ref, *refs):
    *part_refs, joined_ref, total_ref = refs
    rows = kv_ref.shape[0]
    query_cols = query_ref.shape[1]
    joined_ref[:, :query_cols] = query_ref[...]
    total = kv_ref[...]
    for part_ref in part_refs:
        size = part_ref.shape[0]
        part = part_ref[...].astype(jnp.float32)
        if size < rows:
            part = jnp.concatenate(
                [jnp.zeros((rows - size, part.shape[1]), jnp.float32), part], axis=0
            )
        total = total + part
    total = total.astype(jnp.bfloat16)
    joined_ref[:, query_cols:] = total
    total_ref[...] = total


def join(query_part, kv_part, returned):
    rows, query_cols = query_part.shape
    kv_cols = kv_part.shape[1]
    whole = pl.BlockSpec(memory_space=pltpu.VMEM)
    return pl.pallas_call(
        join_kernel,
        out_shape=[
            jax.ShapeDtypeStruct((rows, query_cols + kv_cols), jnp.bfloat16),
            jax.ShapeDtypeStruct((rows, kv_cols), jnp.bfloat16),
        ],
        in_specs=[whole] * (2 + len(returned)),
        out_specs=[whole] * 2,
        compiler_params=pltpu.CompilerParams(vmem_limit_bytes=8 * 1024 * 1024),
        cost_estimate=pl.CostEstimate(flops=1, bytes_accessed=1, transcendentals=0),
    )(query_part, kv_part, *returned)


def project_kernel(pieces, tile, core_ref, *refs):
    flat_refs, (query_weight, key_weight, value_weight) = refs[: sum(pieces)], refs[-6:-3]
    full_ref, give_ref, block_ref = refs[-3:]
    row, at = 0, 0
    for count in pieces:
        column = 0
        for ref in flat_refs[at : at + count]:
            block_ref[row : row + ref.shape[0], column : column + ref.shape[1]] = ref[...]
            column += ref.shape[1]
        at += count
        row += flat_refs[at - 1].shape[0]
    query_cols, kv_cols = query_weight.shape[1], key_weight.shape[1]

    def step(i, carry):
        at = pl.ds(pl.multiple_of(i * tile, 16), tile)
        full_ref[at, :] = (
            dot(query_weight[at, :], block_ref[:, :query_cols], 1, 1)
            + dot(key_weight[at, :], block_ref[:, query_cols : query_cols + kv_cols], 1, 1)
            + dot(value_weight[at, :], block_ref[:, query_cols + kv_cols :], 1, 1)
        )
        return carry

    lax.fori_loop(0, full_ref.shape[0] // tile, step, 0)
    half = give_ref.shape[0]
    other = pl.multiple_of((1 - core_ref[0]) * half, 8)
    give_ref[...] = full_ref[pl.ds(other, half), :].astype(jnp.bfloat16)


def project(blocks, weights, core):
    width = weights[0].shape[0]
    rows = sum(block[0].shape[0] for block in blocks)
    cols = sum(weight.shape[1] for weight in weights)
    tile = max(t for t in range(16, 449, 16) if width % t == 0)
    flat = [piece for block in blocks for piece in block]
    whole = pl.BlockSpec(memory_space=pltpu.VMEM)
    return pl.pallas_call(
        functools.partial(project_kernel, [len(block) for block in blocks], tile),
        out_shape=[
            jax.ShapeDtypeStruct((width, rows), jnp.float32),
            jax.ShapeDtypeStruct((width // 2, rows), jnp.bfloat16),
        ],
        in_specs=[pl.BlockSpec(memory_space=pltpu.SMEM)] + [whole] * (len(flat) + 3),
        out_specs=[whole] * 2,
        scratch_shapes=[pltpu.VMEM((rows, cols), jnp.bfloat16)],
        compiler_params=pltpu.CompilerParams(vmem_limit_bytes=8 * 1024 * 1024),
        cost_estimate=pl.CostEstimate(flops=1, bytes_accessed=1, transcendentals=0),
    )(core, *flat, *weights)


def moved(block, axis, by, first=0):
    size = lax.axis_size(axis)
    if by > 0:
        sources = range(first, size - by)
    else:
        sources = range(-by, size - first)
    return lax.ppermute(block, axis, [(i, i + by) for i in sources])


def after(arrays, *others):
    return lax.optimization_barrier((*arrays, *others))[: len(arrays)]


def passed_along(block, axis, distance):
    devices = range(lax.axis_size(axis))
    return lax.ppermute(block, axis, [((i - distance) % len(devices), i) for i in devices])


def per_device(
    query_rows,
    key_row_matrix,
    value_row_matrix,
    out_grad,
    w_query,
    key_weight,
    value_weight,
    doc_ids,
):
    documents = doc_ids[0]
    tokens = documents.shape[0]
    rows = query_rows.shape[1]
    kv_cols = key_row_matrix.shape[2]
    shards = lax.axis_size("seq")
    place = lax.axis_index("seq")
    back = min(WINDOW, tokens // 3) - 1
    halo_rows = []
    while sum(halo_rows) < back and len(halo_rows) < shards - 1:
        halo_rows.append(min(rows, -(-(back - sum(halo_rows)) // 16) * 16))
    kv = lax.optimization_barrier(
        jnp.concatenate([key_row_matrix[0], value_row_matrix[0]], axis=1)
    )
    halos = [moved(kv[rows - size :], "seq", d) for d, size in enumerate(halo_rows, 1)]
    reach = sum(halo_rows)
    first_row = place * rows
    key_docs = lax.dynamic_slice_in_dim(
        jnp.concatenate([jnp.full((reach,), -1, jnp.int32), documents]), first_row, reach + rows, 0
    )
    query_docs = lax.dynamic_slice_in_dim(documents, first_row, rows, 0)
    offset = (
        jnp.arange(rows, dtype=jnp.int32)[None, :]
        + reach
        - jnp.arange(reach + rows, dtype=jnp.int32)[:, None]
    )
    allowed = (query_docs[None, :] == key_docs[:, None]) & (offset >= 0) & (offset < WINDOW)
    bias = jnp.where(allowed, 0.0, MASKED).astype(jnp.float32)
    grad_query, grad_kv, *grad_halos = attention_backward(
        query_rows[0], out_grad[0], kv, bias, halos[::-1]
    )
    returned = [moved(part, "seq", -d) for d, part in enumerate(grad_halos[::-1], 1)]
    query_up = moved(grad_query, "seq", 1)
    held, *returned = after((grad_query, *returned), query_up)
    own, kv_up = join(held, grad_kv, returned)
    down = own
    weights = (w_query[0], key_weight[0], value_weight[0])
    core = lax.axis_index("mp").astype(jnp.int32)

    def halves_summed(blocks):
        full, give = project(blocks, weights, core[None])
        half = give.shape[0]
        keep = lax.dynamic_slice_in_dim(full, core * half, half, 0)
        got = passed_along(give, "mp", 1)
        return give, (keep + got.astype(jnp.float32)).astype(jnp.bfloat16)

    results, waiting = [], [[own]]
    for step in range(1, shards):
        if 2 * step > shards + 1:
            both = [(i, i + 1) for i in range(step - 1, shards - 1)]
            both += [(i, i - 1) for i in range(1, shards - step + 1)]
            down = lax.ppermute(down, "seq", both)
            arrived = [[down]]
            early = None
        else:
            if step > 1:
                query_up = moved(query_up, "seq", 1, step - 1)
            kv_up = moved(kv_up, "seq", 1, step - 1)
            down = moved(down, "seq", -1, step - 1)
            arrived = [[query_up, kv_up], [down]]
            early = kv_up if step == 1 else query_up
            if 2 * step >= shards:
                up = jnp.concatenate([query_up, kv_up], axis=1)
                down = jnp.where(place >= step, up, down)
                arrived = [[down]]
        others = [] if early is None else [early]
        if step == 2:
            others.append(total)
        elif step > 2:
            others += [results[step - 3], total]
        if others:
            waiting = [after(tuple(block), *others) for block in waiting]
        give, total = halves_summed(waiting)
        if 2 * step <= shards + 1:
            (down,) = after((down,), give)
        results.append(passed_along(total, "section", -1))
        waiting = arrived
        if 2 * step >= shards:
            waiting = [[down]]
    last = tuple(waiting[0])
    if shards > 1:
        last = after(last, total, *results[:-1])
    total = halves_summed([last, *waiting[1:]])[1]
    if shards > 1:
        (total,) = after((total,), results[-1])
    results.append(passed_along(total, "section", -1))
    results = [
        [block[:, i * rows : (i + 1) * rows] for i in range(block.shape[1] // rows)]
        for block in results
    ]
    upstream = jnp.zeros((results[0][0].shape[0], tokens), jnp.bfloat16)
    for s in range(shards):
        behind = results[s][0]
        ahead = results[(shards - s) % shards][-1]
        block = jnp.where(place >= s, behind, ahead)
        upstream = lax.dynamic_update_slice_in_dim(
            upstream, block, ((place - s) % shards) * rows, 1
        )
    return upstream.T[None]


def solution(mesh):
    placed = P("section", "seq", "mp")
    return jax.shard_map(
        per_device,
        mesh=mesh,
        in_specs=(placed,) * 7 + (P("section", None),),
        out_specs=P("section", None, ("seq", "mp")),
        check_vma=False,
    )
```

```python
import functools
import math

import jax
import jax.numpy as jnp
from jax import lax
from jax.experimental import pallas as pl
from jax.experimental.pallas import tpu as pltpu
from jax.sharding import PartitionSpec as P

HEAD_WIDTH = 128
WINDOW = 512
MASKED = -1e30


def dot(left, right, left_dim, right_dim):
    return lax.dot_general(
        left,
        right,
        (((left_dim,), (right_dim,)), ((), ())),
        preferred_element_type=jnp.float32,
    )


def stack_kernel(kv_heads, group_width, query_ref, grad_ref, query_out, grad_out):
    rows = query_ref.shape[0]
    for head in range(kv_heads * group_width):
        cols = slice(head * HEAD_WIDTH, (head + 1) * HEAD_WIDTH)
        query_out[head * rows : (head + 1) * rows, :] = query_ref[:, cols]
        grad_out[head * rows : (head + 1) * rows, :] = grad_ref[:, cols]


def stack(query, grad, kv_heads, group_width):
    rows, query_cols = query.shape
    whole = pl.BlockSpec(memory_space=pltpu.VMEM)
    shape = jax.ShapeDtypeStruct((rows * kv_heads * group_width, HEAD_WIDTH), jnp.bfloat16)
    return pl.pallas_call(
        functools.partial(stack_kernel, kv_heads, group_width),
        out_shape=[shape] * 2,
        in_specs=[whole] * 2,
        out_specs=[whole] * 2,
        compiler_params=pltpu.CompilerParams(vmem_limit_bytes=8 * 1024 * 1024),
        cost_estimate=pl.CostEstimate(flops=1, bytes_accessed=1, transcendentals=0),
    )(query, grad)


def attention_kernel(kv_heads, group_width, halo_rows, *refs):
    halo_count = len(halo_rows)
    query_ref, grad_ref, kv_ref, bias_ref = refs[:4]
    halo_refs = refs[4 : 4 + halo_count]
    grad_query_ref, grad_kv_ref = refs[4 + halo_count : 6 + halo_count]
    grad_halo_refs = refs[6 + halo_count :]
    rows = kv_ref.shape[0]
    kv_cols = kv_heads * HEAD_WIDTH
    scaling = 1.0 / math.sqrt(HEAD_WIDTH)
    bias = jnp.concatenate([bias_ref[...]] * group_width, axis=1)
    for group in range(kv_heads):
        heads = [group * group_width + member for member in range(group_width)]
        stacked = slice(heads[0] * rows, (heads[-1] + 1) * rows)
        query, grad = query_ref[stacked, :], grad_ref[stacked, :]
        key_cols = slice(group * HEAD_WIDTH, (group + 1) * HEAD_WIDTH)
        value_cols = slice(kv_cols + group * HEAD_WIDTH, kv_cols + (group + 1) * HEAD_WIDTH)
        blocks = [*halo_refs, kv_ref]
        key = jnp.concatenate([block[:, key_cols] for block in blocks], axis=0)
        value = jnp.concatenate([block[:, value_cols] for block in blocks], axis=0)
        scores = dot(key, query, 1, 1) * scaling + bias
        raised = jnp.exp(scores - jnp.max(scores, axis=0, keepdims=True))
        weights = raised * (1.0 / jnp.sum(raised, axis=0, keepdims=True))
        weights_half = weights.astype(jnp.bfloat16)
        grad_weights = dot(value, grad, 1, 1)
        delta = jnp.sum(weights_half.astype(jnp.float32) * grad_weights, axis=0, keepdims=True)
        grad_scores = (weights * (grad_weights - delta)).astype(jnp.bfloat16)
        grad_query = (dot(grad_scores, key, 0, 0) * scaling).astype(jnp.bfloat16)
        for member, h in enumerate(heads):
            grad_query_ref[:, h * HEAD_WIDTH : (h + 1) * HEAD_WIDTH] = grad_query[
                member * rows : (member + 1) * rows
            ]
        grad_key = dot(grad_scores, query, 1, 0) * scaling
        grad_value = dot(weights_half, grad, 1, 0)
        start = 0
        for size, out_ref in zip([*halo_rows, rows], [*grad_halo_refs, grad_kv_ref]):
            out_ref[:, key_cols] = grad_key[start : start + size].astype(out_ref.dtype)
            out_ref[:, value_cols] = grad_value[start : start + size].astype(out_ref.dtype)
            start += size


def attention_backward(query, grad, kv, bias, halos):
    rows, kv_cols = kv.shape[0], kv.shape[1] // 2
    kv_heads = kv_cols // HEAD_WIDTH
    group_width = query.shape[0] // (rows * kv_heads)
    query_cols = kv_heads * group_width * HEAD_WIDTH
    halo_rows = [halo.shape[0] for halo in halos]
    span = bias.shape[0]
    whole = pl.BlockSpec(memory_space=pltpu.VMEM)
    outs = [
        jax.ShapeDtypeStruct((rows, query_cols), jnp.bfloat16),
        jax.ShapeDtypeStruct((rows, 2 * kv_cols), jnp.float32),
        *[jax.ShapeDtypeStruct((size, 2 * kv_cols), jnp.bfloat16) for size in halo_rows],
    ]
    return pl.pallas_call(
        functools.partial(attention_kernel, kv_heads, group_width, halo_rows),
        out_shape=outs,
        in_specs=[whole] * (4 + len(halos)),
        out_specs=[whole] * len(outs),
        compiler_params=pltpu.CompilerParams(vmem_limit_bytes=8 * 1024 * 1024),
        cost_estimate=pl.CostEstimate(
            flops=12 * rows * span * query_cols,
            bytes_accessed=4 * rows * query_cols * 2,
            transcendentals=rows * span * kv_heads * group_width,
        ),
    )(query, grad, kv, bias, *halos)


def join_kernel(query_ref, kv_ref, *refs):
    *part_refs, joined_ref = refs
    rows = kv_ref.shape[0]
    query_cols = query_ref.shape[1]
    joined_ref[:, :query_cols] = query_ref[...]
    total = kv_ref[...]
    for part_ref in part_refs:
        size = part_ref.shape[0]
        part = part_ref[...].astype(jnp.float32)
        if size < rows:
            part = jnp.concatenate(
                [jnp.zeros((rows - size, part.shape[1]), jnp.float32), part], axis=0
            )
        total = total + part
    joined_ref[:, query_cols:] = total.astype(jnp.bfloat16)


def join(query_part, kv_part, returned):
    rows, query_cols = query_part.shape
    kv_cols = kv_part.shape[1]
    whole = pl.BlockSpec(memory_space=pltpu.VMEM)
    return pl.pallas_call(
        join_kernel,
        out_shape=jax.ShapeDtypeStruct((rows, query_cols + kv_cols), jnp.bfloat16),
        in_specs=[whole] * (2 + len(returned)),
        out_specs=whole,
        compiler_params=pltpu.CompilerParams(vmem_limit_bytes=8 * 1024 * 1024),
        cost_estimate=pl.CostEstimate(flops=1, bytes_accessed=1, transcendentals=0),
    )(query_part, kv_part, *returned)


def project_kernel(pieces, tile, core_ref, *refs):
    flat_refs, (query_weight, key_weight, value_weight) = refs[: sum(pieces)], refs[-6:-3]
    full_ref, give_ref, block_ref = refs[-3:]
    row, at = 0, 0
    for count in pieces:
        column = 0
        for ref in flat_refs[at : at + count]:
            block_ref[row : row + ref.shape[0], column : column + ref.shape[1]] = ref[...]
            column += ref.shape[1]
        at += count
        row += flat_refs[at - 1].shape[0]
    query_cols, kv_cols = query_weight.shape[1], key_weight.shape[1]

    def step(i, carry):
        at = pl.ds(pl.multiple_of(i * tile, 16), tile)
        full_ref[at, :] = (
            dot(query_weight[at, :], block_ref[:, :query_cols], 1, 1)
            + dot(key_weight[at, :], block_ref[:, query_cols : query_cols + kv_cols], 1, 1)
            + dot(value_weight[at, :], block_ref[:, query_cols + kv_cols :], 1, 1)
        )
        return carry

    lax.fori_loop(0, full_ref.shape[0] // tile, step, 0)
    half = give_ref.shape[0]
    other = pl.multiple_of((1 - core_ref[0]) * half, 8)
    give_ref[...] = full_ref[pl.ds(other, half), :].astype(jnp.bfloat16)


def project(blocks, weights, core):
    width = weights[0].shape[0]
    rows = sum(block[0].shape[0] for block in blocks)
    cols = sum(weight.shape[1] for weight in weights)
    tile = max(t for t in range(16, 449, 16) if width % t == 0)
    flat = [piece for block in blocks for piece in block]
    whole = pl.BlockSpec(memory_space=pltpu.VMEM)
    return pl.pallas_call(
        functools.partial(project_kernel, [len(block) for block in blocks], tile),
        out_shape=[
            jax.ShapeDtypeStruct((width, rows), jnp.float32),
            jax.ShapeDtypeStruct((width // 2, rows), jnp.bfloat16),
        ],
        in_specs=[pl.BlockSpec(memory_space=pltpu.SMEM)] + [whole] * (len(flat) + 3),
        out_specs=[whole] * 2,
        scratch_shapes=[pltpu.VMEM((rows, cols), jnp.bfloat16)],
        compiler_params=pltpu.CompilerParams(vmem_limit_bytes=8 * 1024 * 1024),
        cost_estimate=pl.CostEstimate(
            flops=2 * rows * width * cols,
            bytes_accessed=2 * width * cols + 6 * width * rows,
            transcendentals=0,
        ),
    )(core, *flat, *weights)


def swapped(block, axis, first):
    size = lax.axis_size(axis)
    target = list(range(size))
    for i in range(first, size - 1, 2):
        target[i], target[i + 1] = i + 1, i
    return lax.ppermute(block, axis, list(enumerate(target)))


def after(arrays, *others):
    return lax.optimization_barrier((*arrays, *others))[: len(arrays)]


def passed_along(block, axis, distance):
    devices = range(lax.axis_size(axis))
    return lax.ppermute(block, axis, [((i - distance) % len(devices), i) for i in devices])


def per_device(
    query_rows,
    key_row_matrix,
    value_row_matrix,
    out_grad,
    w_query,
    key_weight,
    value_weight,
    doc_ids,
):
    documents = doc_ids[0]
    tokens = documents.shape[0]
    rows = query_rows.shape[1]
    kv_cols = key_row_matrix.shape[2]
    shards = lax.axis_size("seq")
    place = lax.axis_index("seq")
    back = min(WINDOW, tokens // 3) - 1
    halo_rows = []
    while sum(halo_rows) < back and len(halo_rows) < shards - 1:
        halo_rows.append(min(rows, -(-(back - sum(halo_rows)) // 16) * 16))
    kv = lax.optimization_barrier(
        jnp.concatenate([key_row_matrix[0], value_row_matrix[0]], axis=1)
    )
    halos = [passed_along(kv[rows - size :], "seq", d) for d, size in enumerate(halo_rows, 1)]
    reach = sum(halo_rows)
    first_row = place * rows
    key_docs = lax.dynamic_slice_in_dim(
        jnp.concatenate([jnp.full((reach,), -1, jnp.int32), documents]), first_row, reach + rows, 0
    )
    query_docs = lax.dynamic_slice_in_dim(documents, first_row, rows, 0)
    offset = (
        jnp.arange(rows, dtype=jnp.int32)[None, :]
        + reach
        - jnp.arange(reach + rows, dtype=jnp.int32)[:, None]
    )
    allowed = (query_docs[None, :] == key_docs[:, None]) & (offset >= 0) & (offset < WINDOW)
    bias = jnp.where(allowed, 0.0, MASKED).astype(jnp.float32)
    kv_heads = kv_cols // HEAD_WIDTH
    query_stack, grad_stack = stack(
        *after((query_rows[0], out_grad[0]), kv), kv_heads, query_rows.shape[2] // kv_cols
    )
    grad_query, grad_kv, *grad_halos = attention_backward(
        query_stack, grad_stack, kv, bias, halos[::-1]
    )
    returned = [passed_along(part, "seq", -d) for d, part in enumerate(grad_halos[::-1], 1)]
    own = join(grad_query, grad_kv, returned)
    weights = (w_query[0], key_weight[0], value_weight[0])
    core = lax.axis_index("mp").astype(jnp.int32)

    def halves_summed(blocks):
        full, give = project([(block,) for block in blocks], weights, core[None])
        half = give.shape[0]
        keep = lax.dynamic_slice_in_dim(full, core * half, half, 0)
        got = passed_along(give, "mp", 1)
        return give, (keep + got.astype(jnp.float32)).astype(jnp.bfloat16)

    even = place % 2 == 0
    results, waiting = [], [own]
    by_first, by_second = own, own
    for step in range(1, shards):
        came_first = swapped(by_first, "seq", 0)
        last = step == shards - 1 and shards % 2 == 0
        came_second = came_first if last else swapped(by_second, "seq", 1)
        if step == 2:
            waiting = after(waiting, total)
        elif step > 2:
            waiting = after(waiting, total, results[step - 3])
        give, total = halves_summed(waiting)
        if step < shards - 1:
            came_first, came_second = after((came_first, came_second), give)
        results.append(passed_along(total, "section", -1))
        by_first, by_second = came_second, came_first
        if last:
            waiting = [came_first]
        elif 2 * step < shards:
            waiting = [came_first, came_second]
        else:
            waiting = [jnp.where(even == (place >= step), came_second, came_first)]
    if shards > 1:
        waiting = after(waiting, *results)
    results.append(passed_along(halves_summed(waiting)[1], "section", -1))
    for step, block in enumerate(results):
        if block.shape[1] == rows:
            results[step] = [block]
        else:
            first, second = block[:, :rows], block[:, rows:]
            results[step] = [jnp.where(even, second, first), jnp.where(even, first, second)]
    upstream = jnp.zeros((results[0][0].shape[0], tokens), jnp.bfloat16)
    for s in range(shards):
        behind = results[s][0]
        ahead = results[(shards - s) % shards][-1]
        block = jnp.where(place >= s, behind, ahead)
        upstream = lax.dynamic_update_slice_in_dim(
            upstream, block, ((place - s) % shards) * rows, 1
        )
    return upstream.T[None]


def solution(mesh):
    placed = P("section", "seq", "mp")
    return jax.shard_map(
        per_device,
        mesh=mesh,
        in_specs=(placed,) * 7 + (P("section", None),),
        out_specs=P("section", None, ("seq", "mp")),
        check_vma=False,
    )
```

```python
import functools
import math

import jax
import jax.numpy as jnp
from jax import lax
from jax.experimental import pallas as pl
from jax.experimental.pallas import tpu as pltpu
from jax.sharding import PartitionSpec as P

HEAD_WIDTH = 128
WINDOW = 512
MASKED = -1e30


def dot(left, right, left_dim, right_dim):
    return lax.dot_general(
        left,
        right,
        (((left_dim,), (right_dim,)), ((), ())),
        preferred_element_type=jnp.float32,
    )


def stack_kernel(kv_heads, group_width, query_ref, grad_ref, query_out, grad_out):
    rows = query_ref.shape[0]
    for head in range(kv_heads * group_width):
        cols = slice(head * HEAD_WIDTH, (head + 1) * HEAD_WIDTH)
        query_out[head * rows : (head + 1) * rows, :] = query_ref[:, cols]
        grad_out[head * rows : (head + 1) * rows, :] = grad_ref[:, cols]


def stack(query, grad, kv_heads, group_width):
    rows, query_cols = query.shape
    whole = pl.BlockSpec(memory_space=pltpu.VMEM)
    shape = jax.ShapeDtypeStruct((rows * kv_heads * group_width, HEAD_WIDTH), jnp.bfloat16)
    return pl.pallas_call(
        functools.partial(stack_kernel, kv_heads, group_width),
        out_shape=[shape] * 2,
        in_specs=[whole] * 2,
        out_specs=[whole] * 2,
        compiler_params=pltpu.CompilerParams(vmem_limit_bytes=8 * 1024 * 1024),
        cost_estimate=pl.CostEstimate(flops=1, bytes_accessed=1, transcendentals=0),
    )(query, grad)


def attention_kernel(kv_heads, group_width, halo_rows, *refs):
    halo_count = len(halo_rows)
    query_ref, grad_ref, kv_ref, bias_ref = refs[:4]
    halo_refs = refs[4 : 4 + halo_count]
    grad_query_ref, grad_kv_ref = refs[4 + halo_count : 6 + halo_count]
    grad_halo_refs = refs[6 + halo_count :]
    rows = kv_ref.shape[0]
    kv_cols = kv_heads * HEAD_WIDTH
    scaling = 1.0 / math.sqrt(HEAD_WIDTH)
    bias = jnp.concatenate([bias_ref[...]] * group_width, axis=1)
    for group in range(kv_heads):
        heads = [group * group_width + member for member in range(group_width)]
        stacked = slice(heads[0] * rows, (heads[-1] + 1) * rows)
        query, grad = query_ref[stacked, :], grad_ref[stacked, :]
        key_cols = slice(group * HEAD_WIDTH, (group + 1) * HEAD_WIDTH)
        value_cols = slice(kv_cols + group * HEAD_WIDTH, kv_cols + (group + 1) * HEAD_WIDTH)
        blocks = [*halo_refs, kv_ref]
        key = jnp.concatenate([block[:, key_cols] for block in blocks], axis=0)
        value = jnp.concatenate([block[:, value_cols] for block in blocks], axis=0)
        scores = dot(key, query, 1, 1) * scaling + bias
        raised = jnp.exp(scores - jnp.max(scores, axis=0, keepdims=True))
        weights = raised * (1.0 / jnp.sum(raised, axis=0, keepdims=True))
        weights_half = weights.astype(jnp.bfloat16)
        grad_weights = dot(value, grad, 1, 1)
        delta = jnp.sum(weights_half.astype(jnp.float32) * grad_weights, axis=0, keepdims=True)
        grad_scores = (weights * (grad_weights - delta)).astype(jnp.bfloat16)
        grad_query = (dot(grad_scores, key, 0, 0) * scaling).astype(jnp.bfloat16)
        for member, h in enumerate(heads):
            grad_query_ref[:, h * HEAD_WIDTH : (h + 1) * HEAD_WIDTH] = grad_query[
                member * rows : (member + 1) * rows
            ]
        grad_key = dot(grad_scores, query, 1, 0) * scaling
        grad_value = dot(weights_half, grad, 1, 0)
        start = 0
        for size, out_ref in zip([*halo_rows, rows], [*grad_halo_refs, grad_kv_ref]):
            out_ref[:, key_cols] = grad_key[start : start + size].astype(out_ref.dtype)
            out_ref[:, value_cols] = grad_value[start : start + size].astype(out_ref.dtype)
            start += size


def attention_backward(query, grad, kv, bias, halos):
    rows, kv_cols = kv.shape[0], kv.shape[1] // 2
    kv_heads = kv_cols // HEAD_WIDTH
    group_width = query.shape[0] // (rows * kv_heads)
    query_cols = kv_heads * group_width * HEAD_WIDTH
    halo_rows = [halo.shape[0] for halo in halos]
    span = bias.shape[0]
    whole = pl.BlockSpec(memory_space=pltpu.VMEM)
    outs = [
        jax.ShapeDtypeStruct((rows, query_cols), jnp.bfloat16),
        jax.ShapeDtypeStruct((rows, 2 * kv_cols), jnp.float32),
        *[jax.ShapeDtypeStruct((size, 2 * kv_cols), jnp.bfloat16) for size in halo_rows],
    ]
    return pl.pallas_call(
        functools.partial(attention_kernel, kv_heads, group_width, halo_rows),
        out_shape=outs,
        in_specs=[whole] * (4 + len(halos)),
        out_specs=[whole] * len(outs),
        compiler_params=pltpu.CompilerParams(vmem_limit_bytes=8 * 1024 * 1024),
        cost_estimate=pl.CostEstimate(
            flops=12 * rows * span * query_cols,
            bytes_accessed=4 * rows * query_cols * 2,
            transcendentals=rows * span * kv_heads * group_width,
        ),
    )(query, grad, kv, bias, *halos)


def join_kernel(kv_ref, *refs):
    *part_refs, total_ref = refs
    rows = kv_ref.shape[0]
    total = kv_ref[...]
    for part_ref in part_refs:
        size = part_ref.shape[0]
        part = part_ref[...].astype(jnp.float32)
        if size < rows:
            part = jnp.concatenate(
                [jnp.zeros((rows - size, part.shape[1]), jnp.float32), part], axis=0
            )
        total = total + part
    total_ref[...] = total.astype(jnp.bfloat16)


def join(kv_part, returned):
    whole = pl.BlockSpec(memory_space=pltpu.VMEM)
    return pl.pallas_call(
        join_kernel,
        out_shape=jax.ShapeDtypeStruct(kv_part.shape, jnp.bfloat16),
        in_specs=[whole] * (1 + len(returned)),
        out_specs=whole,
        compiler_params=pltpu.CompilerParams(vmem_limit_bytes=8 * 1024 * 1024),
        cost_estimate=pl.CostEstimate(flops=1, bytes_accessed=1, transcendentals=0),
    )(kv_part, *returned)


def project_kernel(blocks, chosen, tile, scalar_ref, *refs):
    flat_refs, weight_refs = refs[: 2 * blocks], refs[2 * blocks : 2 * blocks + 3]
    full_ref, give_ref, block_ref = refs[2 * blocks + 3 :]
    query_cols = flat_refs[0].shape[1]
    kv_cols = flat_refs[1].shape[1] // 2

    def take(block, row):
        rows = flat_refs[2 * block].shape[0]
        block_ref[row : row + rows, :query_cols] = flat_refs[2 * block][...]
        block_ref[row : row + rows, query_cols:] = flat_refs[2 * block + 1][...]

    if chosen:
        for block in range(blocks):
            pl.when(scalar_ref[1] == block)(functools.partial(take, block, 0))
    else:
        for block in range(blocks):
            take(block, block * flat_refs[0].shape[0])
    query_weight, key_weight, value_weight = weight_refs

    def step(i, carry):
        at = pl.ds(pl.multiple_of(i * tile, 16), tile)
        full_ref[at, :] = (
            dot(query_weight[at, :], block_ref[:, :query_cols], 1, 1)
            + dot(key_weight[at, :], block_ref[:, query_cols : query_cols + kv_cols], 1, 1)
            + dot(value_weight[at, :], block_ref[:, query_cols + kv_cols :], 1, 1)
        )
        return carry

    lax.fori_loop(0, full_ref.shape[0] // tile, step, 0)
    half = give_ref.shape[0]
    other = pl.multiple_of((1 - scalar_ref[0]) * half, 8)
    give_ref[...] = full_ref[pl.ds(other, half), :].astype(jnp.bfloat16)


def project(blocks, weights, core, choice=None):
    width = weights[0].shape[0]
    rows = blocks[0][0].shape[0] * (len(blocks) if choice is None else 1)
    cols = sum(weight.shape[1] for weight in weights)
    tile = max(t for t in range(16, 449, 16) if width % t == 0)
    flat = [piece for block in blocks for piece in block]
    scalars = jnp.stack([core, core if choice is None else choice])
    whole = pl.BlockSpec(memory_space=pltpu.VMEM)
    return pl.pallas_call(
        functools.partial(project_kernel, len(blocks), choice is not None, tile),
        out_shape=[
            jax.ShapeDtypeStruct((width, rows), jnp.float32),
            jax.ShapeDtypeStruct((width // 2, rows), jnp.bfloat16),
        ],
        in_specs=[pl.BlockSpec(memory_space=pltpu.SMEM)]
        + [whole] * (len(flat) + 3),
        out_specs=[whole] * 2,
        scratch_shapes=[pltpu.VMEM((rows, cols), jnp.bfloat16)],
        compiler_params=pltpu.CompilerParams(vmem_limit_bytes=8 * 1024 * 1024),
        cost_estimate=pl.CostEstimate(
            flops=2 * rows * width * cols,
            bytes_accessed=2 * width * cols + 6 * width * rows,
            transcendentals=0,
        ),
    )(scalars, *flat, *weights)


def swapped(block, axis, first):
    pairs = []
    for i in range(first, lax.axis_size(axis) - 1, 2):
        pairs += [(i, i + 1), (i + 1, i)]
    return lax.ppermute(block, axis, pairs)


def after(arrays, *others):
    return lax.optimization_barrier((*arrays, *others))[: len(arrays)]


def passed_along(block, axis, distance):
    devices = range(lax.axis_size(axis))
    return lax.ppermute(block, axis, [((i - distance) % len(devices), i) for i in devices])


def per_device(
    query_rows,
    key_row_matrix,
    value_row_matrix,
    out_grad,
    w_query,
    key_weight,
    value_weight,
    doc_ids,
):
    documents = doc_ids[0]
    tokens = documents.shape[0]
    rows = query_rows.shape[1]
    kv_cols = key_row_matrix.shape[2]
    shards = lax.axis_size("seq")
    place = lax.axis_index("seq")
    back = min(WINDOW, tokens // 3) - 1
    halo_rows = []
    while sum(halo_rows) < back and len(halo_rows) < shards - 1:
        halo_rows.append(min(rows, -(-(back - sum(halo_rows)) // 16) * 16))
    kv = lax.optimization_barrier(
        jnp.concatenate([key_row_matrix[0], value_row_matrix[0]], axis=1)
    )
    halos = [passed_along(kv[rows - size :], "seq", d) for d, size in enumerate(halo_rows, 1)]
    reach = sum(halo_rows)
    first_row = place * rows
    key_docs = lax.dynamic_slice_in_dim(
        jnp.concatenate([jnp.full((reach,), -1, jnp.int32), documents]), first_row, reach + rows, 0
    )
    query_docs = lax.dynamic_slice_in_dim(documents, first_row, rows, 0)
    offset = (
        jnp.arange(rows, dtype=jnp.int32)[None, :]
        + reach
        - jnp.arange(reach + rows, dtype=jnp.int32)[:, None]
    )
    allowed = (query_docs[None, :] == key_docs[:, None]) & (offset >= 0) & (offset < WINDOW)
    bias = jnp.where(allowed, 0.0, MASKED).astype(jnp.float32)
    kv_heads = kv_cols // HEAD_WIDTH
    query_stack, grad_stack = stack(
        *after((query_rows[0], out_grad[0]), kv), kv_heads, query_rows.shape[2] // kv_cols
    )
    grad_query, grad_kv, *grad_halos = attention_backward(
        query_stack, grad_stack, kv, bias, halos[::-1]
    )
    returned = [passed_along(part, "seq", -d) for d, part in enumerate(grad_halos[::-1], 1)]
    weights = (w_query[0], key_weight[0], value_weight[0])
    core = lax.axis_index("mp").astype(jnp.int32)
    even = place % 2 == 0

    def halves_summed(blocks, choice, late):
        full, give = project(blocks, weights, core, choice)
        half = give.shape[0]
        keep = lax.dynamic_slice_in_dim(full, core * half, half, 0)
        got = jnp.concatenate(
            [
                passed_along(give[:, i : i + rows], "mp", 1)
                for i in range(0, give.shape[1], rows)
            ],
            axis=1,
        )
        (got,) = after((got,), *late)
        return (keep + got.astype(jnp.float32)).astype(jnp.bfloat16)

    def swap(pair, step):
        last = step == shards - 1 and shards % 2 == 0
        first = swapped(pair[0], "seq", 0)
        second = first if last else swapped(pair[1], "seq", 1)
        return second, first

    query_steps = [(grad_query, grad_query)]
    if shards > 1:
        query_steps.append(swap(query_steps[0], 1))
        grad_kv, *returned = after((grad_kv, *returned), *query_steps[1])
    kv_own = join(grad_kv, returned)
    kv_steps = [(kv_own, kv_own)]
    results, total = [], None

    def product(step, *gates):
        choice = None
        if step == 0 or (step == shards - 1 and shards % 2 == 0):
            blocks = [(query_steps[step][1], kv_steps[step][1])]
        else:
            blocks = list(zip(query_steps[step][::-1], kv_steps[step][::-1]))
            if 2 * step >= shards:
                choice = (even == (place >= step)).astype(jnp.int32)
        earlier = [*gates, *results[-2:-1]]
        if step:
            earlier.append(total)
        if earlier:
            blocks = [after(block, *earlier) for block in blocks]
        late = kv_steps[step + 1] if 1 < step < shards - 1 else ()
        summed = halves_summed(blocks, choice, late)
        results.append(passed_along(summed, "section", -1))
        return summed

    def gate(step):
        arrived = [*kv_steps[step], *query_steps[step + 1]]
        (rows_out,) = after((kv_steps[step][1][:16, :HEAD_WIDTH],), *arrived)
        return passed_along(rows_out, "mp", 1)

    for step in range(1, shards):
        kv_steps.append(swap(kv_steps[step - 1], step))
        if step + 1 < shards:
            query_steps.append(swap(query_steps[step], step + 1))
        total = product(step - 1, gate(step - 1))
    total = product(shards - 1)
    for step, block in enumerate(results):
        if block.shape[1] == rows:
            results[step] = [block]
        else:
            first, second = block[:, :rows], block[:, rows:]
            results[step] = [jnp.where(even, second, first), jnp.where(even, first, second)]
    upstream = jnp.zeros((results[0][0].shape[0], tokens), jnp.bfloat16)
    for s in range(shards):
        behind = results[s][0]
        ahead = results[(shards - s) % shards][-1]
        block = jnp.where(place >= s, behind, ahead)
        upstream = lax.dynamic_update_slice_in_dim(
            upstream, block, ((place - s) % shards) * rows, 1
        )
    return upstream.T[None]


def solution(mesh):
    placed = P("section", "seq", "mp")
    return jax.shard_map(
        per_device,
        mesh=mesh,
        in_specs=(placed,) * 7 + (P("section", None),),
        out_specs=P("section", None, ("seq", "mp")),
        check_vma=False,
    )
```

```python
import functools
import math

import jax
import jax.numpy as jnp
from jax import lax
from jax.experimental import pallas as pl
from jax.experimental.pallas import tpu as pltpu
from jax.sharding import PartitionSpec as P

HEAD_WIDTH = 128
WINDOW = 512
MASKED = -1e30


def dot(left, right, left_dim, right_dim):
    return lax.dot_general(
        left,
        right,
        (((left_dim,), (right_dim,)), ((), ())),
        preferred_element_type=jnp.float32,
    )


def stack_kernel(kv_heads, group_width, query_ref, grad_ref, query_out, grad_out):
    rows = query_ref.shape[0]
    for head in range(kv_heads * group_width):
        cols = slice(head * HEAD_WIDTH, (head + 1) * HEAD_WIDTH)
        query_out[head * rows : (head + 1) * rows, :] = query_ref[:, cols]
        grad_out[head * rows : (head + 1) * rows, :] = grad_ref[:, cols]


def stack(query, grad, kv_heads, group_width):
    rows, query_cols = query.shape
    whole = pl.BlockSpec(memory_space=pltpu.VMEM)
    shape = jax.ShapeDtypeStruct((rows * kv_heads * group_width, HEAD_WIDTH), jnp.bfloat16)
    return pl.pallas_call(
        functools.partial(stack_kernel, kv_heads, group_width),
        out_shape=[shape] * 2,
        in_specs=[whole] * 2,
        out_specs=[whole] * 2,
        compiler_params=pltpu.CompilerParams(vmem_limit_bytes=8 * 1024 * 1024),
        cost_estimate=pl.CostEstimate(flops=1, bytes_accessed=1, transcendentals=0),
    )(query, grad)


def attention_kernel(kv_heads, group_width, halo_rows, *refs):
    halo_count = len(halo_rows)
    query_ref, grad_ref, kv_ref, bias_ref = refs[:4]
    halo_refs = refs[4 : 4 + halo_count]
    grad_query_ref, grad_kv_ref = refs[4 + halo_count : 6 + halo_count]
    grad_halo_refs = refs[6 + halo_count :]
    rows = kv_ref.shape[0]
    kv_cols = kv_heads * HEAD_WIDTH
    scaling = 1.0 / math.sqrt(HEAD_WIDTH)
    bias = jnp.concatenate([bias_ref[...]] * group_width, axis=1)
    for group in range(kv_heads):
        heads = [group * group_width + member for member in range(group_width)]
        stacked = slice(heads[0] * rows, (heads[-1] + 1) * rows)
        query, grad = query_ref[stacked, :], grad_ref[stacked, :]
        key_cols = slice(group * HEAD_WIDTH, (group + 1) * HEAD_WIDTH)
        value_cols = slice(kv_cols + group * HEAD_WIDTH, kv_cols + (group + 1) * HEAD_WIDTH)
        blocks = [*halo_refs, kv_ref]
        key = jnp.concatenate([block[:, key_cols] for block in blocks], axis=0)
        value = jnp.concatenate([block[:, value_cols] for block in blocks], axis=0)
        scores = dot(key, query, 1, 1) * scaling + bias
        raised = jnp.exp(scores - jnp.max(scores, axis=0, keepdims=True))
        weights = raised * (1.0 / jnp.sum(raised, axis=0, keepdims=True))
        weights_half = weights.astype(jnp.bfloat16)
        grad_weights = dot(value, grad, 1, 1)
        delta = jnp.sum(weights_half.astype(jnp.float32) * grad_weights, axis=0, keepdims=True)
        grad_scores = (weights * (grad_weights - delta)).astype(jnp.bfloat16)
        grad_query = (dot(grad_scores, key, 0, 0) * scaling).astype(jnp.bfloat16)
        for member, h in enumerate(heads):
            grad_query_ref[:, h * HEAD_WIDTH : (h + 1) * HEAD_WIDTH] = grad_query[
                member * rows : (member + 1) * rows
            ]
        grad_key = dot(grad_scores, query, 1, 0) * scaling
        grad_value = dot(weights_half, grad, 1, 0)
        start = 0
        for size, out_ref in zip([*halo_rows, rows], [*grad_halo_refs, grad_kv_ref]):
            out_ref[:, key_cols] = grad_key[start : start + size].astype(out_ref.dtype)
            out_ref[:, value_cols] = grad_value[start : start + size].astype(out_ref.dtype)
            start += size


def attention_backward(query, grad, kv, bias, halos):
    rows, kv_cols = kv.shape[0], kv.shape[1] // 2
    kv_heads = kv_cols // HEAD_WIDTH
    group_width = query.shape[0] // (rows * kv_heads)
    query_cols = kv_heads * group_width * HEAD_WIDTH
    halo_rows = [halo.shape[0] for halo in halos]
    span = bias.shape[0]
    whole = pl.BlockSpec(memory_space=pltpu.VMEM)
    outs = [
        jax.ShapeDtypeStruct((rows, query_cols), jnp.bfloat16),
        jax.ShapeDtypeStruct((rows, 2 * kv_cols), jnp.float32),
        *[jax.ShapeDtypeStruct((size, 2 * kv_cols), jnp.bfloat16) for size in halo_rows],
    ]
    return pl.pallas_call(
        functools.partial(attention_kernel, kv_heads, group_width, halo_rows),
        out_shape=outs,
        in_specs=[whole] * (4 + len(halos)),
        out_specs=[whole] * len(outs),
        compiler_params=pltpu.CompilerParams(vmem_limit_bytes=8 * 1024 * 1024),
        cost_estimate=pl.CostEstimate(
            flops=12 * rows * span * query_cols,
            bytes_accessed=4 * rows * query_cols * 2,
            transcendentals=rows * span * kv_heads * group_width,
        ),
    )(query, grad, kv, bias, *halos)


def join_kernel(query_ref, kv_ref, *refs):
    *part_refs, joined_ref = refs
    rows = kv_ref.shape[0]
    query_cols = query_ref.shape[1]
    joined_ref[:, :query_cols] = query_ref[...]
    total = kv_ref[...]
    for part_ref in part_refs:
        size = part_ref.shape[0]
        part = part_ref[...].astype(jnp.float32)
        if size < rows:
            part = jnp.concatenate(
                [jnp.zeros((rows - size, part.shape[1]), jnp.float32), part], axis=0
            )
        total = total + part
    joined_ref[:, query_cols:] = total.astype(jnp.bfloat16)


def join(query_part, kv_part, returned):
    rows, query_cols = query_part.shape
    kv_cols = kv_part.shape[1]
    whole = pl.BlockSpec(memory_space=pltpu.VMEM)
    return pl.pallas_call(
        join_kernel,
        out_shape=jax.ShapeDtypeStruct((rows, query_cols + kv_cols), jnp.bfloat16),
        in_specs=[whole] * (2 + len(returned)),
        out_specs=whole,
        compiler_params=pltpu.CompilerParams(vmem_limit_bytes=8 * 1024 * 1024),
        cost_estimate=pl.CostEstimate(flops=1, bytes_accessed=1, transcendentals=0),
    )(query_part, kv_part, *returned)


def project_kernel(pieces, tile, core_ref, *refs):
    flat_refs, (query_weight, key_weight, value_weight) = refs[: sum(pieces)], refs[-6:-3]
    full_ref, give_ref, block_ref = refs[-3:]
    row, at = 0, 0
    for count in pieces:
        column = 0
        for ref in flat_refs[at : at + count]:
            block_ref[row : row + ref.shape[0], column : column + ref.shape[1]] = ref[...]
            column += ref.shape[1]
        at += count
        row += flat_refs[at - 1].shape[0]
    query_cols, kv_cols = query_weight.shape[1], key_weight.shape[1]

    def step(i, carry):
        at = pl.ds(pl.multiple_of(i * tile, 16), tile)
        full_ref[at, :] = (
            dot(query_weight[at, :], block_ref[:, :query_cols], 1, 1)
            + dot(key_weight[at, :], block_ref[:, query_cols : query_cols + kv_cols], 1, 1)
            + dot(value_weight[at, :], block_ref[:, query_cols + kv_cols :], 1, 1)
        )
        return carry

    lax.fori_loop(0, full_ref.shape[0] // tile, step, 0)
    half = give_ref.shape[0]
    other = pl.multiple_of((1 - core_ref[0]) * half, 8)
    give_ref[...] = full_ref[pl.ds(other, half), :].astype(jnp.bfloat16)


def project(blocks, weights, core):
    width = weights[0].shape[0]
    rows = sum(block[0].shape[0] for block in blocks)
    cols = sum(weight.shape[1] for weight in weights)
    tile = max(t for t in range(16, 449, 16) if width % t == 0)
    flat = [piece for block in blocks for piece in block]
    whole = pl.BlockSpec(memory_space=pltpu.VMEM)
    return pl.pallas_call(
        functools.partial(project_kernel, [len(block) for block in blocks], tile),
        out_shape=[
            jax.ShapeDtypeStruct((width, rows), jnp.float32),
            jax.ShapeDtypeStruct((width // 2, rows), jnp.bfloat16),
        ],
        in_specs=[pl.BlockSpec(memory_space=pltpu.SMEM)] + [whole] * (len(flat) + 3),
        out_specs=[whole] * 2,
        scratch_shapes=[pltpu.VMEM((rows, cols), jnp.bfloat16)],
        compiler_params=pltpu.CompilerParams(vmem_limit_bytes=8 * 1024 * 1024),
        cost_estimate=pl.CostEstimate(
            flops=2 * rows * width * cols,
            bytes_accessed=2 * width * cols + 6 * width * rows,
            transcendentals=0,
        ),
    )(core, *flat, *weights)


def swapped(block, axis, first):
    pairs = []
    for i in range(first, lax.axis_size(axis) - 1, 2):
        pairs += [(i, i + 1), (i + 1, i)]
    return lax.ppermute(block, axis, pairs)


def after(arrays, *others):
    return lax.optimization_barrier((*arrays, *others))[: len(arrays)]


def passed_along(block, axis, distance):
    devices = range(lax.axis_size(axis))
    return lax.ppermute(block, axis, [((i - distance) % len(devices), i) for i in devices])


def per_device(
    query_rows,
    key_row_matrix,
    value_row_matrix,
    out_grad,
    w_query,
    key_weight,
    value_weight,
    doc_ids,
):
    documents = doc_ids[0]
    tokens = documents.shape[0]
    rows = query_rows.shape[1]
    kv_cols = key_row_matrix.shape[2]
    shards = lax.axis_size("seq")
    place = lax.axis_index("seq")
    back = min(WINDOW, tokens // 3) - 1
    halo_rows = []
    while sum(halo_rows) < back and len(halo_rows) < shards - 1:
        halo_rows.append(min(rows, -(-(back - sum(halo_rows)) // 16) * 16))
    kv = lax.optimization_barrier(
        jnp.concatenate([key_row_matrix[0], value_row_matrix[0]], axis=1)
    )
    halos = [passed_along(kv[rows - size :], "seq", d) for d, size in enumerate(halo_rows, 1)]
    reach = sum(halo_rows)
    first_row = place * rows
    key_docs = lax.dynamic_slice_in_dim(
        jnp.concatenate([jnp.full((reach,), -1, jnp.int32), documents]), first_row, reach + rows, 0
    )
    query_docs = lax.dynamic_slice_in_dim(documents, first_row, rows, 0)
    offset = (
        jnp.arange(rows, dtype=jnp.int32)[None, :]
        + reach
        - jnp.arange(reach + rows, dtype=jnp.int32)[:, None]
    )
    allowed = (query_docs[None, :] == key_docs[:, None]) & (offset >= 0) & (offset < WINDOW)
    bias = jnp.where(allowed, 0.0, MASKED).astype(jnp.float32)
    kv_heads = kv_cols // HEAD_WIDTH
    query_stack, grad_stack = stack(
        *after((query_rows[0], out_grad[0]), kv), kv_heads, query_rows.shape[2] // kv_cols
    )
    grad_query, grad_kv, *grad_halos = attention_backward(
        query_stack, grad_stack, kv, bias, halos[::-1]
    )
    returned = [passed_along(part, "seq", -d) for d, part in enumerate(grad_halos[::-1], 1)]
    own = join(grad_query, grad_kv, returned)
    weights = (w_query[0], key_weight[0], value_weight[0])
    core = lax.axis_index("mp").astype(jnp.int32)

    def halves_summed(blocks, *late):
        full, give = project([(block,) for block in blocks], weights, core[None])
        half = give.shape[0]
        keep = lax.dynamic_slice_in_dim(full, core * half, half, 0)
        sums = []
        for i in range(0, give.shape[1], rows):
            got = passed_along(give[:, i : i + rows], "mp", 1)
            if late:
                (got,) = after((got,), *late)
            sums.append((keep[:, i : i + rows] + got.astype(jnp.float32)).astype(jnp.bfloat16))
        return jnp.concatenate(sums, axis=1)

    even = place % 2 == 0
    results, waiting = [], [own]
    by_first, by_second = own, own
    for step in range(1, shards):
        came_first = swapped(by_first, "seq", 0)
        last = step == shards - 1 and shards % 2 == 0
        came_second = came_first if last else swapped(by_second, "seq", 1)
        if step > 1:
            waiting = after(waiting, total, *(results[-2:] if 2 * step > shards else ()))
        total = halves_summed(waiting, *((came_first, came_second) if step > 1 else ()))
        results.append(passed_along(total, "section", -1))
        by_first, by_second = came_second, came_first
        if last:
            waiting = [came_first]
        elif 2 * step < shards:
            waiting = [came_first, came_second]
        else:
            waiting = [jnp.where(even == (place >= step), came_second, came_first)]
    if shards > 1:
        waiting = after(waiting, total)
    results.append(passed_along(halves_summed(waiting), "section", -1))
    for step, block in enumerate(results):
        if block.shape[1] == rows:
            results[step] = [block]
        else:
            first, second = block[:, :rows], block[:, rows:]
            results[step] = [jnp.where(even, second, first), jnp.where(even, first, second)]
    upstream = jnp.zeros((results[0][0].shape[0], tokens), jnp.bfloat16)
    for s in range(shards):
        behind = results[s][0]
        ahead = results[(shards - s) % shards][-1]
        block = jnp.where(place >= s, behind, ahead)
        upstream = lax.dynamic_update_slice_in_dim(
            upstream, block, ((place - s) % shards) * rows, 1
        )
    return upstream.T[None]


def solution(mesh):
    placed = P("section", "seq", "mp")
    return jax.shard_map(
        per_device,
        mesh=mesh,
        in_specs=(placed,) * 7 + (P("section", None),),
        out_specs=P("section", None, ("seq", "mp")),
        check_vma=False,
    )
```

```python
import functools
import math

import jax
import jax.numpy as jnp
from jax import lax
from jax.experimental import pallas as pl
from jax.experimental.pallas import tpu as pltpu
from jax.sharding import PartitionSpec as P

HEAD_WIDTH = 128
WINDOW = 512
MASKED = -1e30


def dot(left, right, left_dim, right_dim):
    return lax.dot_general(
        left,
        right,
        (((left_dim,), (right_dim,)), ((), ())),
        preferred_element_type=jnp.float32,
    )


def stack_kernel(kv_heads, group_width, query_ref, grad_ref, query_out, grad_out):
    rows = query_ref.shape[0]
    for head in range(kv_heads * group_width):
        cols = slice(head * HEAD_WIDTH, (head + 1) * HEAD_WIDTH)
        query_out[head * rows : (head + 1) * rows, :] = query_ref[:, cols]
        grad_out[head * rows : (head + 1) * rows, :] = grad_ref[:, cols]


def stack(query, grad, kv_heads, group_width):
    rows, query_cols = query.shape
    whole = pl.BlockSpec(memory_space=pltpu.VMEM)
    shape = jax.ShapeDtypeStruct((rows * kv_heads * group_width, HEAD_WIDTH), jnp.bfloat16)
    return pl.pallas_call(
        functools.partial(stack_kernel, kv_heads, group_width),
        out_shape=[shape] * 2,
        in_specs=[whole] * 2,
        out_specs=[whole] * 2,
        compiler_params=pltpu.CompilerParams(vmem_limit_bytes=8 * 1024 * 1024),
        cost_estimate=pl.CostEstimate(flops=1, bytes_accessed=1, transcendentals=0),
    )(query, grad)


def attention_kernel(kv_heads, group_width, halo_rows, *refs):
    halo_count = len(halo_rows)
    query_ref, grad_ref, kv_ref, bias_ref = refs[:4]
    halo_refs = refs[4 : 4 + halo_count]
    grad_query_ref, grad_kv_ref = refs[4 + halo_count : 6 + halo_count]
    grad_halo_refs = refs[6 + halo_count :]
    rows = kv_ref.shape[0]
    kv_cols = kv_heads * HEAD_WIDTH
    scaling = 1.0 / math.sqrt(HEAD_WIDTH)
    bias = jnp.concatenate([bias_ref[...]] * group_width, axis=1)
    for group in range(kv_heads):
        heads = [group * group_width + member for member in range(group_width)]
        stacked = slice(heads[0] * rows, (heads[-1] + 1) * rows)
        query, grad = query_ref[stacked, :], grad_ref[stacked, :]
        key_cols = slice(group * HEAD_WIDTH, (group + 1) * HEAD_WIDTH)
        value_cols = slice(kv_cols + group * HEAD_WIDTH, kv_cols + (group + 1) * HEAD_WIDTH)
        blocks = [*halo_refs, kv_ref]
        key = jnp.concatenate([block[:, key_cols] for block in blocks], axis=0)
        value = jnp.concatenate([block[:, value_cols] for block in blocks], axis=0)
        scores = dot(key, query, 1, 1) * scaling + bias
        raised = jnp.exp(scores - jnp.max(scores, axis=0, keepdims=True))
        weights = raised * (1.0 / jnp.sum(raised, axis=0, keepdims=True))
        weights_half = weights.astype(jnp.bfloat16)
        grad_weights = dot(value, grad, 1, 1)
        delta = jnp.sum(weights_half.astype(jnp.float32) * grad_weights, axis=0, keepdims=True)
        grad_scores = (weights * (grad_weights - delta)).astype(jnp.bfloat16)
        grad_query = (dot(grad_scores, key, 0, 0) * scaling).astype(jnp.bfloat16)
        for member, h in enumerate(heads):
            grad_query_ref[:, h * HEAD_WIDTH : (h + 1) * HEAD_WIDTH] = grad_query[
                member * rows : (member + 1) * rows
            ]
        grad_key = dot(grad_scores, query, 1, 0) * scaling
        grad_value = dot(weights_half, grad, 1, 0)
        start = 0
        for size, out_ref in zip([*halo_rows, rows], [*grad_halo_refs, grad_kv_ref]):
            out_ref[:, key_cols] = grad_key[start : start + size].astype(out_ref.dtype)
            out_ref[:, value_cols] = grad_value[start : start + size].astype(out_ref.dtype)
            start += size


def attention_backward(query, grad, kv, bias, halos):
    rows, kv_cols = kv.shape[0], kv.shape[1] // 2
    kv_heads = kv_cols // HEAD_WIDTH
    group_width = query.shape[0] // (rows * kv_heads)
    query_cols = kv_heads * group_width * HEAD_WIDTH
    halo_rows = [halo.shape[0] for halo in halos]
    span = bias.shape[0]
    whole = pl.BlockSpec(memory_space=pltpu.VMEM)
    outs = [
        jax.ShapeDtypeStruct((rows, query_cols), jnp.bfloat16),
        jax.ShapeDtypeStruct((rows, 2 * kv_cols), jnp.float32),
        *[jax.ShapeDtypeStruct((size, 2 * kv_cols), jnp.bfloat16) for size in halo_rows],
    ]
    return pl.pallas_call(
        functools.partial(attention_kernel, kv_heads, group_width, halo_rows),
        out_shape=outs,
        in_specs=[whole] * (4 + len(halos)),
        out_specs=[whole] * len(outs),
        compiler_params=pltpu.CompilerParams(vmem_limit_bytes=8 * 1024 * 1024),
        cost_estimate=pl.CostEstimate(
            flops=12 * rows * span * query_cols,
            bytes_accessed=4 * rows * query_cols * 2,
            transcendentals=rows * span * kv_heads * group_width,
        ),
    )(query, grad, kv, bias, *halos)


def join_kernel(query_ref, kv_ref, *refs):
    *part_refs, joined_ref = refs
    rows = kv_ref.shape[0]
    query_cols = query_ref.shape[1]
    joined_ref[:, :query_cols] = query_ref[...]
    total = kv_ref[...]
    for part_ref in part_refs:
        size = part_ref.shape[0]
        part = part_ref[...].astype(jnp.float32)
        if size < rows:
            part = jnp.concatenate(
                [jnp.zeros((rows - size, part.shape[1]), jnp.float32), part], axis=0
            )
        total = total + part
    joined_ref[:, query_cols:] = total.astype(jnp.bfloat16)


def join(query_part, kv_part, returned):
    rows, query_cols = query_part.shape
    kv_cols = kv_part.shape[1]
    whole = pl.BlockSpec(memory_space=pltpu.VMEM)
    return pl.pallas_call(
        join_kernel,
        out_shape=jax.ShapeDtypeStruct((rows, query_cols + kv_cols), jnp.bfloat16),
        in_specs=[whole] * (2 + len(returned)),
        out_specs=whole,
        compiler_params=pltpu.CompilerParams(vmem_limit_bytes=8 * 1024 * 1024),
        cost_estimate=pl.CostEstimate(flops=1, bytes_accessed=1, transcendentals=0),
    )(query_part, kv_part, *returned)


def project_kernel(pieces, tile, core_ref, *refs):
    count = len(pieces)
    flat_refs, (query_weight, key_weight, value_weight) = refs[: sum(pieces)], refs[sum(pieces) :][:3]
    keep_refs, give_refs = refs[-2 * count - 2 : -count - 2], refs[-count - 2 : -2]
    full_ref, block_ref = refs[-2:]
    row, at = 0, 0
    for count in pieces:
        column = 0
        for ref in flat_refs[at : at + count]:
            block_ref[row : row + ref.shape[0], column : column + ref.shape[1]] = ref[...]
            column += ref.shape[1]
        at += count
        row += flat_refs[at - 1].shape[0]
    query_cols, kv_cols = query_weight.shape[1], key_weight.shape[1]

    def step(i, carry):
        at = pl.ds(pl.multiple_of(i * tile, 16), tile)
        full_ref[at, :] = (
            dot(query_weight[at, :], block_ref[:, :query_cols], 1, 1)
            + dot(key_weight[at, :], block_ref[:, query_cols : query_cols + kv_cols], 1, 1)
            + dot(value_weight[at, :], block_ref[:, query_cols + kv_cols :], 1, 1)
        )
        return carry

    lax.fori_loop(0, full_ref.shape[0] // tile, step, 0)
    half, rows = give_refs[0].shape
    own = pl.ds(pl.multiple_of(core_ref[0] * half, 8), half)
    other = pl.ds(pl.multiple_of((1 - core_ref[0]) * half, 8), half)
    for i, (keep_ref, give_ref) in enumerate(zip(keep_refs, give_refs)):
        cols = slice(i * rows, (i + 1) * rows)
        keep_ref[...] = full_ref[own, cols]
        give_ref[...] = full_ref[other, cols].astype(jnp.bfloat16)


def project(blocks, weights, core):
    width = weights[0].shape[0]
    rows = sum(block[0].shape[0] for block in blocks)
    half = (width // 2, rows // len(blocks))
    cols = sum(weight.shape[1] for weight in weights)
    tile = max(t for t in range(16, 449, 16) if width % t == 0)
    flat = [piece for block in blocks for piece in block]
    whole = pl.BlockSpec(memory_space=pltpu.VMEM)
    return pl.pallas_call(
        functools.partial(project_kernel, [len(block) for block in blocks], tile),
        out_shape=[jax.ShapeDtypeStruct(half, jnp.float32)] * len(blocks)
        + [jax.ShapeDtypeStruct(half, jnp.bfloat16)] * len(blocks),
        in_specs=[pl.BlockSpec(memory_space=pltpu.SMEM)] + [whole] * (len(flat) + 3),
        out_specs=[whole] * (2 * len(blocks)),
        scratch_shapes=[
            pltpu.VMEM((width, rows), jnp.float32),
            pltpu.VMEM((rows, cols), jnp.bfloat16),
        ],
        compiler_params=pltpu.CompilerParams(vmem_limit_bytes=8 * 1024 * 1024),
        cost_estimate=pl.CostEstimate(
            flops=2 * rows * width * cols,
            bytes_accessed=2 * width * cols + 6 * width * rows,
            transcendentals=0,
        ),
    )(core, *flat, *weights)


def moved(block, axis, by):
    size = lax.axis_size(axis)
    return lax.ppermute(block, axis, [(i, i + by) for i in range(size) if 0 <= i + by < size])


def swapped(block, axis, first):
    pairs = []
    for i in range(first, lax.axis_size(axis) - 1, 2):
        pairs += [(i, i + 1), (i + 1, i)]
    return lax.ppermute(block, axis, pairs)


def after(arrays, *others):
    return lax.optimization_barrier((*arrays, *others))[: len(arrays)]


def passed_along(block, axis, distance):
    devices = range(lax.axis_size(axis))
    return lax.ppermute(block, axis, [((i - distance) % len(devices), i) for i in devices])


def per_device(
    query_rows,
    key_row_matrix,
    value_row_matrix,
    out_grad,
    w_query,
    key_weight,
    value_weight,
    doc_ids,
):
    documents = doc_ids[0]
    tokens = documents.shape[0]
    rows = query_rows.shape[1]
    kv_cols = key_row_matrix.shape[2]
    shards = lax.axis_size("seq")
    place = lax.axis_index("seq")
    back = min(WINDOW, tokens // 3) - 1
    halo_rows = []
    while sum(halo_rows) < back and len(halo_rows) < shards - 1:
        halo_rows.append(min(rows, -(-(back - sum(halo_rows)) // 16) * 16))
    kv = lax.optimization_barrier(
        jnp.concatenate([key_row_matrix[0], value_row_matrix[0]], axis=1)
    )
    halos = [moved(kv[rows - size :], "seq", d) for d, size in enumerate(halo_rows, 1)]
    reach = sum(halo_rows)
    first_row = place * rows
    key_docs = lax.dynamic_slice_in_dim(
        jnp.concatenate([jnp.full((reach,), -1, jnp.int32), documents]), first_row, reach + rows, 0
    )
    query_docs = lax.dynamic_slice_in_dim(documents, first_row, rows, 0)
    offset = (
        jnp.arange(rows, dtype=jnp.int32)[None, :]
        + reach
        - jnp.arange(reach + rows, dtype=jnp.int32)[:, None]
    )
    allowed = (query_docs[None, :] == key_docs[:, None]) & (offset >= 0) & (offset < WINDOW)
    bias = jnp.where(allowed, 0.0, MASKED).astype(jnp.float32)
    kv_heads = kv_cols // HEAD_WIDTH
    query_stack, grad_stack = stack(
        *after((query_rows[0], out_grad[0]), kv), kv_heads, query_rows.shape[2] // kv_cols
    )
    grad_query, grad_kv, *grad_halos = attention_backward(
        query_stack, grad_stack, kv, bias, halos[::-1]
    )
    returned = [moved(part, "seq", -d) for d, part in enumerate(grad_halos[::-1], 1)]
    own = join(grad_query, grad_kv, returned)
    weights = (w_query[0], key_weight[0], value_weight[0])
    core = lax.axis_index("mp").astype(jnp.int32)

    def halves_summed(blocks, *late):
        halves = project([(block,) for block in blocks], weights, core[None])
        sums = []
        for keep, give in zip(halves[: len(blocks)], halves[len(blocks) :]):
            got = passed_along(give, "mp", 1)
            if late:
                (got,) = after((got,), *late)
            sums.append((keep + got.astype(jnp.float32)).astype(jnp.bfloat16))
        return jnp.concatenate(sums, axis=1)

    even = place % 2 == 0
    results, waiting = [], [own]
    by_first, by_second = own, own
    for step in range(1, shards):
        came_first = swapped(by_first, "seq", 0)
        last = step == shards - 1 and shards % 2 == 0
        came_second = came_first if last else swapped(by_second, "seq", 1)
        if step > 1:
            waiting = after(waiting, total, *results[-2:-1])
        late = (came_second, came_first) if step > 1 else ()
        if step > 2:
            late += (results[-1],)
        total = halves_summed(waiting, *late)
        results.append(passed_along(total, "section", -1))
        by_first, by_second = came_second, came_first
        if last:
            waiting = [came_first]
        elif 2 * step < shards:
            waiting = [came_second, came_first]
        else:
            waiting = [jnp.where(even == (place >= step), came_second, came_first)]
    if shards > 1:
        waiting = after(waiting, total)
    results.append(passed_along(halves_summed(waiting), "section", -1))
    for step, block in enumerate(results):
        if block.shape[1] == rows:
            results[step] = [block]
        else:
            second, first = block[:, :rows], block[:, rows:]
            results[step] = [jnp.where(even, second, first), jnp.where(even, first, second)]
    upstream = jnp.zeros((results[0][0].shape[0], tokens), jnp.bfloat16)
    for s in range(shards):
        behind = results[s][0]
        ahead = results[(shards - s) % shards][-1]
        block = jnp.where(place >= s, behind, ahead)
        upstream = lax.dynamic_update_slice_in_dim(
            upstream, block, ((place - s) % shards) * rows, 1
        )
    return upstream.T[None]


def solution(mesh):
    placed = P("section", "seq", "mp")
    return jax.shard_map(
        per_device,
        mesh=mesh,
        in_specs=(placed,) * 7 + (P("section", None),),
        out_specs=P("section", None, ("seq", "mp")),
        check_vma=False,
    )
```

```python
import functools
import math

import jax
import jax.numpy as jnp
from jax import lax
from jax.experimental import pallas as pl
from jax.experimental.pallas import tpu as pltpu
from jax.sharding import PartitionSpec as P

HEAD_WIDTH = 128
WINDOW = 512
MASKED = -1e30


def dot(left, right, left_dim, right_dim):
    return lax.dot_general(
        left,
        right,
        (((left_dim,), (right_dim,)), ((), ())),
        preferred_element_type=jnp.float32,
    )


def stack_kernel(kv_heads, group_width, query_ref, grad_ref, query_out, grad_out):
    rows = query_ref.shape[0]
    for head in range(kv_heads * group_width):
        cols = slice(head * HEAD_WIDTH, (head + 1) * HEAD_WIDTH)
        query_out[head * rows : (head + 1) * rows, :] = query_ref[:, cols]
        grad_out[head * rows : (head + 1) * rows, :] = grad_ref[:, cols]


def stack(query, grad, kv_heads, group_width):
    rows, query_cols = query.shape
    whole = pl.BlockSpec(memory_space=pltpu.VMEM)
    shape = jax.ShapeDtypeStruct((rows * kv_heads * group_width, HEAD_WIDTH), jnp.bfloat16)
    return pl.pallas_call(
        functools.partial(stack_kernel, kv_heads, group_width),
        out_shape=[shape] * 2,
        in_specs=[whole] * 2,
        out_specs=[whole] * 2,
        compiler_params=pltpu.CompilerParams(vmem_limit_bytes=8 * 1024 * 1024),
        cost_estimate=pl.CostEstimate(flops=1, bytes_accessed=1, transcendentals=0),
    )(query, grad)


def attention_kernel(kv_heads, group_width, halo_rows, *refs):
    halo_count = len(halo_rows)
    query_ref, grad_ref, kv_ref, bias_ref = refs[:4]
    halo_refs = refs[4 : 4 + halo_count]
    grad_query_ref, grad_kv_ref = refs[4 + halo_count : 6 + halo_count]
    grad_halo_refs = refs[6 + halo_count :]
    rows = kv_ref.shape[0]
    kv_cols = kv_heads * HEAD_WIDTH
    scaling = 1.0 / math.sqrt(HEAD_WIDTH)
    bias = jnp.concatenate([bias_ref[...]] * group_width, axis=1)
    for group in range(kv_heads):
        heads = [group * group_width + member for member in range(group_width)]
        stacked = slice(heads[0] * rows, (heads[-1] + 1) * rows)
        query, grad = query_ref[stacked, :], grad_ref[stacked, :]
        key_cols = slice(group * HEAD_WIDTH, (group + 1) * HEAD_WIDTH)
        value_cols = slice(kv_cols + group * HEAD_WIDTH, kv_cols + (group + 1) * HEAD_WIDTH)
        blocks = [*halo_refs, kv_ref]
        key = jnp.concatenate([block[:, key_cols] for block in blocks], axis=0)
        value = jnp.concatenate([block[:, value_cols] for block in blocks], axis=0)
        scores = dot(key, query, 1, 1) * scaling + bias
        raised = jnp.exp(scores - jnp.max(scores, axis=0, keepdims=True))
        weights = raised * (1.0 / jnp.sum(raised, axis=0, keepdims=True))
        weights_half = weights.astype(jnp.bfloat16)
        grad_weights = dot(value, grad, 1, 1)
        delta = jnp.sum(weights_half.astype(jnp.float32) * grad_weights, axis=0, keepdims=True)
        grad_scores = (weights * (grad_weights - delta)).astype(jnp.bfloat16)
        grad_query = (dot(grad_scores, key, 0, 0) * scaling).astype(jnp.bfloat16)
        for member, h in enumerate(heads):
            grad_query_ref[:, h * HEAD_WIDTH : (h + 1) * HEAD_WIDTH] = grad_query[
                member * rows : (member + 1) * rows
            ]
        grad_key = dot(grad_scores, query, 1, 0) * scaling
        grad_value = dot(weights_half, grad, 1, 0)
        start = 0
        for size, out_ref in zip([*halo_rows, rows], [*grad_halo_refs, grad_kv_ref]):
            out_ref[:, key_cols] = grad_key[start : start + size].astype(out_ref.dtype)
            out_ref[:, value_cols] = grad_value[start : start + size].astype(out_ref.dtype)
            start += size


def attention_backward(query, grad, kv, bias, halos):
    rows, kv_cols = kv.shape[0], kv.shape[1] // 2
    kv_heads = kv_cols // HEAD_WIDTH
    group_width = query.shape[0] // (rows * kv_heads)
    query_cols = kv_heads * group_width * HEAD_WIDTH
    halo_rows = [halo.shape[0] for halo in halos]
    span = bias.shape[0]
    whole = pl.BlockSpec(memory_space=pltpu.VMEM)
    outs = [
        jax.ShapeDtypeStruct((rows, query_cols), jnp.bfloat16),
        jax.ShapeDtypeStruct((rows, 2 * kv_cols), jnp.float32),
        *[jax.ShapeDtypeStruct((size, 2 * kv_cols), jnp.bfloat16) for size in halo_rows],
    ]
    return pl.pallas_call(
        functools.partial(attention_kernel, kv_heads, group_width, halo_rows),
        out_shape=outs,
        in_specs=[whole] * (4 + len(halos)),
        out_specs=[whole] * len(outs),
        compiler_params=pltpu.CompilerParams(vmem_limit_bytes=8 * 1024 * 1024),
        cost_estimate=pl.CostEstimate(
            flops=12 * rows * span * query_cols,
            bytes_accessed=4 * rows * query_cols * 2,
            transcendentals=rows * span * kv_heads * group_width,
        ),
    )(query, grad, kv, bias, *halos)


def join_kernel(query_ref, kv_ref, *refs):
    *part_refs, joined_ref = refs
    rows = kv_ref.shape[0]
    query_cols = query_ref.shape[1]
    joined_ref[:, :query_cols] = query_ref[...]
    total = kv_ref[...]
    for part_ref in part_refs:
        size = part_ref.shape[0]
        part = part_ref[...].astype(jnp.float32)
        if size < rows:
            part = jnp.concatenate(
                [jnp.zeros((rows - size, part.shape[1]), jnp.float32), part], axis=0
            )
        total = total + part
    joined_ref[:, query_cols:] = total.astype(jnp.bfloat16)


def join(query_part, kv_part, returned):
    rows, query_cols = query_part.shape
    kv_cols = kv_part.shape[1]
    whole = pl.BlockSpec(memory_space=pltpu.VMEM)
    return pl.pallas_call(
        join_kernel,
        out_shape=jax.ShapeDtypeStruct((rows, query_cols + kv_cols), jnp.bfloat16),
        in_specs=[whole] * (2 + len(returned)),
        out_specs=whole,
        compiler_params=pltpu.CompilerParams(vmem_limit_bytes=8 * 1024 * 1024),
        cost_estimate=pl.CostEstimate(flops=1, bytes_accessed=1, transcendentals=0),
    )(query_part, kv_part, *returned)


def project_kernel(pieces, tile, core_ref, *refs):
    count = len(pieces)
    flat_refs, (query_weight, key_weight, value_weight) = refs[: sum(pieces)], refs[sum(pieces) :][:3]
    keep_refs, give_refs = refs[-2 * count - 2 : -count - 2], refs[-count - 2 : -2]
    full_ref, block_ref = refs[-2:]
    row, at = 0, 0
    for count in pieces:
        column = 0
        for ref in flat_refs[at : at + count]:
            block_ref[row : row + ref.shape[0], column : column + ref.shape[1]] = ref[...]
            column += ref.shape[1]
        at += count
        row += flat_refs[at - 1].shape[0]
    query_cols, kv_cols = query_weight.shape[1], key_weight.shape[1]

    def step(i, carry):
        at = pl.ds(pl.multiple_of(i * tile, 16), tile)
        full_ref[at, :] = (
            dot(query_weight[at, :], block_ref[:, :query_cols], 1, 1)
            + dot(key_weight[at, :], block_ref[:, query_cols : query_cols + kv_cols], 1, 1)
            + dot(value_weight[at, :], block_ref[:, query_cols + kv_cols :], 1, 1)
        )
        return carry

    lax.fori_loop(0, full_ref.shape[0] // tile, step, 0)
    half, rows = give_refs[0].shape
    own = pl.ds(pl.multiple_of(core_ref[0] * half, 8), half)
    other = pl.ds(pl.multiple_of((1 - core_ref[0]) * half, 8), half)
    for i, (keep_ref, give_ref) in enumerate(zip(keep_refs, give_refs)):
        cols = slice(i * rows, (i + 1) * rows)
        keep_ref[...] = full_ref[own, cols]
        give_ref[...] = full_ref[other, cols].astype(jnp.bfloat16)


def project(blocks, weights, core):
    width = weights[0].shape[0]
    rows = sum(block[0].shape[0] for block in blocks)
    half = (width // 2, rows // len(blocks))
    cols = sum(weight.shape[1] for weight in weights)
    tile = max(t for t in range(16, 449, 16) if width % t == 0)
    flat = [piece for block in blocks for piece in block]
    whole = pl.BlockSpec(memory_space=pltpu.VMEM)
    return pl.pallas_call(
        functools.partial(project_kernel, [len(block) for block in blocks], tile),
        out_shape=[jax.ShapeDtypeStruct(half, jnp.float32)] * len(blocks)
        + [jax.ShapeDtypeStruct(half, jnp.bfloat16)] * len(blocks),
        in_specs=[pl.BlockSpec(memory_space=pltpu.SMEM)] + [whole] * (len(flat) + 3),
        out_specs=[whole] * (2 * len(blocks)),
        scratch_shapes=[
            pltpu.VMEM((width, rows), jnp.float32),
            pltpu.VMEM((rows, cols), jnp.bfloat16),
        ],
        compiler_params=pltpu.CompilerParams(vmem_limit_bytes=8 * 1024 * 1024),
        cost_estimate=pl.CostEstimate(
            flops=2 * rows * width * cols,
            bytes_accessed=2 * width * cols + 6 * width * rows,
            transcendentals=0,
        ),
    )(core, *flat, *weights)


def moved(block, axis, by):
    size = lax.axis_size(axis)
    return lax.ppermute(block, axis, [(i, i + by) for i in range(size) if 0 <= i + by < size])


def swapped(block, axis, first):
    pairs = []
    for i in range(first, lax.axis_size(axis) - 1, 2):
        pairs += [(i, i + 1), (i + 1, i)]
    return lax.ppermute(block, axis, pairs)


def after(arrays, *others):
    return lax.optimization_barrier((*arrays, *others))[: len(arrays)]


def passed_along(block, axis, distance):
    devices = range(lax.axis_size(axis))
    return lax.ppermute(block, axis, [((i - distance) % len(devices), i) for i in devices])


def per_device(
    query_rows,
    key_row_matrix,
    value_row_matrix,
    out_grad,
    w_query,
    key_weight,
    value_weight,
    doc_ids,
):
    documents = doc_ids[0]
    tokens = documents.shape[0]
    rows = query_rows.shape[1]
    kv_cols = key_row_matrix.shape[2]
    shards = lax.axis_size("seq")
    place = lax.axis_index("seq")
    back = min(WINDOW, tokens // 3) - 1
    halo_rows = []
    while sum(halo_rows) < back and len(halo_rows) < shards - 1:
        halo_rows.append(min(rows, -(-(back - sum(halo_rows)) // 16) * 16))
    kv = lax.optimization_barrier(
        jnp.concatenate([key_row_matrix[0], value_row_matrix[0]], axis=1)
    )
    halos = [moved(kv[rows - size :], "seq", d) for d, size in enumerate(halo_rows, 1)]
    reach = sum(halo_rows)
    first_row = place * rows
    key_docs = lax.dynamic_slice_in_dim(
        jnp.concatenate([jnp.full((reach,), -1, jnp.int32), documents]), first_row, reach + rows, 0
    )
    query_docs = lax.dynamic_slice_in_dim(documents, first_row, rows, 0)
    offset = (
        jnp.arange(rows, dtype=jnp.int32)[None, :]
        + reach
        - jnp.arange(reach + rows, dtype=jnp.int32)[:, None]
    )
    allowed = (query_docs[None, :] == key_docs[:, None]) & (offset >= 0) & (offset < WINDOW)
    bias = jnp.where(allowed, 0.0, MASKED).astype(jnp.float32)
    kv_heads = kv_cols // HEAD_WIDTH
    query_stack, grad_stack = stack(
        *after((query_rows[0], out_grad[0]), kv), kv_heads, query_rows.shape[2] // kv_cols
    )
    grad_query, grad_kv, *grad_halos = attention_backward(
        query_stack, grad_stack, kv, bias, halos[::-1]
    )
    returned = [moved(part, "seq", -d) for d, part in enumerate(grad_halos[::-1], 1)]
    own = join(grad_query, grad_kv, returned)
    weights = (w_query[0], key_weight[0], value_weight[0])
    core = lax.axis_index("mp").astype(jnp.int32)

    def halves_summed(blocks, *late):
        halves = project([(block,) for block in blocks], weights, core[None])
        sums = []
        for keep, give in zip(halves[: len(blocks)], halves[len(blocks) :]):
            got = passed_along(give, "mp", 1)
            if late:
                (got,) = after((got,), *late)
            sums.append((keep + got.astype(jnp.float32)).astype(jnp.bfloat16))
        return sums

    even = place % 2 == 0
    results, waiting = [], [own]
    by_first, by_second = own, own
    for step in range(1, shards):
        came_first = swapped(by_first, "seq", 0)
        last = step == shards - 1 and shards % 2 == 0
        came_second = came_first if last else swapped(by_second, "seq", 1)
        if step > 1:
            waiting = after(waiting, *sums, *(results[-2] if step > 2 else ()))
        late = (came_first, came_second) if step > 1 else ()
        sums = halves_summed(waiting, *late, *(results[-1] if step > 2 else ()))
        results.append([passed_along(block, "section", -1) for block in sums])
        by_first, by_second = came_second, came_first
        if last:
            waiting = [came_first]
        elif 2 * step < shards:
            waiting = [came_first, came_second]
        else:
            waiting = [jnp.where(even == (place >= step), came_second, came_first)]
    if shards > 1:
        waiting = after(waiting, *sums)
    sums = halves_summed(waiting, *(results[-1] if shards > 1 else ()))
    results.append([passed_along(block, "section", -1) for block in sums])
    for step, blocks in enumerate(results):
        if len(blocks) > 1:
            first, second = blocks
            results[step] = [jnp.where(even, second, first), jnp.where(even, first, second)]
    upstream = jnp.zeros((results[0][0].shape[0], tokens), jnp.bfloat16)
    for s in range(shards):
        behind = results[s][0]
        ahead = results[(shards - s) % shards][-1]
        block = jnp.where(place >= s, behind, ahead)
        upstream = lax.dynamic_update_slice_in_dim(
            upstream, block, ((place - s) % shards) * rows, 1
        )
    return upstream.T[None]


def solution(mesh):
    placed = P("section", "seq", "mp")
    return jax.shard_map(
        per_device,
        mesh=mesh,
        in_specs=(placed,) * 7 + (P("section", None),),
        out_specs=P("section", None, ("seq", "mp")),
        check_vma=False,
    )
```

```python
import functools
import math

import jax
import jax.numpy as jnp
from jax import lax
from jax.experimental import pallas as pl
from jax.experimental.pallas import tpu as pltpu
from jax.sharding import PartitionSpec as P

HEAD_WIDTH = 128
WINDOW = 512
MASKED = -1e30


def dot(left, right, left_dim, right_dim):
    return lax.dot_general(
        left,
        right,
        (((left_dim,), (right_dim,)), ((), ())),
        preferred_element_type=jnp.float32,
    )


def stack_kernel(kv_heads, group_width, query_ref, grad_ref, query_out, grad_out):
    rows = query_ref.shape[0]
    for head in range(kv_heads * group_width):
        cols = slice(head * HEAD_WIDTH, (head + 1) * HEAD_WIDTH)
        query_out[head * rows : (head + 1) * rows, :] = query_ref[:, cols]
        grad_out[head * rows : (head + 1) * rows, :] = grad_ref[:, cols]


def stack(query, grad, kv_heads, group_width):
    rows, query_cols = query.shape
    whole = pl.BlockSpec(memory_space=pltpu.VMEM)
    shape = jax.ShapeDtypeStruct((rows * kv_heads * group_width, HEAD_WIDTH), jnp.bfloat16)
    return pl.pallas_call(
        functools.partial(stack_kernel, kv_heads, group_width),
        out_shape=[shape] * 2,
        in_specs=[whole] * 2,
        out_specs=[whole] * 2,
        compiler_params=pltpu.CompilerParams(vmem_limit_bytes=8 * 1024 * 1024),
        cost_estimate=pl.CostEstimate(flops=1, bytes_accessed=1, transcendentals=0),
    )(query, grad)


def attention_kernel(kv_heads, group_width, halo_rows, *refs):
    halo_count = len(halo_rows)
    query_ref, grad_ref, kv_ref, bias_ref = refs[:4]
    halo_refs = refs[4 : 4 + halo_count]
    grad_query_ref, grad_kv_ref = refs[4 + halo_count : 6 + halo_count]
    grad_halo_refs = refs[6 + halo_count :]
    rows = kv_ref.shape[0]
    kv_cols = kv_heads * HEAD_WIDTH
    scaling = 1.0 / math.sqrt(HEAD_WIDTH)
    bias = jnp.concatenate([bias_ref[...]] * group_width, axis=1)
    for group in range(kv_heads):
        heads = [group * group_width + member for member in range(group_width)]
        stacked = slice(heads[0] * rows, (heads[-1] + 1) * rows)
        query, grad = query_ref[stacked, :], grad_ref[stacked, :]
        key_cols = slice(group * HEAD_WIDTH, (group + 1) * HEAD_WIDTH)
        value_cols = slice(kv_cols + group * HEAD_WIDTH, kv_cols + (group + 1) * HEAD_WIDTH)
        blocks = [*halo_refs, kv_ref]
        key = jnp.concatenate([block[:, key_cols] for block in blocks], axis=0)
        value = jnp.concatenate([block[:, value_cols] for block in blocks], axis=0)
        scores = dot(key, query, 1, 1) * scaling + bias
        raised = jnp.exp(scores - jnp.max(scores, axis=0, keepdims=True))
        weights = raised * (1.0 / jnp.sum(raised, axis=0, keepdims=True))
        weights_half = weights.astype(jnp.bfloat16)
        grad_weights = dot(value, grad, 1, 1)
        delta = jnp.sum(weights_half.astype(jnp.float32) * grad_weights, axis=0, keepdims=True)
        grad_scores = (weights * (grad_weights - delta)).astype(jnp.bfloat16)
        grad_query = (dot(grad_scores, key, 0, 0) * scaling).astype(jnp.bfloat16)
        for member, h in enumerate(heads):
            grad_query_ref[:, h * HEAD_WIDTH : (h + 1) * HEAD_WIDTH] = grad_query[
                member * rows : (member + 1) * rows
            ]
        grad_key = dot(grad_scores, query, 1, 0) * scaling
        grad_value = dot(weights_half, grad, 1, 0)
        start = 0
        for size, out_ref in zip([*halo_rows, rows], [*grad_halo_refs, grad_kv_ref]):
            out_ref[:, key_cols] = grad_key[start : start + size].astype(out_ref.dtype)
            out_ref[:, value_cols] = grad_value[start : start + size].astype(out_ref.dtype)
            start += size


def attention_backward(query, grad, kv, bias, halos):
    rows, kv_cols = kv.shape[0], kv.shape[1] // 2
    kv_heads = kv_cols // HEAD_WIDTH
    group_width = query.shape[0] // (rows * kv_heads)
    query_cols = kv_heads * group_width * HEAD_WIDTH
    halo_rows = [halo.shape[0] for halo in halos]
    span = bias.shape[0]
    whole = pl.BlockSpec(memory_space=pltpu.VMEM)
    outs = [
        jax.ShapeDtypeStruct((rows, query_cols), jnp.bfloat16),
        jax.ShapeDtypeStruct((rows, 2 * kv_cols), jnp.float32),
        *[jax.ShapeDtypeStruct((size, 2 * kv_cols), jnp.bfloat16) for size in halo_rows],
    ]
    return pl.pallas_call(
        functools.partial(attention_kernel, kv_heads, group_width, halo_rows),
        out_shape=outs,
        in_specs=[whole] * (4 + len(halos)),
        out_specs=[whole] * len(outs),
        compiler_params=pltpu.CompilerParams(vmem_limit_bytes=8 * 1024 * 1024),
        cost_estimate=pl.CostEstimate(
            flops=12 * rows * span * query_cols,
            bytes_accessed=4 * rows * query_cols * 2,
            transcendentals=rows * span * kv_heads * group_width,
        ),
    )(query, grad, kv, bias, *halos)


def join_kernel(query_ref, kv_ref, *refs):
    *part_refs, joined_ref = refs
    rows = kv_ref.shape[0]
    query_cols = query_ref.shape[1]
    joined_ref[:, :query_cols] = query_ref[...]
    total = kv_ref[...]
    for part_ref in part_refs:
        size = part_ref.shape[0]
        part = part_ref[...].astype(jnp.float32)
        if size < rows:
            part = jnp.concatenate(
                [jnp.zeros((rows - size, part.shape[1]), jnp.float32), part], axis=0
            )
        total = total + part
    joined_ref[:, query_cols:] = total.astype(jnp.bfloat16)


def join(query_part, kv_part, returned):
    rows, query_cols = query_part.shape
    kv_cols = kv_part.shape[1]
    whole = pl.BlockSpec(memory_space=pltpu.VMEM)
    return pl.pallas_call(
        join_kernel,
        out_shape=jax.ShapeDtypeStruct((rows, query_cols + kv_cols), jnp.bfloat16),
        in_specs=[whole] * (2 + len(returned)),
        out_specs=whole,
        compiler_params=pltpu.CompilerParams(vmem_limit_bytes=8 * 1024 * 1024),
        cost_estimate=pl.CostEstimate(flops=1, bytes_accessed=1, transcendentals=0),
    )(query_part, kv_part, *returned)


def project_kernel(pieces, tile, core_ref, *refs):
    count = len(pieces)
    flat_refs, (query_weight, key_weight, value_weight) = refs[: sum(pieces)], refs[sum(pieces) :][:3]
    keep_refs, give_refs = refs[-2 * count - 2 : -count - 2], refs[-count - 2 : -2]
    full_ref, block_ref = refs[-2:]
    row, at = 0, 0
    for count in pieces:
        column = 0
        for ref in flat_refs[at : at + count]:
            block_ref[row : row + ref.shape[0], column : column + ref.shape[1]] = ref[...]
            column += ref.shape[1]
        at += count
        row += flat_refs[at - 1].shape[0]
    query_cols, kv_cols = query_weight.shape[1], key_weight.shape[1]

    def step(i, carry):
        at = pl.ds(pl.multiple_of(i * tile, 16), tile)
        full_ref[at, :] = (
            dot(query_weight[at, :], block_ref[:, :query_cols], 1, 1)
            + dot(key_weight[at, :], block_ref[:, query_cols : query_cols + kv_cols], 1, 1)
            + dot(value_weight[at, :], block_ref[:, query_cols + kv_cols :], 1, 1)
        )
        return carry

    lax.fori_loop(0, full_ref.shape[0] // tile, step, 0)
    half, rows = give_refs[0].shape
    own = pl.ds(pl.multiple_of(core_ref[0] * half, 8), half)
    other = pl.ds(pl.multiple_of((1 - core_ref[0]) * half, 8), half)
    for i, (keep_ref, give_ref) in enumerate(zip(keep_refs, give_refs)):
        cols = slice(i * rows, (i + 1) * rows)
        keep_ref[...] = full_ref[own, cols]
        give_ref[...] = full_ref[other, cols].astype(jnp.bfloat16)


def project(blocks, weights, core):
    width = weights[0].shape[0]
    rows = sum(block[0].shape[0] for block in blocks)
    half = (width // 2, rows // len(blocks))
    cols = sum(weight.shape[1] for weight in weights)
    tile = max(t for t in range(16, 449, 16) if width % t == 0)
    flat = [piece for block in blocks for piece in block]
    whole = pl.BlockSpec(memory_space=pltpu.VMEM)
    return pl.pallas_call(
        functools.partial(project_kernel, [len(block) for block in blocks], tile),
        out_shape=[jax.ShapeDtypeStruct(half, jnp.float32)] * len(blocks)
        + [jax.ShapeDtypeStruct(half, jnp.bfloat16)] * len(blocks),
        in_specs=[pl.BlockSpec(memory_space=pltpu.SMEM)] + [whole] * (len(flat) + 3),
        out_specs=[whole] * (2 * len(blocks)),
        scratch_shapes=[
            pltpu.VMEM((width, rows), jnp.float32),
            pltpu.VMEM((rows, cols), jnp.bfloat16),
        ],
        compiler_params=pltpu.CompilerParams(vmem_limit_bytes=8 * 1024 * 1024),
        cost_estimate=pl.CostEstimate(
            flops=2 * rows * width * cols,
            bytes_accessed=2 * width * cols + 6 * width * rows,
            transcendentals=0,
        ),
    )(core, *flat, *weights)


def moved(block, axis, by):
    size = lax.axis_size(axis)
    return lax.ppermute(block, axis, [(i, i + by) for i in range(size) if 0 <= i + by < size])


def swapped(block, axis, first):
    pairs = []
    for i in range(first, lax.axis_size(axis) - 1, 2):
        pairs += [(i, i + 1), (i + 1, i)]
    return lax.ppermute(block, axis, pairs)


def after(arrays, *others):
    return lax.optimization_barrier((*arrays, *others))[: len(arrays)]


def passed_along(block, axis, distance):
    devices = range(lax.axis_size(axis))
    return lax.ppermute(block, axis, [((i - distance) % len(devices), i) for i in devices])


def per_device(
    query_rows,
    key_row_matrix,
    value_row_matrix,
    out_grad,
    w_query,
    key_weight,
    value_weight,
    doc_ids,
):
    documents = doc_ids[0]
    tokens = documents.shape[0]
    rows = query_rows.shape[1]
    kv_cols = key_row_matrix.shape[2]
    shards = lax.axis_size("seq")
    place = lax.axis_index("seq")
    back = min(WINDOW, tokens // 3) - 1
    halo_rows = []
    while sum(halo_rows) < back and len(halo_rows) < shards - 1:
        halo_rows.append(min(rows, -(-(back - sum(halo_rows)) // 16) * 16))
    kv = lax.optimization_barrier(
        jnp.concatenate([key_row_matrix[0], value_row_matrix[0]], axis=1)
    )
    halos = [moved(kv[rows - size :], "seq", d) for d, size in enumerate(halo_rows, 1)]
    reach = sum(halo_rows)
    first_row = place * rows
    key_docs = lax.dynamic_slice_in_dim(
        jnp.concatenate([jnp.full((reach,), -1, jnp.int32), documents]), first_row, reach + rows, 0
    )
    query_docs = lax.dynamic_slice_in_dim(documents, first_row, rows, 0)
    offset = (
        jnp.arange(rows, dtype=jnp.int32)[None, :]
        + reach
        - jnp.arange(reach + rows, dtype=jnp.int32)[:, None]
    )
    allowed = (query_docs[None, :] == key_docs[:, None]) & (offset >= 0) & (offset < WINDOW)
    bias = jnp.where(allowed, 0.0, MASKED).astype(jnp.float32)
    kv_heads = kv_cols // HEAD_WIDTH
    query_stack, grad_stack = stack(
        *after((query_rows[0], out_grad[0]), kv), kv_heads, query_rows.shape[2] // kv_cols
    )
    grad_query, grad_kv, *grad_halos = attention_backward(
        query_stack, grad_stack, kv, bias, halos[::-1]
    )
    returned = [moved(part, "seq", -d) for d, part in enumerate(grad_halos[::-1], 1)]
    own = join(grad_query, grad_kv, returned)
    weights = (w_query[0], key_weight[0], value_weight[0])
    core = lax.axis_index("mp").astype(jnp.int32)

    def halves_summed(blocks, late, before=()):
        halves = project([(block,) for block in blocks], weights, core[None])
        sums = []
        for keep, give in zip(halves[: len(blocks)], halves[len(blocks) :]):
            if before:
                (give,) = after((give,), *before)
            got = passed_along(give, "mp", 1)
            if late:
                (got,) = after((got,), *late)
            sums.append((keep + got.astype(jnp.float32)).astype(jnp.bfloat16))
        return sums

    even = place % 2 == 0
    results, waiting = [], [own]
    by_first, by_second = own, own
    for step in range(1, shards):
        came_first = swapped(by_first, "seq", 0)
        last = step == shards - 1 and shards % 2 == 0
        came_second = came_first if last else swapped(by_second, "seq", 1)
        if step > 1:
            waiting = after(waiting, *sums, *(results[-2] if step > 2 else ()))
        late = (came_first, came_second) if step > 1 else ()
        sums = halves_summed(waiting, late)
        results.append([passed_along(block, "section", -1) for block in sums])
        by_first, by_second = came_second, came_first
        if last:
            waiting = [came_first]
        elif 2 * step < shards:
            waiting = [came_first, came_second]
        else:
            waiting = [jnp.where(even == (place >= step), came_second, came_first)]
    if shards > 1:
        waiting = after(waiting, *sums)
    sums = halves_summed(waiting, (), results[-2] if shards > 2 else ())
    results.append([passed_along(block, "section", -1) for block in sums])
    for step, blocks in enumerate(results):
        if len(blocks) > 1:
            first, second = blocks
            results[step] = [jnp.where(even, second, first), jnp.where(even, first, second)]
    upstream = jnp.zeros((results[0][0].shape[0], tokens), jnp.bfloat16)
    for s in range(shards):
        behind = results[s][0]
        ahead = results[(shards - s) % shards][-1]
        block = jnp.where(place >= s, behind, ahead)
        upstream = lax.dynamic_update_slice_in_dim(
            upstream, block, ((place - s) % shards) * rows, 1
        )
    return upstream.T[None]


def solution(mesh):
    placed = P("section", "seq", "mp")
    return jax.shard_map(
        per_device,
        mesh=mesh,
        in_specs=(placed,) * 7 + (P("section", None),),
        out_specs=P("section", None, ("seq", "mp")),
        check_vma=False,
    )
```

```python
import functools
import math

import jax
import jax.numpy as jnp
from jax import lax
from jax.experimental import pallas as pl
from jax.experimental.pallas import tpu as pltpu
from jax.sharding import PartitionSpec as P

HEAD_WIDTH = 128
WINDOW = 512
MASKED = -1e30


def dot(left, right, left_dim, right_dim):
    return lax.dot_general(
        left,
        right,
        (((left_dim,), (right_dim,)), ((), ())),
        preferred_element_type=jnp.float32,
    )


def stack_kernel(kv_heads, group_width, query_ref, grad_ref, query_out, grad_out):
    rows = query_ref.shape[0]
    for head in range(kv_heads * group_width):
        cols = slice(head * HEAD_WIDTH, (head + 1) * HEAD_WIDTH)
        query_out[head * rows : (head + 1) * rows, :] = query_ref[:, cols]
        grad_out[head * rows : (head + 1) * rows, :] = grad_ref[:, cols]


def stack(query, grad, kv_heads, group_width):
    rows, query_cols = query.shape
    whole = pl.BlockSpec(memory_space=pltpu.VMEM)
    shape = jax.ShapeDtypeStruct((rows * kv_heads * group_width, HEAD_WIDTH), jnp.bfloat16)
    return pl.pallas_call(
        functools.partial(stack_kernel, kv_heads, group_width),
        out_shape=[shape] * 2,
        in_specs=[whole] * 2,
        out_specs=[whole] * 2,
        compiler_params=pltpu.CompilerParams(vmem_limit_bytes=8 * 1024 * 1024),
        cost_estimate=pl.CostEstimate(flops=1, bytes_accessed=1, transcendentals=0),
    )(query, grad)


def attention_kernel(kv_heads, group_width, halo_rows, *refs):
    halo_count = len(halo_rows)
    query_ref, grad_ref, kv_ref, bias_ref = refs[:4]
    halo_refs = refs[4 : 4 + halo_count]
    grad_query_ref, grad_kv_ref = refs[4 + halo_count : 6 + halo_count]
    grad_halo_refs = refs[6 + halo_count :]
    rows = kv_ref.shape[0]
    kv_cols = kv_heads * HEAD_WIDTH
    scaling = 1.0 / math.sqrt(HEAD_WIDTH)
    bias = jnp.concatenate([bias_ref[...]] * group_width, axis=1)
    for group in range(kv_heads):
        heads = [group * group_width + member for member in range(group_width)]
        stacked = slice(heads[0] * rows, (heads[-1] + 1) * rows)
        query, grad = query_ref[stacked, :], grad_ref[stacked, :]
        key_cols = slice(group * HEAD_WIDTH, (group + 1) * HEAD_WIDTH)
        value_cols = slice(kv_cols + group * HEAD_WIDTH, kv_cols + (group + 1) * HEAD_WIDTH)
        blocks = [*halo_refs, kv_ref]
        key = jnp.concatenate([block[:, key_cols] for block in blocks], axis=0)
        value = jnp.concatenate([block[:, value_cols] for block in blocks], axis=0)
        scores = dot(key, query, 1, 1) * scaling + bias
        raised = jnp.exp(scores - jnp.max(scores, axis=0, keepdims=True))
        weights = raised * (1.0 / jnp.sum(raised, axis=0, keepdims=True))
        weights_half = weights.astype(jnp.bfloat16)
        grad_weights = dot(value, grad, 1, 1)
        delta = jnp.sum(weights_half.astype(jnp.float32) * grad_weights, axis=0, keepdims=True)
        grad_scores = (weights * (grad_weights - delta)).astype(jnp.bfloat16)
        grad_query = (dot(grad_scores, key, 0, 0) * scaling).astype(jnp.bfloat16)
        for member, h in enumerate(heads):
            grad_query_ref[:, h * HEAD_WIDTH : (h + 1) * HEAD_WIDTH] = grad_query[
                member * rows : (member + 1) * rows
            ]
        grad_key = dot(grad_scores, query, 1, 0) * scaling
        grad_value = dot(weights_half, grad, 1, 0)
        start = 0
        for size, out_ref in zip([*halo_rows, rows], [*grad_halo_refs, grad_kv_ref]):
            out_ref[:, key_cols] = grad_key[start : start + size].astype(out_ref.dtype)
            out_ref[:, value_cols] = grad_value[start : start + size].astype(out_ref.dtype)
            start += size


def attention_backward(query, grad, kv, bias, halos):
    rows, kv_cols = kv.shape[0], kv.shape[1] // 2
    kv_heads = kv_cols // HEAD_WIDTH
    group_width = query.shape[0] // (rows * kv_heads)
    query_cols = kv_heads * group_width * HEAD_WIDTH
    halo_rows = [halo.shape[0] for halo in halos]
    span = bias.shape[0]
    whole = pl.BlockSpec(memory_space=pltpu.VMEM)
    outs = [
        jax.ShapeDtypeStruct((rows, query_cols), jnp.bfloat16),
        jax.ShapeDtypeStruct((rows, 2 * kv_cols), jnp.float32),
        *[jax.ShapeDtypeStruct((size, 2 * kv_cols), jnp.bfloat16) for size in halo_rows],
    ]
    return pl.pallas_call(
        functools.partial(attention_kernel, kv_heads, group_width, halo_rows),
        out_shape=outs,
        in_specs=[whole] * (4 + len(halos)),
        out_specs=[whole] * len(outs),
        compiler_params=pltpu.CompilerParams(vmem_limit_bytes=8 * 1024 * 1024),
        cost_estimate=pl.CostEstimate(
            flops=12 * rows * span * query_cols,
            bytes_accessed=4 * rows * query_cols * 2,
            transcendentals=rows * span * kv_heads * group_width,
        ),
    )(query, grad, kv, bias, *halos)


def join_kernel(query_ref, kv_ref, *refs):
    *part_refs, joined_ref = refs
    rows = kv_ref.shape[0]
    query_cols = query_ref.shape[1]
    joined_ref[:, :query_cols] = query_ref[...]
    total = kv_ref[...]
    for part_ref in part_refs:
        size = part_ref.shape[0]
        part = part_ref[...].astype(jnp.float32)
        if size < rows:
            part = jnp.concatenate(
                [jnp.zeros((rows - size, part.shape[1]), jnp.float32), part], axis=0
            )
        total = total + part
    joined_ref[:, query_cols:] = total.astype(jnp.bfloat16)


def join(query_part, kv_part, returned):
    rows, query_cols = query_part.shape
    kv_cols = kv_part.shape[1]
    whole = pl.BlockSpec(memory_space=pltpu.VMEM)
    return pl.pallas_call(
        join_kernel,
        out_shape=jax.ShapeDtypeStruct((rows, query_cols + kv_cols), jnp.bfloat16),
        in_specs=[whole] * (2 + len(returned)),
        out_specs=whole,
        compiler_params=pltpu.CompilerParams(vmem_limit_bytes=8 * 1024 * 1024),
        cost_estimate=pl.CostEstimate(flops=1, bytes_accessed=1, transcendentals=0),
    )(query_part, kv_part, *returned)


def project_kernel(pieces, tile, core_ref, *refs):
    count = len(pieces)
    flat_refs, (query_weight, key_weight, value_weight) = refs[: sum(pieces)], refs[sum(pieces) :][:3]
    keep_refs, give_refs = refs[-2 * count - 2 : -count - 2], refs[-count - 2 : -2]
    full_ref, block_ref = refs[-2:]
    row, at = 0, 0
    for count in pieces:
        column = 0
        for ref in flat_refs[at : at + count]:
            block_ref[row : row + ref.shape[0], column : column + ref.shape[1]] = ref[...]
            column += ref.shape[1]
        at += count
        row += flat_refs[at - 1].shape[0]
    query_cols, kv_cols = query_weight.shape[1], key_weight.shape[1]

    def step(i, carry):
        at = pl.ds(pl.multiple_of(i * tile, 16), tile)
        full_ref[at, :] = (
            dot(query_weight[at, :], block_ref[:, :query_cols], 1, 1)
            + dot(key_weight[at, :], block_ref[:, query_cols : query_cols + kv_cols], 1, 1)
            + dot(value_weight[at, :], block_ref[:, query_cols + kv_cols :], 1, 1)
        )
        return carry

    lax.fori_loop(0, full_ref.shape[0] // tile, step, 0)
    half, rows = give_refs[0].shape
    own = pl.ds(pl.multiple_of(core_ref[0] * half, 8), half)
    other = pl.ds(pl.multiple_of((1 - core_ref[0]) * half, 8), half)
    for i, (keep_ref, give_ref) in enumerate(zip(keep_refs, give_refs)):
        cols = slice(i * rows, (i + 1) * rows)
        keep_ref[...] = full_ref[own, cols]
        give_ref[...] = full_ref[other, cols].astype(jnp.bfloat16)


def project(blocks, weights, core, final):
    width = weights[0].shape[0]
    rows = sum(block[0].shape[0] for block in blocks)
    half = (width // 2, rows // len(blocks))
    cols = sum(weight.shape[1] for weight in weights)
    tile = max(t for t in range(16, 449, 16) if width % t == 0)
    flat = [piece for block in blocks for piece in block]
    whole = pl.BlockSpec(memory_space=pltpu.VMEM)
    return pl.pallas_call(
        functools.partial(project_kernel, [len(block) for block in blocks], tile),
        out_shape=[jax.ShapeDtypeStruct(half, jnp.float32)] * len(blocks)
        + [jax.ShapeDtypeStruct(half, jnp.bfloat16)] * len(blocks),
        in_specs=[pl.BlockSpec(memory_space=pltpu.SMEM)] + [whole] * (len(flat) + 3),
        out_specs=[whole] * (2 * len(blocks)),
        scratch_shapes=[
            pltpu.VMEM((width, rows), jnp.float32),
            pltpu.VMEM((rows, cols), jnp.bfloat16),
        ],
        compiler_params=pltpu.CompilerParams(vmem_limit_bytes=8 * 1024 * 1024),
        cost_estimate=pl.CostEstimate(
            flops=1 if final else 2 * rows * width * cols,
            bytes_accessed=1 if final else 2 * width * cols + 6 * width * rows,
            transcendentals=0,
        ),
    )(core, *flat, *weights)


def moved(block, axis, by):
    size = lax.axis_size(axis)
    return lax.ppermute(block, axis, [(i, i + by) for i in range(size) if 0 <= i + by < size])


def swapped(block, axis, first):
    pairs = []
    for i in range(first, lax.axis_size(axis) - 1, 2):
        pairs += [(i, i + 1), (i + 1, i)]
    return lax.ppermute(block, axis, pairs)


def after(arrays, *others):
    return lax.optimization_barrier((*arrays, *others))[: len(arrays)]


def passed_along(block, axis, distance):
    devices = range(lax.axis_size(axis))
    return lax.ppermute(block, axis, [((i - distance) % len(devices), i) for i in devices])


def per_device(
    query_rows,
    key_row_matrix,
    value_row_matrix,
    out_grad,
    w_query,
    key_weight,
    value_weight,
    doc_ids,
):
    documents = doc_ids[0]
    tokens = documents.shape[0]
    rows = query_rows.shape[1]
    kv_cols = key_row_matrix.shape[2]
    shards = lax.axis_size("seq")
    place = lax.axis_index("seq")
    back = min(WINDOW, tokens // 3) - 1
    halo_rows = []
    while sum(halo_rows) < back and len(halo_rows) < shards - 1:
        halo_rows.append(min(rows, -(-(back - sum(halo_rows)) // 16) * 16))
    kv = lax.optimization_barrier(
        jnp.concatenate([key_row_matrix[0], value_row_matrix[0]], axis=1)
    )
    halos = [moved(kv[rows - size :], "seq", d) for d, size in enumerate(halo_rows, 1)]
    reach = sum(halo_rows)
    first_row = place * rows
    key_docs = lax.dynamic_slice_in_dim(
        jnp.concatenate([jnp.full((reach,), -1, jnp.int32), documents]), first_row, reach + rows, 0
    )
    query_docs = lax.dynamic_slice_in_dim(documents, first_row, rows, 0)
    offset = (
        jnp.arange(rows, dtype=jnp.int32)[None, :]
        + reach
        - jnp.arange(reach + rows, dtype=jnp.int32)[:, None]
    )
    allowed = (query_docs[None, :] == key_docs[:, None]) & (offset >= 0) & (offset < WINDOW)
    bias = jnp.where(allowed, 0.0, MASKED).astype(jnp.float32)
    kv_heads = kv_cols // HEAD_WIDTH
    query_stack, grad_stack = stack(
        *after((query_rows[0], out_grad[0]), kv), kv_heads, query_rows.shape[2] // kv_cols
    )
    grad_query, grad_kv, *grad_halos = attention_backward(
        query_stack, grad_stack, kv, bias, halos[::-1]
    )
    returned = [moved(part, "seq", -d) for d, part in enumerate(grad_halos[::-1], 1)]
    own = join(grad_query, grad_kv, returned)
    weights = (w_query[0], key_weight[0], value_weight[0])
    core = lax.axis_index("mp").astype(jnp.int32)

    def halves_summed(blocks, late, before=(), final=False):
        halves = project([(block,) for block in blocks], weights, core[None], final)
        sums = []
        for keep, give in zip(halves[: len(blocks)], halves[len(blocks) :]):
            if before:
                (give,) = after((give,), *before)
            got = passed_along(give, "mp", 1)
            if late:
                (got,) = after((got,), *late)
            sums.append((keep + got.astype(jnp.float32)).astype(jnp.bfloat16))
        return sums

    even = place % 2 == 0
    results, waiting = [], [own]
    by_first, by_second = own, own
    for step in range(1, shards):
        came_first = swapped(by_first, "seq", 0)
        last = step == shards - 1 and shards % 2 == 0
        came_second = came_first if last else swapped(by_second, "seq", 1)
        if step > 1:
            waiting = after(waiting, *sums, *(results[-2] if step > 2 else ()))
        late = (came_first, came_second) if step > 1 else ()
        sums = halves_summed(waiting, late)
        results.append([passed_along(block, "section", -1) for block in sums])
        by_first, by_second = came_second, came_first
        if last:
            waiting = [came_first]
        elif 2 * step < shards:
            waiting = [came_first, came_second]
        else:
            waiting = [jnp.where(even == (place >= step), came_second, came_first)]
    if shards > 1:
        waiting = after(waiting, *sums)
    sums = halves_summed(waiting, (), sum(results[-2:], []) if shards > 1 else (), True)
    results.append([passed_along(block, "section", -1) for block in sums])
    for step, blocks in enumerate(results):
        if len(blocks) > 1:
            first, second = blocks
            results[step] = [jnp.where(even, second, first), jnp.where(even, first, second)]
    upstream = jnp.zeros((results[0][0].shape[0], tokens), jnp.bfloat16)
    for s in range(shards):
        behind = results[s][0]
        ahead = results[(shards - s) % shards][-1]
        block = jnp.where(place >= s, behind, ahead)
        upstream = lax.dynamic_update_slice_in_dim(
            upstream, block, ((place - s) % shards) * rows, 1
        )
    return upstream.T[None]


def solution(mesh):
    placed = P("section", "seq", "mp")
    return jax.shard_map(
        per_device,
        mesh=mesh,
        in_specs=(placed,) * 7 + (P("section", None),),
        out_specs=P("section", None, ("seq", "mp")),
        check_vma=False,
    )
```

```python
import functools
import math

import jax
import jax.numpy as jnp
from jax import lax
from jax.experimental import pallas as pl
from jax.experimental.pallas import tpu as pltpu
from jax.sharding import PartitionSpec as P

HEAD_WIDTH = 128
WINDOW = 512
MASKED = -1e30


def dot(left, right, left_dim, right_dim):
    return lax.dot_general(
        left,
        right,
        (((left_dim,), (right_dim,)), ((), ())),
        preferred_element_type=jnp.float32,
    )


def stack_kernel(kv_heads, group_width, query_ref, grad_ref, query_out, grad_out):
    rows = query_ref.shape[0]
    for head in range(kv_heads * group_width):
        cols = slice(head * HEAD_WIDTH, (head + 1) * HEAD_WIDTH)
        query_out[head * rows : (head + 1) * rows, :] = query_ref[:, cols]
        grad_out[head * rows : (head + 1) * rows, :] = grad_ref[:, cols]


def stack(query, grad, kv_heads, group_width):
    rows, query_cols = query.shape
    whole = pl.BlockSpec(memory_space=pltpu.VMEM)
    shape = jax.ShapeDtypeStruct((rows * kv_heads * group_width, HEAD_WIDTH), jnp.bfloat16)
    return pl.pallas_call(
        functools.partial(stack_kernel, kv_heads, group_width),
        out_shape=[shape] * 2,
        in_specs=[whole] * 2,
        out_specs=[whole] * 2,
        compiler_params=pltpu.CompilerParams(vmem_limit_bytes=8 * 1024 * 1024),
        cost_estimate=pl.CostEstimate(flops=1, bytes_accessed=1, transcendentals=0),
    )(query, grad)


def attention_kernel(kv_heads, group_width, halo_rows, *refs):
    halo_count = len(halo_rows)
    query_ref, grad_ref, kv_ref, bias_ref = refs[:4]
    halo_refs = refs[4 : 4 + halo_count]
    grad_query_ref, grad_kv_ref = refs[4 + halo_count : 6 + halo_count]
    grad_halo_refs = refs[6 + halo_count :]
    rows = kv_ref.shape[0]
    kv_cols = kv_heads * HEAD_WIDTH
    scaling = 1.0 / math.sqrt(HEAD_WIDTH)
    bias = jnp.concatenate([bias_ref[...]] * group_width, axis=1)
    for group in range(kv_heads):
        heads = [group * group_width + member for member in range(group_width)]
        stacked = slice(heads[0] * rows, (heads[-1] + 1) * rows)
        query, grad = query_ref[stacked, :], grad_ref[stacked, :]
        key_cols = slice(group * HEAD_WIDTH, (group + 1) * HEAD_WIDTH)
        value_cols = slice(kv_cols + group * HEAD_WIDTH, kv_cols + (group + 1) * HEAD_WIDTH)
        blocks = [*halo_refs, kv_ref]
        key = jnp.concatenate([block[:, key_cols] for block in blocks], axis=0)
        value = jnp.concatenate([block[:, value_cols] for block in blocks], axis=0)
        scores = dot(key, query, 1, 1) * scaling + bias
        raised = jnp.exp(scores - jnp.max(scores, axis=0, keepdims=True))
        weights = raised * (1.0 / jnp.sum(raised, axis=0, keepdims=True))
        weights_half = weights.astype(jnp.bfloat16)
        grad_weights = dot(value, grad, 1, 1)
        delta = jnp.sum(weights_half.astype(jnp.float32) * grad_weights, axis=0, keepdims=True)
        grad_scores = (weights * (grad_weights - delta)).astype(jnp.bfloat16)
        grad_query = (dot(grad_scores, key, 0, 0) * scaling).astype(jnp.bfloat16)
        for member, h in enumerate(heads):
            grad_query_ref[:, h * HEAD_WIDTH : (h + 1) * HEAD_WIDTH] = grad_query[
                member * rows : (member + 1) * rows
            ]
        grad_key = dot(grad_scores, query, 1, 0) * scaling
        grad_value = dot(weights_half, grad, 1, 0)
        start = 0
        for size, out_ref in zip([*halo_rows, rows], [*grad_halo_refs, grad_kv_ref]):
            out_ref[:, key_cols] = grad_key[start : start + size].astype(out_ref.dtype)
            out_ref[:, value_cols] = grad_value[start : start + size].astype(out_ref.dtype)
            start += size


def attention_backward(query, grad, kv, bias, halos):
    rows, kv_cols = kv.shape[0], kv.shape[1] // 2
    kv_heads = kv_cols // HEAD_WIDTH
    group_width = query.shape[0] // (rows * kv_heads)
    query_cols = kv_heads * group_width * HEAD_WIDTH
    halo_rows = [halo.shape[0] for halo in halos]
    span = bias.shape[0]
    whole = pl.BlockSpec(memory_space=pltpu.VMEM)
    outs = [
        jax.ShapeDtypeStruct((rows, query_cols), jnp.bfloat16),
        jax.ShapeDtypeStruct((rows, 2 * kv_cols), jnp.float32),
        *[jax.ShapeDtypeStruct((size, 2 * kv_cols), jnp.bfloat16) for size in halo_rows],
    ]
    return pl.pallas_call(
        functools.partial(attention_kernel, kv_heads, group_width, halo_rows),
        out_shape=outs,
        in_specs=[whole] * (4 + len(halos)),
        out_specs=[whole] * len(outs),
        compiler_params=pltpu.CompilerParams(vmem_limit_bytes=8 * 1024 * 1024),
        cost_estimate=pl.CostEstimate(
            flops=12 * rows * span * query_cols,
            bytes_accessed=4 * rows * query_cols * 2,
            transcendentals=rows * span * kv_heads * group_width,
        ),
    )(query, grad, kv, bias, *halos)


def join_kernel(query_ref, kv_ref, *refs):
    *part_refs, joined_ref = refs
    rows = kv_ref.shape[0]
    query_cols = query_ref.shape[1]
    joined_ref[:, :query_cols] = query_ref[...]
    total = kv_ref[...]
    for part_ref in part_refs:
        size = part_ref.shape[0]
        part = part_ref[...].astype(jnp.float32)
        if size < rows:
            part = jnp.concatenate(
                [jnp.zeros((rows - size, part.shape[1]), jnp.float32), part], axis=0
            )
        total = total + part
    joined_ref[:, query_cols:] = total.astype(jnp.bfloat16)


def join(query_part, kv_part, returned):
    rows, query_cols = query_part.shape
    kv_cols = kv_part.shape[1]
    whole = pl.BlockSpec(memory_space=pltpu.VMEM)
    return pl.pallas_call(
        join_kernel,
        out_shape=jax.ShapeDtypeStruct((rows, query_cols + kv_cols), jnp.bfloat16),
        in_specs=[whole] * (2 + len(returned)),
        out_specs=whole,
        compiler_params=pltpu.CompilerParams(vmem_limit_bytes=8 * 1024 * 1024),
        cost_estimate=pl.CostEstimate(flops=1, bytes_accessed=1, transcendentals=0),
    )(query_part, kv_part, *returned)


def project_kernel(pieces, tile, core_ref, *refs):
    count = len(pieces)
    flat_refs, (query_weight, key_weight, value_weight) = refs[: sum(pieces)], refs[sum(pieces) :][:3]
    keep_refs, give_refs = refs[-2 * count - 2 : -count - 2], refs[-count - 2 : -2]
    full_ref, block_ref = refs[-2:]
    row, at = 0, 0
    for count in pieces:
        column = 0
        for ref in flat_refs[at : at + count]:
            block_ref[row : row + ref.shape[0], column : column + ref.shape[1]] = ref[...]
            column += ref.shape[1]
        at += count
        row += flat_refs[at - 1].shape[0]
    query_cols, kv_cols = query_weight.shape[1], key_weight.shape[1]

    def step(i, carry):
        at = pl.ds(pl.multiple_of(i * tile, 16), tile)
        full_ref[at, :] = (
            dot(query_weight[at, :], block_ref[:, :query_cols], 1, 1)
            + dot(key_weight[at, :], block_ref[:, query_cols : query_cols + kv_cols], 1, 1)
            + dot(value_weight[at, :], block_ref[:, query_cols + kv_cols :], 1, 1)
        )
        return carry

    lax.fori_loop(0, full_ref.shape[0] // tile, step, 0)
    half, rows = give_refs[0].shape
    own = pl.ds(pl.multiple_of(core_ref[0] * half, 8), half)
    other = pl.ds(pl.multiple_of((1 - core_ref[0]) * half, 8), half)
    for i, (keep_ref, give_ref) in enumerate(zip(keep_refs, give_refs)):
        cols = slice(i * rows, (i + 1) * rows)
        keep_ref[...] = full_ref[own, cols]
        give_ref[...] = full_ref[other, cols].astype(jnp.bfloat16)


def project(blocks, weights, core):
    width = weights[0].shape[0]
    rows = sum(block[0].shape[0] for block in blocks)
    half = (width // 2, rows // len(blocks))
    cols = sum(weight.shape[1] for weight in weights)
    tile = max(t for t in range(16, 449, 16) if width % t == 0)
    flat = [piece for block in blocks for piece in block]
    whole = pl.BlockSpec(memory_space=pltpu.VMEM)
    return pl.pallas_call(
        functools.partial(project_kernel, [len(block) for block in blocks], tile),
        out_shape=[jax.ShapeDtypeStruct(half, jnp.float32)] * len(blocks)
        + [jax.ShapeDtypeStruct(half, jnp.bfloat16)] * len(blocks),
        in_specs=[pl.BlockSpec(memory_space=pltpu.SMEM)] + [whole] * (len(flat) + 3),
        out_specs=[whole] * (2 * len(blocks)),
        scratch_shapes=[
            pltpu.VMEM((width, rows), jnp.float32),
            pltpu.VMEM((rows, cols), jnp.bfloat16),
        ],
        compiler_params=pltpu.CompilerParams(vmem_limit_bytes=8 * 1024 * 1024),
        cost_estimate=pl.CostEstimate(
            flops=2 * rows * width * cols,
            bytes_accessed=2 * width * cols + 6 * width * rows,
            transcendentals=0,
        ),
    )(core, *flat, *weights)


def moved(block, axis, by):
    size = lax.axis_size(axis)
    return lax.ppermute(block, axis, [(i, i + by) for i in range(size) if 0 <= i + by < size])


def swapped(block, axis, first):
    pairs = []
    for i in range(first, lax.axis_size(axis) - 1, 2):
        pairs += [(i, i + 1), (i + 1, i)]
    return lax.ppermute(block, axis, pairs)


def after(arrays, *others):
    return lax.optimization_barrier((*arrays, *others))[: len(arrays)]


def passed_along(block, axis, distance):
    devices = range(lax.axis_size(axis))
    return lax.ppermute(block, axis, [((i - distance) % len(devices), i) for i in devices])


def per_device(
    query_rows,
    key_row_matrix,
    value_row_matrix,
    out_grad,
    w_query,
    key_weight,
    value_weight,
    doc_ids,
):
    documents = doc_ids[0]
    tokens = documents.shape[0]
    rows = query_rows.shape[1]
    kv_cols = key_row_matrix.shape[2]
    shards = lax.axis_size("seq")
    place = lax.axis_index("seq")
    back = min(WINDOW, tokens // 3) - 1
    halo_rows = []
    while sum(halo_rows) < back and len(halo_rows) < shards - 1:
        halo_rows.append(min(rows, -(-(back - sum(halo_rows)) // 16) * 16))
    kv = lax.optimization_barrier(
        jnp.concatenate([key_row_matrix[0], value_row_matrix[0]], axis=1)
    )
    halos = [moved(kv[rows - size :], "seq", d) for d, size in enumerate(halo_rows, 1)]
    reach = sum(halo_rows)
    first_row = place * rows
    key_docs = lax.dynamic_slice_in_dim(
        jnp.concatenate([jnp.full((reach,), -1, jnp.int32), documents]), first_row, reach + rows, 0
    )
    query_docs = lax.dynamic_slice_in_dim(documents, first_row, rows, 0)
    offset = (
        jnp.arange(rows, dtype=jnp.int32)[None, :]
        + reach
        - jnp.arange(reach + rows, dtype=jnp.int32)[:, None]
    )
    allowed = (query_docs[None, :] == key_docs[:, None]) & (offset >= 0) & (offset < WINDOW)
    bias = jnp.where(allowed, 0.0, MASKED).astype(jnp.float32)
    kv_heads = kv_cols // HEAD_WIDTH
    query_stack, grad_stack = stack(
        *after((query_rows[0], out_grad[0]), kv), kv_heads, query_rows.shape[2] // kv_cols
    )
    grad_query, grad_kv, *grad_halos = attention_backward(
        query_stack, grad_stack, kv, bias, halos[::-1]
    )
    returned = [moved(part, "seq", -d) for d, part in enumerate(grad_halos[::-1], 1)]
    own = join(grad_query, grad_kv, returned)
    weights = (w_query[0], key_weight[0], value_weight[0])
    core = lax.axis_index("mp").astype(jnp.int32)

    def halves_summed(blocks, late, before=()):
        halves = project([(block,) for block in blocks], weights, core[None])
        sums = []
        for keep, give in zip(halves[: len(blocks)], halves[len(blocks) :]):
            if before:
                (give,) = after((give,), *before)
            got = passed_along(give, "mp", 1)
            if late:
                (got,) = after((got,), *late)
            sums.append((keep + got.astype(jnp.float32)).astype(jnp.bfloat16))
        return sums

    even = place % 2 == 0
    results, waiting, held, hops = [], [own], [], []

    def hop(blocks):
        came = passed_along(jnp.concatenate(blocks, axis=1), "section", -1)
        hops.append(came)
        return [came[:, i * rows : (i + 1) * rows] for i in range(len(blocks))]

    by_first, by_second = own, own
    for step in range(1, shards):
        came_first = swapped(by_first, "seq", 0)
        last = step == shards - 1 and shards % 2 == 0
        came_second = came_first if last else swapped(by_second, "seq", 1)
        if step > 1:
            waiting = after(waiting, *sums, *(hops[-2:-1] if step > 2 else ()))
        late = (came_first, came_second) if step > 1 else ()
        sums = halves_summed(waiting, late)
        if step > 2 and last:
            held = sums
        else:
            results.append(hop(sums))
        by_first, by_second = came_second, came_first
        if last:
            waiting = [came_first]
        elif 2 * step < shards:
            waiting = [came_first, came_second]
        else:
            waiting = [jnp.where(even == (place >= step), came_second, came_first)]
    if shards > 1:
        waiting = after(waiting, *sums)
    sums = halves_summed(waiting, (), hops[-1:])
    came = hop([*held, *sums])
    results += [[block] for block in came] if held else [came]
    for step, blocks in enumerate(results):
        if len(blocks) > 1:
            first, second = blocks
            results[step] = [jnp.where(even, second, first), jnp.where(even, first, second)]
    upstream = jnp.zeros((results[0][0].shape[0], tokens), jnp.bfloat16)
    for s in range(shards):
        behind = results[s][0]
        ahead = results[(shards - s) % shards][-1]
        block = jnp.where(place >= s, behind, ahead)
        upstream = lax.dynamic_update_slice_in_dim(
            upstream, block, ((place - s) % shards) * rows, 1
        )
    return upstream.T[None]


def solution(mesh):
    placed = P("section", "seq", "mp")
    return jax.shard_map(
        per_device,
        mesh=mesh,
        in_specs=(placed,) * 7 + (P("section", None),),
        out_specs=P("section", None, ("seq", "mp")),
        check_vma=False,
    )
```

```python
import functools
import math

import jax
import jax.numpy as jnp
from jax import lax
from jax.experimental import pallas as pl
from jax.experimental.pallas import tpu as pltpu
from jax.sharding import PartitionSpec as P

HEAD_WIDTH = 128
WINDOW = 512
MASKED = -1e30


def dot(left, right, left_dim, right_dim):
    return lax.dot_general(
        left,
        right,
        (((left_dim,), (right_dim,)), ((), ())),
        preferred_element_type=jnp.float32,
    )


def stack_kernel(kv_heads, group_width, query_ref, grad_ref, query_out, grad_out):
    rows = query_ref.shape[0]
    for head in range(kv_heads * group_width):
        cols = slice(head * HEAD_WIDTH, (head + 1) * HEAD_WIDTH)
        query_out[head * rows : (head + 1) * rows, :] = query_ref[:, cols]
        grad_out[head * rows : (head + 1) * rows, :] = grad_ref[:, cols]


def stack(query, grad, kv_heads, group_width):
    rows, query_cols = query.shape
    whole = pl.BlockSpec(memory_space=pltpu.VMEM)
    shape = jax.ShapeDtypeStruct((rows * kv_heads * group_width, HEAD_WIDTH), jnp.bfloat16)
    return pl.pallas_call(
        functools.partial(stack_kernel, kv_heads, group_width),
        out_shape=[shape] * 2,
        in_specs=[whole] * 2,
        out_specs=[whole] * 2,
        compiler_params=pltpu.CompilerParams(vmem_limit_bytes=8 * 1024 * 1024),
        cost_estimate=pl.CostEstimate(flops=1, bytes_accessed=1, transcendentals=0),
    )(query, grad)


def attention_kernel(kv_heads, group_width, halo_rows, *refs):
    halo_count = len(halo_rows)
    query_ref, grad_ref, kv_ref, bias_ref = refs[:4]
    halo_refs = refs[4 : 4 + halo_count]
    grad_query_ref, grad_kv_ref = refs[4 + halo_count : 6 + halo_count]
    grad_halo_refs = refs[6 + halo_count :]
    rows = kv_ref.shape[0]
    kv_cols = kv_heads * HEAD_WIDTH
    scaling = 1.0 / math.sqrt(HEAD_WIDTH)
    bias = jnp.concatenate([bias_ref[...]] * group_width, axis=1)
    for group in range(kv_heads):
        heads = [group * group_width + member for member in range(group_width)]
        stacked = slice(heads[0] * rows, (heads[-1] + 1) * rows)
        query, grad = query_ref[stacked, :], grad_ref[stacked, :]
        key_cols = slice(group * HEAD_WIDTH, (group + 1) * HEAD_WIDTH)
        value_cols = slice(kv_cols + group * HEAD_WIDTH, kv_cols + (group + 1) * HEAD_WIDTH)
        blocks = [*halo_refs, kv_ref]
        key = jnp.concatenate([block[:, key_cols] for block in blocks], axis=0)
        value = jnp.concatenate([block[:, value_cols] for block in blocks], axis=0)
        scores = dot(key, query, 1, 1) * scaling + bias
        raised = jnp.exp(scores - jnp.max(scores, axis=0, keepdims=True))
        weights = raised * (1.0 / jnp.sum(raised, axis=0, keepdims=True))
        weights_half = weights.astype(jnp.bfloat16)
        grad_weights = dot(value, grad, 1, 1)
        delta = jnp.sum(weights_half.astype(jnp.float32) * grad_weights, axis=0, keepdims=True)
        grad_scores = (weights * (grad_weights - delta)).astype(jnp.bfloat16)
        grad_query = (dot(grad_scores, key, 0, 0) * scaling).astype(jnp.bfloat16)
        for member, h in enumerate(heads):
            grad_query_ref[:, h * HEAD_WIDTH : (h + 1) * HEAD_WIDTH] = grad_query[
                member * rows : (member + 1) * rows
            ]
        grad_key = dot(grad_scores, query, 1, 0) * scaling
        grad_value = dot(weights_half, grad, 1, 0)
        start = 0
        for size, out_ref in zip([*halo_rows, rows], [*grad_halo_refs, grad_kv_ref]):
            out_ref[:, key_cols] = grad_key[start : start + size].astype(out_ref.dtype)
            out_ref[:, value_cols] = grad_value[start : start + size].astype(out_ref.dtype)
            start += size


def attention_backward(query, grad, kv, bias, halos):
    rows, kv_cols = kv.shape[0], kv.shape[1] // 2
    kv_heads = kv_cols // HEAD_WIDTH
    group_width = query.shape[0] // (rows * kv_heads)
    query_cols = kv_heads * group_width * HEAD_WIDTH
    halo_rows = [halo.shape[0] for halo in halos]
    span = bias.shape[0]
    whole = pl.BlockSpec(memory_space=pltpu.VMEM)
    outs = [
        jax.ShapeDtypeStruct((rows, query_cols), jnp.bfloat16),
        jax.ShapeDtypeStruct((rows, 2 * kv_cols), jnp.float32),
        *[jax.ShapeDtypeStruct((size, 2 * kv_cols), jnp.bfloat16) for size in halo_rows],
    ]
    return pl.pallas_call(
        functools.partial(attention_kernel, kv_heads, group_width, halo_rows),
        out_shape=outs,
        in_specs=[whole] * (4 + len(halos)),
        out_specs=[whole] * len(outs),
        compiler_params=pltpu.CompilerParams(vmem_limit_bytes=8 * 1024 * 1024),
        cost_estimate=pl.CostEstimate(
            flops=12 * rows * span * query_cols,
            bytes_accessed=4 * rows * query_cols * 2,
            transcendentals=rows * span * kv_heads * group_width,
        ),
    )(query, grad, kv, bias, *halos)


def join_kernel(query_ref, kv_ref, *refs):
    *part_refs, joined_ref = refs
    rows = kv_ref.shape[0]
    query_cols = query_ref.shape[1]
    joined_ref[:, :query_cols] = query_ref[...]
    total = kv_ref[...]
    for part_ref in part_refs:
        size = part_ref.shape[0]
        part = part_ref[...].astype(jnp.float32)
        if size < rows:
            part = jnp.concatenate(
                [jnp.zeros((rows - size, part.shape[1]), jnp.float32), part], axis=0
            )
        total = total + part
    joined_ref[:, query_cols:] = total.astype(jnp.bfloat16)


def join(query_part, kv_part, returned):
    rows, query_cols = query_part.shape
    kv_cols = kv_part.shape[1]
    whole = pl.BlockSpec(memory_space=pltpu.VMEM)
    return pl.pallas_call(
        join_kernel,
        out_shape=jax.ShapeDtypeStruct((rows, query_cols + kv_cols), jnp.bfloat16),
        in_specs=[whole] * (2 + len(returned)),
        out_specs=whole,
        compiler_params=pltpu.CompilerParams(vmem_limit_bytes=8 * 1024 * 1024),
        cost_estimate=pl.CostEstimate(flops=1, bytes_accessed=1, transcendentals=0),
    )(query_part, kv_part, *returned)


def project_kernel(pieces, tile, core_ref, *refs):
    count = len(pieces)
    flat_refs, (query_weight, key_weight, value_weight) = refs[: sum(pieces)], refs[sum(pieces) :][:3]
    keep_refs, give_refs = refs[-2 * count - 2 : -count - 2], refs[-count - 2 : -2]
    full_ref, block_ref = refs[-2:]
    row, at = 0, 0
    for count in pieces:
        column = 0
        for ref in flat_refs[at : at + count]:
            block_ref[row : row + ref.shape[0], column : column + ref.shape[1]] = ref[...]
            column += ref.shape[1]
        at += count
        row += flat_refs[at - 1].shape[0]
    query_cols, kv_cols = query_weight.shape[1], key_weight.shape[1]

    def step(i, carry):
        at = pl.ds(pl.multiple_of(i * tile, 16), tile)
        full_ref[at, :] = (
            dot(query_weight[at, :], block_ref[:, :query_cols], 1, 1)
            + dot(key_weight[at, :], block_ref[:, query_cols : query_cols + kv_cols], 1, 1)
            + dot(value_weight[at, :], block_ref[:, query_cols + kv_cols :], 1, 1)
        )
        return carry

    lax.fori_loop(0, full_ref.shape[0] // tile, step, 0)
    half, rows = give_refs[0].shape
    own = pl.ds(pl.multiple_of(core_ref[0] * half, 8), half)
    other = pl.ds(pl.multiple_of((1 - core_ref[0]) * half, 8), half)
    for i, (keep_ref, give_ref) in enumerate(zip(keep_refs, give_refs)):
        cols = slice(i * rows, (i + 1) * rows)
        keep_ref[...] = full_ref[own, cols]
        give_ref[...] = full_ref[other, cols].astype(jnp.bfloat16)


def project(blocks, weights, core, light):
    width = weights[0].shape[0]
    rows = sum(block[0].shape[0] for block in blocks)
    half = (width // 2, rows // len(blocks))
    cols = sum(weight.shape[1] for weight in weights)
    tile = max(t for t in range(16, 449, 16) if width % t == 0)
    flat = [piece for block in blocks for piece in block]
    whole = pl.BlockSpec(memory_space=pltpu.VMEM)
    return pl.pallas_call(
        functools.partial(project_kernel, [len(block) for block in blocks], tile),
        out_shape=[jax.ShapeDtypeStruct(half, jnp.float32)] * len(blocks)
        + [jax.ShapeDtypeStruct(half, jnp.bfloat16)] * len(blocks),
        in_specs=[pl.BlockSpec(memory_space=pltpu.SMEM)] + [whole] * (len(flat) + 3),
        out_specs=[whole] * (2 * len(blocks)),
        scratch_shapes=[
            pltpu.VMEM((width, rows), jnp.float32),
            pltpu.VMEM((rows, cols), jnp.bfloat16),
        ],
        compiler_params=pltpu.CompilerParams(vmem_limit_bytes=8 * 1024 * 1024),
        cost_estimate=pl.CostEstimate(
            flops=1 if light else 2 * rows * width * cols,
            bytes_accessed=1 if light else 2 * width * cols + 6 * width * rows,
            transcendentals=0,
        ),
    )(core, *flat, *weights)


def moved(block, axis, by):
    size = lax.axis_size(axis)
    return lax.ppermute(block, axis, [(i, i + by) for i in range(size) if 0 <= i + by < size])


def swapped(block, axis, first):
    pairs = []
    for i in range(first, lax.axis_size(axis) - 1, 2):
        pairs += [(i, i + 1), (i + 1, i)]
    return lax.ppermute(block, axis, pairs)


def after(arrays, *others):
    return lax.optimization_barrier((*arrays, *others))[: len(arrays)]


def passed_along(block, axis, distance):
    devices = range(lax.axis_size(axis))
    return lax.ppermute(block, axis, [((i - distance) % len(devices), i) for i in devices])


def per_device(
    query_rows,
    key_row_matrix,
    value_row_matrix,
    out_grad,
    w_query,
    key_weight,
    value_weight,
    doc_ids,
):
    documents = doc_ids[0]
    tokens = documents.shape[0]
    rows = query_rows.shape[1]
    kv_cols = key_row_matrix.shape[2]
    shards = lax.axis_size("seq")
    place = lax.axis_index("seq")
    back = min(WINDOW, tokens // 3) - 1
    halo_rows = []
    while sum(halo_rows) < back and len(halo_rows) < shards - 1:
        halo_rows.append(min(rows, -(-(back - sum(halo_rows)) // 16) * 16))
    kv = lax.optimization_barrier(
        jnp.concatenate([key_row_matrix[0], value_row_matrix[0]], axis=1)
    )
    halos = [moved(kv[rows - size :], "seq", d) for d, size in enumerate(halo_rows, 1)]
    reach = sum(halo_rows)
    first_row = place * rows
    key_docs = lax.dynamic_slice_in_dim(
        jnp.concatenate([jnp.full((reach,), -1, jnp.int32), documents]), first_row, reach + rows, 0
    )
    query_docs = lax.dynamic_slice_in_dim(documents, first_row, rows, 0)
    offset = (
        jnp.arange(rows, dtype=jnp.int32)[None, :]
        + reach
        - jnp.arange(reach + rows, dtype=jnp.int32)[:, None]
    )
    allowed = (query_docs[None, :] == key_docs[:, None]) & (offset >= 0) & (offset < WINDOW)
    bias = jnp.where(allowed, 0.0, MASKED).astype(jnp.float32)
    kv_heads = kv_cols // HEAD_WIDTH
    query_stack, grad_stack = stack(
        *after((query_rows[0], out_grad[0]), kv), kv_heads, query_rows.shape[2] // kv_cols
    )
    grad_query, grad_kv, *grad_halos = attention_backward(
        query_stack, grad_stack, kv, bias, halos[::-1]
    )
    returned = [moved(part, "seq", -d) for d, part in enumerate(grad_halos[::-1], 1)]
    own = join(grad_query, grad_kv, returned)
    weights = (w_query[0], key_weight[0], value_weight[0])
    core = lax.axis_index("mp").astype(jnp.int32)

    def halves_summed(blocks, late, before=(), light=False):
        halves = project([(block,) for block in blocks], weights, core[None], light)
        sums = []
        for keep, give in zip(halves[: len(blocks)], halves[len(blocks) :]):
            if before:
                (give,) = after((give,), *before)
            got = passed_along(give, "mp", 1)
            if late:
                (got,) = after((got,), *late)
            sums.append((keep + got.astype(jnp.float32)).astype(jnp.bfloat16))
        return sums

    even = place % 2 == 0
    results, waiting, hops = [], [own], []

    def hop(blocks):
        came = passed_along(jnp.concatenate(blocks, axis=1), "section", -1)
        hops.append(came)
        return [came[:, i * rows : (i + 1) * rows] for i in range(len(blocks))]

    by_first, by_second = own, own
    for step in range(1, shards):
        came_first = swapped(by_first, "seq", 0)
        last = step == shards - 1 and shards % 2 == 0
        came_second = came_first if last else swapped(by_second, "seq", 1)
        if step > 1:
            waiting = after(waiting, *sums, *(hops[-2:-1] if step > 2 else ()))
        late = (came_first, came_second) if step > 1 and not (step > 2 and last) else ()
        sums = halves_summed(waiting, late, light=step > 2 and last)
        results.append(hop(sums))
        by_first, by_second = came_second, came_first
        if last:
            waiting = [came_first]
        elif 2 * step < shards:
            waiting = [came_first, came_second]
        else:
            waiting = [jnp.where(even == (place >= step), came_second, came_first)]
    sums = halves_summed(waiting, (), hops[-2:])
    results.append(hop(sums))
    for step, blocks in enumerate(results):
        if len(blocks) > 1:
            first, second = blocks
            results[step] = [jnp.where(even, second, first), jnp.where(even, first, second)]
    upstream = jnp.zeros((results[0][0].shape[0], tokens), jnp.bfloat16)
    for s in range(shards):
        behind = results[s][0]
        ahead = results[(shards - s) % shards][-1]
        block = jnp.where(place >= s, behind, ahead)
        upstream = lax.dynamic_update_slice_in_dim(
            upstream, block, ((place - s) % shards) * rows, 1
        )
    return upstream.T[None]


def solution(mesh):
    placed = P("section", "seq", "mp")
    return jax.shard_map(
        per_device,
        mesh=mesh,
        in_specs=(placed,) * 7 + (P("section", None),),
        out_specs=P("section", None, ("seq", "mp")),
        check_vma=False,
    )
```

```python
import functools
import math

import jax
import jax.numpy as jnp
from jax import lax
from jax.experimental import pallas as pl
from jax.experimental.pallas import tpu as pltpu
from jax.sharding import PartitionSpec as P

HEAD_WIDTH = 128
WINDOW = 512
MASKED = -1e30


def dot(left, right, left_dim, right_dim):
    return lax.dot_general(
        left,
        right,
        (((left_dim,), (right_dim,)), ((), ())),
        preferred_element_type=jnp.float32,
    )


def stack_kernel(kv_heads, group_width, query_ref, grad_ref, query_out, grad_out):
    rows = query_ref.shape[0]
    for head in range(kv_heads * group_width):
        cols = slice(head * HEAD_WIDTH, (head + 1) * HEAD_WIDTH)
        query_out[head * rows : (head + 1) * rows, :] = query_ref[:, cols]
        grad_out[head * rows : (head + 1) * rows, :] = grad_ref[:, cols]


def stack(query, grad, kv_heads, group_width):
    rows, query_cols = query.shape
    whole = pl.BlockSpec(memory_space=pltpu.VMEM)
    shape = jax.ShapeDtypeStruct((rows * kv_heads * group_width, HEAD_WIDTH), jnp.bfloat16)
    return pl.pallas_call(
        functools.partial(stack_kernel, kv_heads, group_width),
        out_shape=[shape] * 2,
        in_specs=[whole] * 2,
        out_specs=[whole] * 2,
        compiler_params=pltpu.CompilerParams(vmem_limit_bytes=8 * 1024 * 1024),
        cost_estimate=pl.CostEstimate(flops=1, bytes_accessed=1, transcendentals=0),
    )(query, grad)


def attention_kernel(kv_heads, group_width, halo_rows, *refs):
    halo_count = len(halo_rows)
    query_ref, grad_ref, kv_ref, bias_ref = refs[:4]
    halo_refs = refs[4 : 4 + halo_count]
    grad_query_ref, grad_kv_ref = refs[4 + halo_count : 6 + halo_count]
    grad_halo_refs = refs[6 + halo_count :]
    rows = kv_ref.shape[0]
    kv_cols = kv_heads * HEAD_WIDTH
    scaling = 1.0 / math.sqrt(HEAD_WIDTH)
    bias = jnp.concatenate([bias_ref[...]] * group_width, axis=1)
    for group in range(kv_heads):
        heads = [group * group_width + member for member in range(group_width)]
        stacked = slice(heads[0] * rows, (heads[-1] + 1) * rows)
        query, grad = query_ref[stacked, :], grad_ref[stacked, :]
        key_cols = slice(group * HEAD_WIDTH, (group + 1) * HEAD_WIDTH)
        value_cols = slice(kv_cols + group * HEAD_WIDTH, kv_cols + (group + 1) * HEAD_WIDTH)
        blocks = [*halo_refs, kv_ref]
        key = jnp.concatenate([block[:, key_cols] for block in blocks], axis=0)
        value = jnp.concatenate([block[:, value_cols] for block in blocks], axis=0)
        scores = dot(key, query, 1, 1) * scaling + bias
        raised = jnp.exp(scores - jnp.max(scores, axis=0, keepdims=True))
        weights = raised * (1.0 / jnp.sum(raised, axis=0, keepdims=True))
        weights_half = weights.astype(jnp.bfloat16)
        grad_weights = dot(value, grad, 1, 1)
        delta = jnp.sum(weights_half.astype(jnp.float32) * grad_weights, axis=0, keepdims=True)
        grad_scores = (weights * (grad_weights - delta)).astype(jnp.bfloat16)
        grad_query = (dot(grad_scores, key, 0, 0) * scaling).astype(jnp.bfloat16)
        for member, h in enumerate(heads):
            grad_query_ref[:, h * HEAD_WIDTH : (h + 1) * HEAD_WIDTH] = grad_query[
                member * rows : (member + 1) * rows
            ]
        grad_key = dot(grad_scores, query, 1, 0) * scaling
        grad_value = dot(weights_half, grad, 1, 0)
        start = 0
        for size, out_ref in zip([*halo_rows, rows], [*grad_halo_refs, grad_kv_ref]):
            out_ref[:, key_cols] = grad_key[start : start + size].astype(out_ref.dtype)
            out_ref[:, value_cols] = grad_value[start : start + size].astype(out_ref.dtype)
            start += size


def attention_backward(query, grad, kv, bias, halos):
    rows, kv_cols = kv.shape[0], kv.shape[1] // 2
    kv_heads = kv_cols // HEAD_WIDTH
    group_width = query.shape[0] // (rows * kv_heads)
    query_cols = kv_heads * group_width * HEAD_WIDTH
    halo_rows = [halo.shape[0] for halo in halos]
    span = bias.shape[0]
    whole = pl.BlockSpec(memory_space=pltpu.VMEM)
    outs = [
        jax.ShapeDtypeStruct((rows, query_cols), jnp.bfloat16),
        jax.ShapeDtypeStruct((rows, 2 * kv_cols), jnp.float32),
        *[jax.ShapeDtypeStruct((size, 2 * kv_cols), jnp.bfloat16) for size in halo_rows],
    ]
    return pl.pallas_call(
        functools.partial(attention_kernel, kv_heads, group_width, halo_rows),
        out_shape=outs,
        in_specs=[whole] * (4 + len(halos)),
        out_specs=[whole] * len(outs),
        compiler_params=pltpu.CompilerParams(vmem_limit_bytes=8 * 1024 * 1024),
        cost_estimate=pl.CostEstimate(
            flops=12 * rows * span * query_cols,
            bytes_accessed=4 * rows * query_cols * 2,
            transcendentals=rows * span * kv_heads * group_width,
        ),
    )(query, grad, kv, bias, *halos)


def join_kernel(query_ref, kv_ref, *refs):
    *part_refs, joined_ref = refs
    rows = kv_ref.shape[0]
    query_cols = query_ref.shape[1]
    joined_ref[:, :query_cols] = query_ref[...]
    total = kv_ref[...]
    for part_ref in part_refs:
        size = part_ref.shape[0]
        part = part_ref[...].astype(jnp.float32)
        if size < rows:
            part = jnp.concatenate(
                [jnp.zeros((rows - size, part.shape[1]), jnp.float32), part], axis=0
            )
        total = total + part
    joined_ref[:, query_cols:] = total.astype(jnp.bfloat16)


def join(query_part, kv_part, returned):
    rows, query_cols = query_part.shape
    kv_cols = kv_part.shape[1]
    whole = pl.BlockSpec(memory_space=pltpu.VMEM)
    return pl.pallas_call(
        join_kernel,
        out_shape=jax.ShapeDtypeStruct((rows, query_cols + kv_cols), jnp.bfloat16),
        in_specs=[whole] * (2 + len(returned)),
        out_specs=whole,
        compiler_params=pltpu.CompilerParams(vmem_limit_bytes=8 * 1024 * 1024),
        cost_estimate=pl.CostEstimate(flops=1, bytes_accessed=1, transcendentals=0),
    )(query_part, kv_part, *returned)


def project_kernel(pieces, tile, core_ref, *refs):
    count = len(pieces)
    flat_refs, (query_weight, key_weight, value_weight) = refs[: sum(pieces)], refs[sum(pieces) :][:3]
    keep_refs, give_refs = refs[-2 * count - 2 : -count - 2], refs[-count - 2 : -2]
    full_ref, block_ref = refs[-2:]
    row, at = 0, 0
    for count in pieces:
        column = 0
        for ref in flat_refs[at : at + count]:
            block_ref[row : row + ref.shape[0], column : column + ref.shape[1]] = ref[...]
            column += ref.shape[1]
        at += count
        row += flat_refs[at - 1].shape[0]
    query_cols, kv_cols = query_weight.shape[1], key_weight.shape[1]

    def step(i, carry):
        at = pl.ds(pl.multiple_of(i * tile, 16), tile)
        full_ref[at, :] = (
            dot(query_weight[at, :], block_ref[:, :query_cols], 1, 1)
            + dot(key_weight[at, :], block_ref[:, query_cols : query_cols + kv_cols], 1, 1)
            + dot(value_weight[at, :], block_ref[:, query_cols + kv_cols :], 1, 1)
        )
        return carry

    lax.fori_loop(0, full_ref.shape[0] // tile, step, 0)
    half, rows = give_refs[0].shape
    own = pl.ds(pl.multiple_of(core_ref[0] * half, 8), half)
    other = pl.ds(pl.multiple_of((1 - core_ref[0]) * half, 8), half)
    for i, (keep_ref, give_ref) in enumerate(zip(keep_refs, give_refs)):
        cols = slice(i * rows, (i + 1) * rows)
        keep_ref[...] = full_ref[own, cols]
        give_ref[...] = full_ref[other, cols].astype(jnp.bfloat16)


def project(blocks, weights, core, light):
    width = weights[0].shape[0]
    rows = sum(block[0].shape[0] for block in blocks)
    half = (width // 2, rows // len(blocks))
    cols = sum(weight.shape[1] for weight in weights)
    tile = max(t for t in range(16, 449, 16) if width % t == 0)
    flat = [piece for block in blocks for piece in block]
    whole = pl.BlockSpec(memory_space=pltpu.VMEM)
    return pl.pallas_call(
        functools.partial(project_kernel, [len(block) for block in blocks], tile),
        out_shape=[jax.ShapeDtypeStruct(half, jnp.float32)] * len(blocks)
        + [jax.ShapeDtypeStruct(half, jnp.bfloat16)] * len(blocks),
        in_specs=[pl.BlockSpec(memory_space=pltpu.SMEM)] + [whole] * (len(flat) + 3),
        out_specs=[whole] * (2 * len(blocks)),
        scratch_shapes=[
            pltpu.VMEM((width, rows), jnp.float32),
            pltpu.VMEM((rows, cols), jnp.bfloat16),
        ],
        compiler_params=pltpu.CompilerParams(vmem_limit_bytes=8 * 1024 * 1024),
        cost_estimate=pl.CostEstimate(
            flops=1 if light else 2 * rows * width * cols,
            bytes_accessed=1 if light else 2 * width * cols + 6 * width * rows,
            transcendentals=0,
        ),
    )(core, *flat, *weights)


def moved(block, axis, by):
    size = lax.axis_size(axis)
    return lax.ppermute(block, axis, [(i, i + by) for i in range(size) if 0 <= i + by < size])


def swapped(block, axis, first):
    pairs = []
    for i in range(first, lax.axis_size(axis) - 1, 2):
        pairs += [(i, i + 1), (i + 1, i)]
    return lax.ppermute(block, axis, pairs)


def after(arrays, *others):
    return lax.optimization_barrier((*arrays, *others))[: len(arrays)]


def passed_along(block, axis, distance):
    devices = range(lax.axis_size(axis))
    return lax.ppermute(block, axis, [((i - distance) % len(devices), i) for i in devices])


def per_device(
    query_rows,
    key_row_matrix,
    value_row_matrix,
    out_grad,
    w_query,
    key_weight,
    value_weight,
    doc_ids,
):
    documents = doc_ids[0]
    tokens = documents.shape[0]
    rows = query_rows.shape[1]
    kv_cols = key_row_matrix.shape[2]
    shards = lax.axis_size("seq")
    place = lax.axis_index("seq")
    back = min(WINDOW, tokens // 3) - 1
    halo_rows = []
    while sum(halo_rows) < back and len(halo_rows) < shards - 1:
        halo_rows.append(min(rows, -(-(back - sum(halo_rows)) // 16) * 16))
    kv = lax.optimization_barrier(
        jnp.concatenate([key_row_matrix[0], value_row_matrix[0]], axis=1)
    )
    halos = [moved(kv[rows - size :], "seq", d) for d, size in enumerate(halo_rows, 1)]
    reach = sum(halo_rows)
    first_row = place * rows
    key_docs = lax.dynamic_slice_in_dim(
        jnp.concatenate([jnp.full((reach,), -1, jnp.int32), documents]), first_row, reach + rows, 0
    )
    query_docs = lax.dynamic_slice_in_dim(documents, first_row, rows, 0)
    offset = (
        jnp.arange(rows, dtype=jnp.int32)[None, :]
        + reach
        - jnp.arange(reach + rows, dtype=jnp.int32)[:, None]
    )
    allowed = (query_docs[None, :] == key_docs[:, None]) & (offset >= 0) & (offset < WINDOW)
    bias = jnp.where(allowed, 0.0, MASKED).astype(jnp.float32)
    kv_heads = kv_cols // HEAD_WIDTH
    query_stack, grad_stack = stack(
        *after((query_rows[0], out_grad[0]), kv), kv_heads, query_rows.shape[2] // kv_cols
    )
    grad_query, grad_kv, *grad_halos = attention_backward(
        query_stack, grad_stack, kv, bias, halos[::-1]
    )
    returned = [moved(part, "seq", -d) for d, part in enumerate(grad_halos[::-1], 1)]
    own = join(grad_query, grad_kv, returned)
    weights = (w_query[0], key_weight[0], value_weight[0])
    core = lax.axis_index("mp").astype(jnp.int32)

    def halves_summed(blocks, late, before=(), light=False):
        halves = project([(block,) for block in blocks], weights, core[None], light)
        sums = []
        for keep, give in zip(halves[: len(blocks)], halves[len(blocks) :]):
            if before:
                (give,) = after((give,), *before)
            got = passed_along(give, "mp", 1)
            if late:
                (got,) = after((got,), *late)
            sums.append((keep + got.astype(jnp.float32)).astype(jnp.bfloat16))
        return sums

    even = place % 2 == 0
    results, waiting, hops = [], [own], []

    def hop(blocks):
        hops.append([passed_along(block, "section", -1) for block in blocks])
        return list(hops[-1])

    by_first, by_second = own, own
    for step in range(1, shards):
        came_first = swapped(by_first, "seq", 0)
        last = step == shards - 1 and shards % 2 == 0
        came_second = came_first if last else swapped(by_second, "seq", 1)
        if step > 1:
            waiting = after(waiting, *sums, *(hops[-2] if step > 2 else ()))
        late = (came_first, came_second) if step > 1 else ()
        if step > 2 and last:
            late = hops[-1]
        sums = halves_summed(waiting, late, light=step > 2 and last)
        results.append(hop(sums))
        by_first, by_second = came_second, came_first
        if last:
            waiting = [came_first]
        elif 2 * step < shards:
            waiting = [came_first, came_second]
        else:
            waiting = [jnp.where(even == (place >= step), came_second, came_first)]
    sums = halves_summed(waiting, (), sum(hops[-2:], []))
    results.append(hop(sums))
    for step, blocks in enumerate(results):
        if len(blocks) > 1:
            first, second = blocks
            results[step] = [jnp.where(even, second, first), jnp.where(even, first, second)]
    upstream = jnp.zeros((results[0][0].shape[0], tokens), jnp.bfloat16)
    for s in range(shards):
        behind = results[s][0]
        ahead = results[(shards - s) % shards][-1]
        block = jnp.where(place >= s, behind, ahead)
        upstream = lax.dynamic_update_slice_in_dim(
            upstream, block, ((place - s) % shards) * rows, 1
        )
    return upstream.T[None]


def solution(mesh):
    placed = P("section", "seq", "mp")
    return jax.shard_map(
        per_device,
        mesh=mesh,
        in_specs=(placed,) * 7 + (P("section", None),),
        out_specs=P("section", None, ("seq", "mp")),
        check_vma=False,
    )
```

```python
import functools
import math

import jax
import jax.numpy as jnp
from jax import lax
from jax.experimental import pallas as pl
from jax.experimental.pallas import tpu as pltpu
from jax.sharding import PartitionSpec as P

HEAD_WIDTH = 128
WINDOW = 512
MASKED = -1e30


def dot(left, right, left_dim, right_dim):
    return lax.dot_general(
        left,
        right,
        (((left_dim,), (right_dim,)), ((), ())),
        preferred_element_type=jnp.float32,
    )


def stack_kernel(kv_heads, group_width, query_ref, grad_ref, query_out, grad_out):
    rows = query_ref.shape[0]
    for head in range(kv_heads * group_width):
        cols = slice(head * HEAD_WIDTH, (head + 1) * HEAD_WIDTH)
        query_out[head * rows : (head + 1) * rows, :] = query_ref[:, cols]
        grad_out[head * rows : (head + 1) * rows, :] = grad_ref[:, cols]


def stack(query, grad, kv_heads, group_width):
    rows, query_cols = query.shape
    whole = pl.BlockSpec(memory_space=pltpu.VMEM)
    shape = jax.ShapeDtypeStruct((rows * kv_heads * group_width, HEAD_WIDTH), jnp.bfloat16)
    return pl.pallas_call(
        functools.partial(stack_kernel, kv_heads, group_width),
        out_shape=[shape] * 2,
        in_specs=[whole] * 2,
        out_specs=[whole] * 2,
        compiler_params=pltpu.CompilerParams(vmem_limit_bytes=8 * 1024 * 1024),
        cost_estimate=pl.CostEstimate(flops=1, bytes_accessed=1, transcendentals=0),
    )(query, grad)


def attention_kernel(kv_heads, group_width, halo_rows, *refs):
    halo_count = len(halo_rows)
    query_ref, grad_ref, kv_ref, bias_ref = refs[:4]
    halo_refs = refs[4 : 4 + halo_count]
    grad_query_ref, grad_kv_ref = refs[4 + halo_count : 6 + halo_count]
    grad_halo_refs = refs[6 + halo_count :]
    rows = kv_ref.shape[0]
    kv_cols = kv_heads * HEAD_WIDTH
    scaling = 1.0 / math.sqrt(HEAD_WIDTH)
    bias = jnp.concatenate([bias_ref[...]] * group_width, axis=1)
    for group in range(kv_heads):
        heads = [group * group_width + member for member in range(group_width)]
        stacked = slice(heads[0] * rows, (heads[-1] + 1) * rows)
        query, grad = query_ref[stacked, :], grad_ref[stacked, :]
        key_cols = slice(group * HEAD_WIDTH, (group + 1) * HEAD_WIDTH)
        value_cols = slice(kv_cols + group * HEAD_WIDTH, kv_cols + (group + 1) * HEAD_WIDTH)
        blocks = [*halo_refs, kv_ref]
        key = jnp.concatenate([block[:, key_cols] for block in blocks], axis=0)
        value = jnp.concatenate([block[:, value_cols] for block in blocks], axis=0)
        scores = dot(key, query, 1, 1) * scaling + bias
        raised = jnp.exp(scores - jnp.max(scores, axis=0, keepdims=True))
        weights = raised * (1.0 / jnp.sum(raised, axis=0, keepdims=True))
        weights_half = weights.astype(jnp.bfloat16)
        grad_weights = dot(value, grad, 1, 1)
        delta = jnp.sum(weights_half.astype(jnp.float32) * grad_weights, axis=0, keepdims=True)
        grad_scores = (weights * (grad_weights - delta)).astype(jnp.bfloat16)
        grad_query = (dot(grad_scores, key, 0, 0) * scaling).astype(jnp.bfloat16)
        for member, h in enumerate(heads):
            grad_query_ref[:, h * HEAD_WIDTH : (h + 1) * HEAD_WIDTH] = grad_query[
                member * rows : (member + 1) * rows
            ]
        grad_key = dot(grad_scores, query, 1, 0) * scaling
        grad_value = dot(weights_half, grad, 1, 0)
        start = 0
        for size, out_ref in zip([*halo_rows, rows], [*grad_halo_refs, grad_kv_ref]):
            out_ref[:, key_cols] = grad_key[start : start + size].astype(out_ref.dtype)
            out_ref[:, value_cols] = grad_value[start : start + size].astype(out_ref.dtype)
            start += size


def attention_backward(query, grad, kv, bias, halos):
    rows, kv_cols = kv.shape[0], kv.shape[1] // 2
    kv_heads = kv_cols // HEAD_WIDTH
    group_width = query.shape[0] // (rows * kv_heads)
    query_cols = kv_heads * group_width * HEAD_WIDTH
    halo_rows = [halo.shape[0] for halo in halos]
    span = bias.shape[0]
    whole = pl.BlockSpec(memory_space=pltpu.VMEM)
    outs = [
        jax.ShapeDtypeStruct((rows, query_cols), jnp.bfloat16),
        jax.ShapeDtypeStruct((rows, 2 * kv_cols), jnp.float32),
        *[jax.ShapeDtypeStruct((size, 2 * kv_cols), jnp.bfloat16) for size in halo_rows],
    ]
    return pl.pallas_call(
        functools.partial(attention_kernel, kv_heads, group_width, halo_rows),
        out_shape=outs,
        in_specs=[whole] * (4 + len(halos)),
        out_specs=[whole] * len(outs),
        compiler_params=pltpu.CompilerParams(vmem_limit_bytes=8 * 1024 * 1024),
        cost_estimate=pl.CostEstimate(
            flops=12 * rows * span * query_cols,
            bytes_accessed=4 * rows * query_cols * 2,
            transcendentals=rows * span * kv_heads * group_width,
        ),
    )(query, grad, kv, bias, *halos)


def join_kernel(query_ref, kv_ref, *refs):
    *part_refs, joined_ref = refs
    rows = kv_ref.shape[0]
    query_cols = query_ref.shape[1]
    joined_ref[:, :query_cols] = query_ref[...]
    total = kv_ref[...]
    for part_ref in part_refs:
        size = part_ref.shape[0]
        part = part_ref[...].astype(jnp.float32)
        if size < rows:
            part = jnp.concatenate(
                [jnp.zeros((rows - size, part.shape[1]), jnp.float32), part], axis=0
            )
        total = total + part
    joined_ref[:, query_cols:] = total.astype(jnp.bfloat16)


def join(query_part, kv_part, returned):
    rows, query_cols = query_part.shape
    kv_cols = kv_part.shape[1]
    whole = pl.BlockSpec(memory_space=pltpu.VMEM)
    return pl.pallas_call(
        join_kernel,
        out_shape=jax.ShapeDtypeStruct((rows, query_cols + kv_cols), jnp.bfloat16),
        in_specs=[whole] * (2 + len(returned)),
        out_specs=whole,
        compiler_params=pltpu.CompilerParams(vmem_limit_bytes=8 * 1024 * 1024),
        cost_estimate=pl.CostEstimate(flops=1, bytes_accessed=1, transcendentals=0),
    )(query_part, kv_part, *returned)


def project_kernel(pieces, tile, core_ref, *refs):
    count = len(pieces)
    flat_refs, (query_weight, key_weight, value_weight) = refs[: sum(pieces)], refs[sum(pieces) :][:3]
    keep_refs, give_refs = refs[-2 * count - 2 : -count - 2], refs[-count - 2 : -2]
    full_ref, block_ref = refs[-2:]
    row, at = 0, 0
    for count in pieces:
        column = 0
        for ref in flat_refs[at : at + count]:
            block_ref[row : row + ref.shape[0], column : column + ref.shape[1]] = ref[...]
            column += ref.shape[1]
        at += count
        row += flat_refs[at - 1].shape[0]
    query_cols, kv_cols = query_weight.shape[1], key_weight.shape[1]

    def step(i, carry):
        at = pl.ds(pl.multiple_of(i * tile, 16), tile)
        full_ref[at, :] = (
            dot(query_weight[at, :], block_ref[:, :query_cols], 1, 1)
            + dot(key_weight[at, :], block_ref[:, query_cols : query_cols + kv_cols], 1, 1)
            + dot(value_weight[at, :], block_ref[:, query_cols + kv_cols :], 1, 1)
        )
        return carry

    lax.fori_loop(0, full_ref.shape[0] // tile, step, 0)
    half, rows = give_refs[0].shape
    own = pl.ds(pl.multiple_of(core_ref[0] * half, 8), half)
    other = pl.ds(pl.multiple_of((1 - core_ref[0]) * half, 8), half)
    for i, (keep_ref, give_ref) in enumerate(zip(keep_refs, give_refs)):
        cols = slice(i * rows, (i + 1) * rows)
        keep_ref[...] = full_ref[own, cols].astype(jnp.bfloat16)
        give_ref[...] = full_ref[other, cols].astype(jnp.bfloat16)


def project(blocks, weights, core, light):
    width = weights[0].shape[0]
    rows = sum(block[0].shape[0] for block in blocks)
    half = (width // 2, rows // len(blocks))
    cols = sum(weight.shape[1] for weight in weights)
    tile = max(t for t in range(16, 449, 16) if width % t == 0)
    flat = [piece for block in blocks for piece in block]
    whole = pl.BlockSpec(memory_space=pltpu.VMEM)
    return pl.pallas_call(
        functools.partial(project_kernel, [len(block) for block in blocks], tile),
        out_shape=[jax.ShapeDtypeStruct(half, jnp.bfloat16)] * (2 * len(blocks)),
        in_specs=[pl.BlockSpec(memory_space=pltpu.SMEM)] + [whole] * (len(flat) + 3),
        out_specs=[whole] * (2 * len(blocks)),
        scratch_shapes=[
            pltpu.VMEM((width, rows), jnp.float32),
            pltpu.VMEM((rows, cols), jnp.bfloat16),
        ],
        compiler_params=pltpu.CompilerParams(vmem_limit_bytes=8 * 1024 * 1024),
        cost_estimate=pl.CostEstimate(
            flops=1 if light else 2 * rows * width * cols,
            bytes_accessed=1 if light else 2 * width * cols + 6 * width * rows,
            transcendentals=0,
        ),
    )(core, *flat, *weights)


def moved(block, axis, by):
    size = lax.axis_size(axis)
    return lax.ppermute(block, axis, [(i, i + by) for i in range(size) if 0 <= i + by < size])


def swapped(block, axis, first):
    pairs = []
    for i in range(first, lax.axis_size(axis) - 1, 2):
        pairs += [(i, i + 1), (i + 1, i)]
    return lax.ppermute(block, axis, pairs)


def after(arrays, *others):
    return lax.optimization_barrier((*arrays, *others))[: len(arrays)]


def passed_along(block, axis, distance):
    devices = range(lax.axis_size(axis))
    return lax.ppermute(block, axis, [((i - distance) % len(devices), i) for i in devices])


def per_device(
    query_rows,
    key_row_matrix,
    value_row_matrix,
    out_grad,
    w_query,
    key_weight,
    value_weight,
    doc_ids,
):
    documents = doc_ids[0]
    tokens = documents.shape[0]
    rows = query_rows.shape[1]
    kv_cols = key_row_matrix.shape[2]
    shards = lax.axis_size("seq")
    place = lax.axis_index("seq")
    back = min(WINDOW, tokens // 3) - 1
    halo_rows = []
    while sum(halo_rows) < back and len(halo_rows) < shards - 1:
        halo_rows.append(min(rows, -(-(back - sum(halo_rows)) // 16) * 16))
    kv = lax.optimization_barrier(
        jnp.concatenate([key_row_matrix[0], value_row_matrix[0]], axis=1)
    )
    halos = [moved(kv[rows - size :], "seq", d) for d, size in enumerate(halo_rows, 1)]
    reach = sum(halo_rows)
    first_row = place * rows
    key_docs = lax.dynamic_slice_in_dim(
        jnp.concatenate([jnp.full((reach,), -1, jnp.int32), documents]), first_row, reach + rows, 0
    )
    query_docs = lax.dynamic_slice_in_dim(documents, first_row, rows, 0)
    offset = (
        jnp.arange(rows, dtype=jnp.int32)[None, :]
        + reach
        - jnp.arange(reach + rows, dtype=jnp.int32)[:, None]
    )
    allowed = (query_docs[None, :] == key_docs[:, None]) & (offset >= 0) & (offset < WINDOW)
    bias = jnp.where(allowed, 0.0, MASKED).astype(jnp.float32)
    kv_heads = kv_cols // HEAD_WIDTH
    query_stack, grad_stack = stack(
        *after((query_rows[0], out_grad[0]), kv), kv_heads, query_rows.shape[2] // kv_cols
    )
    grad_query, grad_kv, *grad_halos = attention_backward(
        query_stack, grad_stack, kv, bias, halos[::-1]
    )
    returned = [moved(part, "seq", -d) for d, part in enumerate(grad_halos[::-1], 1)]
    own = join(grad_query, grad_kv, returned)
    weights = (w_query[0], key_weight[0], value_weight[0])
    core = lax.axis_index("mp").astype(jnp.int32)

    def halves_summed(blocks, late, before=(), light=False):
        halves = project([(block,) for block in blocks], weights, core[None], light)
        sums = []
        for keep, give in zip(halves[: len(blocks)], halves[len(blocks) :]):
            if before:
                (give,) = after((give,), *before)
            got = passed_along(give, "mp", 1)
            if late:
                (got,) = after((got,), *late)
            sums.append((keep.astype(jnp.float32) + got.astype(jnp.float32)).astype(jnp.bfloat16))
        return sums

    even = place % 2 == 0
    results, waiting, hops = [], [own], []

    def hop(blocks):
        hops.append([passed_along(block, "section", -1) for block in blocks])
        return list(hops[-1])

    by_first, by_second = own, own
    for step in range(1, shards):
        came_first = swapped(by_first, "seq", 0)
        last = step == shards - 1 and shards % 2 == 0
        came_second = came_first if last else swapped(by_second, "seq", 1)
        if step > 1:
            waiting = after(waiting, *sums, *(hops[-2] if step > 2 else ()))
        late = (came_first, came_second) if step > 1 else ()
        if step > 2 and last:
            late = hops[-1]
        sums = halves_summed(waiting, late, light=step > 2 and last)
        results.append(hop(sums))
        by_first, by_second = came_second, came_first
        if last:
            waiting = [came_first]
        elif 2 * step < shards:
            waiting = [came_first, came_second]
        else:
            waiting = [jnp.where(even == (place >= step), came_second, came_first)]
    sums = halves_summed(waiting, (), sum(hops[-2:], []))
    results.append(hop(sums))
    for step, blocks in enumerate(results):
        if len(blocks) > 1:
            first, second = blocks
            results[step] = [jnp.where(even, second, first), jnp.where(even, first, second)]
    upstream = jnp.zeros((results[0][0].shape[0], tokens), jnp.bfloat16)
    for s in range(shards):
        behind = results[s][0]
        ahead = results[(shards - s) % shards][-1]
        block = jnp.where(place >= s, behind, ahead)
        upstream = lax.dynamic_update_slice_in_dim(
            upstream, block, ((place - s) % shards) * rows, 1
        )
    return upstream.T[None]


def solution(mesh):
    placed = P("section", "seq", "mp")
    return jax.shard_map(
        per_device,
        mesh=mesh,
        in_specs=(placed,) * 7 + (P("section", None),),
        out_specs=P("section", None, ("seq", "mp")),
        check_vma=False,
    )
```

```python
import functools
import math

import jax
import jax.numpy as jnp
from jax import lax
from jax.experimental import pallas as pl
from jax.experimental.pallas import tpu as pltpu
from jax.sharding import PartitionSpec as P

HEAD_WIDTH = 128
WINDOW = 512
MASKED = -1e30


def dot(left, right, left_dim, right_dim):
    return lax.dot_general(
        left,
        right,
        (((left_dim,), (right_dim,)), ((), ())),
        preferred_element_type=jnp.float32,
    )


def stack_kernel(kv_heads, group_width, query_ref, grad_ref, query_out, grad_out):
    rows = query_ref.shape[0]
    for head in range(kv_heads * group_width):
        cols = slice(head * HEAD_WIDTH, (head + 1) * HEAD_WIDTH)
        query_out[head * rows : (head + 1) * rows, :] = query_ref[:, cols]
        grad_out[head * rows : (head + 1) * rows, :] = grad_ref[:, cols]


def stack(query, grad, kv_heads, group_width):
    rows, query_cols = query.shape
    whole = pl.BlockSpec(memory_space=pltpu.VMEM)
    shape = jax.ShapeDtypeStruct((rows * kv_heads * group_width, HEAD_WIDTH), jnp.bfloat16)
    return pl.pallas_call(
        functools.partial(stack_kernel, kv_heads, group_width),
        out_shape=[shape] * 2,
        in_specs=[whole] * 2,
        out_specs=[whole] * 2,
        compiler_params=pltpu.CompilerParams(vmem_limit_bytes=8 * 1024 * 1024),
        cost_estimate=pl.CostEstimate(flops=1, bytes_accessed=1, transcendentals=0),
    )(query, grad)


def attention_kernel(kv_heads, group_width, halo_rows, *refs):
    halo_count = len(halo_rows)
    query_ref, grad_ref, kv_ref, bias_ref = refs[:4]
    halo_refs = refs[4 : 4 + halo_count]
    grad_query_ref, grad_kv_ref = refs[4 + halo_count : 6 + halo_count]
    grad_halo_refs = refs[6 + halo_count :]
    rows = kv_ref.shape[0]
    kv_cols = kv_heads * HEAD_WIDTH
    scaling = 1.0 / math.sqrt(HEAD_WIDTH)
    bias = jnp.concatenate([bias_ref[...]] * group_width, axis=1)
    for group in range(kv_heads):
        heads = [group * group_width + member for member in range(group_width)]
        stacked = slice(heads[0] * rows, (heads[-1] + 1) * rows)
        query, grad = query_ref[stacked, :], grad_ref[stacked, :]
        key_cols = slice(group * HEAD_WIDTH, (group + 1) * HEAD_WIDTH)
        value_cols = slice(kv_cols + group * HEAD_WIDTH, kv_cols + (group + 1) * HEAD_WIDTH)
        blocks = [*halo_refs, kv_ref]
        key = jnp.concatenate([block[:, key_cols] for block in blocks], axis=0)
        value = jnp.concatenate([block[:, value_cols] for block in blocks], axis=0)
        scores = dot(key, query, 1, 1) * scaling + bias
        raised = jnp.exp(scores - jnp.max(scores, axis=0, keepdims=True))
        weights = raised * (1.0 / jnp.sum(raised, axis=0, keepdims=True))
        weights_half = weights.astype(jnp.bfloat16)
        grad_weights = dot(value, grad, 1, 1)
        delta = jnp.sum(weights_half.astype(jnp.float32) * grad_weights, axis=0, keepdims=True)
        grad_scores = (weights * (grad_weights - delta)).astype(jnp.bfloat16)
        grad_query = (dot(grad_scores, key, 0, 0) * scaling).astype(jnp.bfloat16)
        for member, h in enumerate(heads):
            grad_query_ref[:, h * HEAD_WIDTH : (h + 1) * HEAD_WIDTH] = grad_query[
                member * rows : (member + 1) * rows
            ]
        grad_key = dot(grad_scores, query, 1, 0) * scaling
        grad_value = dot(weights_half, grad, 1, 0)
        start = 0
        for size, out_ref in zip([*halo_rows, rows], [*grad_halo_refs, grad_kv_ref]):
            out_ref[:, key_cols] = grad_key[start : start + size].astype(out_ref.dtype)
            out_ref[:, value_cols] = grad_value[start : start + size].astype(out_ref.dtype)
            start += size


def attention_backward(query, grad, kv, bias, halos):
    rows, kv_cols = kv.shape[0], kv.shape[1] // 2
    kv_heads = kv_cols // HEAD_WIDTH
    group_width = query.shape[0] // (rows * kv_heads)
    query_cols = kv_heads * group_width * HEAD_WIDTH
    halo_rows = [halo.shape[0] for halo in halos]
    span = bias.shape[0]
    whole = pl.BlockSpec(memory_space=pltpu.VMEM)
    outs = [
        jax.ShapeDtypeStruct((rows, query_cols), jnp.bfloat16),
        jax.ShapeDtypeStruct((rows, 2 * kv_cols), jnp.float32),
        *[jax.ShapeDtypeStruct((size, 2 * kv_cols), jnp.bfloat16) for size in halo_rows],
    ]
    return pl.pallas_call(
        functools.partial(attention_kernel, kv_heads, group_width, halo_rows),
        out_shape=outs,
        in_specs=[whole] * (4 + len(halos)),
        out_specs=[whole] * len(outs),
        compiler_params=pltpu.CompilerParams(vmem_limit_bytes=8 * 1024 * 1024),
        cost_estimate=pl.CostEstimate(
            flops=12 * rows * span * query_cols,
            bytes_accessed=4 * rows * query_cols * 2,
            transcendentals=rows * span * kv_heads * group_width,
        ),
    )(query, grad, kv, bias, *halos)


def join_kernel(query_ref, kv_ref, *refs):
    *part_refs, joined_ref = refs
    rows = kv_ref.shape[0]
    query_cols = query_ref.shape[1]
    joined_ref[:, :query_cols] = query_ref[...]
    total = kv_ref[...]
    for part_ref in part_refs:
        size = part_ref.shape[0]
        part = part_ref[...].astype(jnp.float32)
        if size < rows:
            part = jnp.concatenate(
                [jnp.zeros((rows - size, part.shape[1]), jnp.float32), part], axis=0
            )
        total = total + part
    joined_ref[:, query_cols:] = total.astype(jnp.bfloat16)


def join(query_part, kv_part, returned):
    rows, query_cols = query_part.shape
    kv_cols = kv_part.shape[1]
    whole = pl.BlockSpec(memory_space=pltpu.VMEM)
    return pl.pallas_call(
        join_kernel,
        out_shape=jax.ShapeDtypeStruct((rows, query_cols + kv_cols), jnp.bfloat16),
        in_specs=[whole] * (2 + len(returned)),
        out_specs=whole,
        compiler_params=pltpu.CompilerParams(vmem_limit_bytes=8 * 1024 * 1024),
        cost_estimate=pl.CostEstimate(flops=1, bytes_accessed=1, transcendentals=0),
    )(query_part, kv_part, *returned)


def project_kernel(pieces, tile, core_ref, *refs):
    count = len(pieces)
    flat_refs, (query_weight, key_weight, value_weight) = refs[: sum(pieces)], refs[sum(pieces) :][:3]
    keep_refs, give_refs = refs[-2 * count - 2 : -count - 2], refs[-count - 2 : -2]
    full_ref, block_ref = refs[-2:]
    row, at = 0, 0
    for count in pieces:
        column = 0
        for ref in flat_refs[at : at + count]:
            block_ref[row : row + ref.shape[0], column : column + ref.shape[1]] = ref[...]
            column += ref.shape[1]
        at += count
        row += flat_refs[at - 1].shape[0]
    query_cols, kv_cols = query_weight.shape[1], key_weight.shape[1]

    def step(i, carry):
        at = pl.ds(pl.multiple_of(i * tile, 16), tile)
        full_ref[at, :] = (
            dot(query_weight[at, :], block_ref[:, :query_cols], 1, 1)
            + dot(key_weight[at, :], block_ref[:, query_cols : query_cols + kv_cols], 1, 1)
            + dot(value_weight[at, :], block_ref[:, query_cols + kv_cols :], 1, 1)
        )
        return carry

    lax.fori_loop(0, full_ref.shape[0] // tile, step, 0)
    half, rows = give_refs[0].shape
    own = pl.ds(pl.multiple_of(core_ref[0] * half, 8), half)
    other = pl.ds(pl.multiple_of((1 - core_ref[0]) * half, 8), half)
    for i, (keep_ref, give_ref) in enumerate(zip(keep_refs, give_refs)):
        cols = slice(i * rows, (i + 1) * rows)
        keep_ref[...] = full_ref[own, cols].astype(jnp.bfloat16)
        give_ref[...] = full_ref[other, cols].astype(jnp.bfloat16)


def project(blocks, weights, core, light):
    width = weights[0].shape[0]
    rows = sum(block[0].shape[0] for block in blocks)
    half = (width // 2, rows // len(blocks))
    cols = sum(weight.shape[1] for weight in weights)
    tile = max(t for t in range(16, 449, 16) if width % t == 0)
    flat = [piece for block in blocks for piece in block]
    whole = pl.BlockSpec(memory_space=pltpu.VMEM)
    return pl.pallas_call(
        functools.partial(project_kernel, [len(block) for block in blocks], tile),
        out_shape=[jax.ShapeDtypeStruct(half, jnp.bfloat16)] * (2 * len(blocks)),
        in_specs=[pl.BlockSpec(memory_space=pltpu.SMEM)] + [whole] * (len(flat) + 3),
        out_specs=[whole] * (2 * len(blocks)),
        scratch_shapes=[
            pltpu.VMEM((width, rows), jnp.float32),
            pltpu.VMEM((rows, cols), jnp.bfloat16),
        ],
        compiler_params=pltpu.CompilerParams(vmem_limit_bytes=8 * 1024 * 1024),
        cost_estimate=pl.CostEstimate(
            flops=1 if light else 2 * rows * width * cols,
            bytes_accessed=1 if light else 2 * width * cols + 6 * width * rows,
            transcendentals=0,
        ),
    )(core, *flat, *weights)


def moved(block, axis, by):
    size = lax.axis_size(axis)
    return lax.ppermute(block, axis, [(i, i + by) for i in range(size) if 0 <= i + by < size])


def swapped(block, axis, first):
    pairs = []
    for i in range(first, lax.axis_size(axis) - 1, 2):
        pairs += [(i, i + 1), (i + 1, i)]
    return lax.ppermute(block, axis, pairs)


def after(arrays, *others):
    return lax.optimization_barrier((*arrays, *others))[: len(arrays)]


def passed_along(block, axis, distance):
    devices = range(lax.axis_size(axis))
    return lax.ppermute(block, axis, [((i - distance) % len(devices), i) for i in devices])


def per_device(
    query_rows,
    key_row_matrix,
    value_row_matrix,
    out_grad,
    w_query,
    key_weight,
    value_weight,
    doc_ids,
):
    documents = doc_ids[0]
    tokens = documents.shape[0]
    rows = query_rows.shape[1]
    kv_cols = key_row_matrix.shape[2]
    shards = lax.axis_size("seq")
    place = lax.axis_index("seq")
    back = min(WINDOW, tokens // 3) - 1
    halo_rows = []
    while sum(halo_rows) < back and len(halo_rows) < shards - 1:
        halo_rows.append(min(rows, -(-(back - sum(halo_rows)) // 16) * 16))
    kv = lax.optimization_barrier(
        jnp.concatenate([key_row_matrix[0], value_row_matrix[0]], axis=1)
    )
    halos = [moved(kv[rows - size :], "seq", d) for d, size in enumerate(halo_rows, 1)]
    reach = sum(halo_rows)
    first_row = place * rows
    key_docs = lax.dynamic_slice_in_dim(
        jnp.concatenate([jnp.full((reach,), -1, jnp.int32), documents]), first_row, reach + rows, 0
    )
    query_docs = lax.dynamic_slice_in_dim(documents, first_row, rows, 0)
    offset = (
        jnp.arange(rows, dtype=jnp.int32)[None, :]
        + reach
        - jnp.arange(reach + rows, dtype=jnp.int32)[:, None]
    )
    allowed = (query_docs[None, :] == key_docs[:, None]) & (offset >= 0) & (offset < WINDOW)
    bias = jnp.where(allowed, 0.0, MASKED).astype(jnp.float32)
    kv_heads = kv_cols // HEAD_WIDTH
    query_stack, grad_stack = stack(
        *after((query_rows[0], out_grad[0]), kv), kv_heads, query_rows.shape[2] // kv_cols
    )
    grad_query, grad_kv, *grad_halos = attention_backward(
        query_stack, grad_stack, kv, bias, halos[::-1]
    )
    returned = [moved(part, "seq", -d) for d, part in enumerate(grad_halos[::-1], 1)]
    own = join(grad_query, grad_kv, returned)
    weights = (w_query[0], key_weight[0], value_weight[0])
    core = lax.axis_index("mp").astype(jnp.int32)

    def halves_summed(blocks, late, before=(), light=False):
        halves = project([(block,) for block in blocks], weights, core[None], light)
        sums = []
        for keep, give in zip(halves[: len(blocks)], halves[len(blocks) :]):
            if before:
                (give,) = after((give,), *before)
            got = passed_along(give, "mp", 1)
            if late:
                (got,) = after((got,), *late)
            sums.append((keep.astype(jnp.float32) + got.astype(jnp.float32)).astype(jnp.bfloat16))
        return sums

    even = place % 2 == 0
    results, waiting, hops = [], [own], []

    def hop(blocks):
        hops.append([passed_along(block, "section", -1) for block in blocks])
        return list(hops[-1])

    by_first, by_second = own, own
    for step in range(1, shards):
        came_first = swapped(by_first, "seq", 0)
        last = step == shards - 1 and shards % 2 == 0
        came_second = came_first if last else swapped(by_second, "seq", 1)
        if step > 1:
            waiting = after(waiting, *sums, *(hops[-2] if step > 2 else ()))
        late = (came_first, came_second) if step > 1 else ()
        if step > 2 and last:
            late = hops[-1][:1]
        sums = halves_summed(waiting, late, light=step > 2 and last)
        results.append(hop(sums))
        by_first, by_second = came_second, came_first
        if last:
            waiting = [came_first]
        elif 2 * step < shards:
            waiting = [came_first, came_second]
        else:
            waiting = [jnp.where(even == (place >= step), came_second, came_first)]
    sums = halves_summed(waiting, (), sum(hops[-2:], []))
    results.append(hop(sums))
    for step, blocks in enumerate(results):
        if len(blocks) > 1:
            first, second = blocks
            results[step] = [jnp.where(even, second, first), jnp.where(even, first, second)]
    upstream = jnp.zeros((results[0][0].shape[0], tokens), jnp.bfloat16)
    for s in range(shards):
        behind = results[s][0]
        ahead = results[(shards - s) % shards][-1]
        block = jnp.where(place >= s, behind, ahead)
        upstream = lax.dynamic_update_slice_in_dim(
            upstream, block, ((place - s) % shards) * rows, 1
        )
    return upstream.T[None]


def solution(mesh):
    placed = P("section", "seq", "mp")
    return jax.shard_map(
        per_device,
        mesh=mesh,
        in_specs=(placed,) * 7 + (P("section", None),),
        out_specs=P("section", None, ("seq", "mp")),
        check_vma=False,
    )
```

```python
import functools
import math

import jax
import jax.numpy as jnp
from jax import lax
from jax.experimental import pallas as pl
from jax.experimental.pallas import tpu as pltpu
from jax.sharding import PartitionSpec as P

HEAD_WIDTH = 128
WINDOW = 512
MASKED = -1e30


def dot(left, right, left_dim, right_dim):
    return lax.dot_general(
        left,
        right,
        (((left_dim,), (right_dim,)), ((), ())),
        preferred_element_type=jnp.float32,
    )


def stack_kernel(kv_heads, group_width, query_ref, grad_ref, query_out, grad_out):
    rows = query_ref.shape[0]
    for head in range(kv_heads * group_width):
        cols = slice(head * HEAD_WIDTH, (head + 1) * HEAD_WIDTH)
        query_out[head * rows : (head + 1) * rows, :] = query_ref[:, cols]
        grad_out[head * rows : (head + 1) * rows, :] = grad_ref[:, cols]


def stack(query, grad, kv_heads, group_width):
    rows, query_cols = query.shape
    whole = pl.BlockSpec(memory_space=pltpu.VMEM)
    shape = jax.ShapeDtypeStruct((rows * kv_heads * group_width, HEAD_WIDTH), jnp.bfloat16)
    return pl.pallas_call(
        functools.partial(stack_kernel, kv_heads, group_width),
        out_shape=[shape] * 2,
        in_specs=[whole] * 2,
        out_specs=[whole] * 2,
        compiler_params=pltpu.CompilerParams(vmem_limit_bytes=8 * 1024 * 1024),
        cost_estimate=pl.CostEstimate(flops=1, bytes_accessed=1, transcendentals=0),
    )(query, grad)


def attention_kernel(kv_heads, group_width, halo_rows, *refs):
    halo_count = len(halo_rows)
    query_ref, grad_ref, kv_ref, bias_ref = refs[:4]
    halo_refs = refs[4 : 4 + halo_count]
    grad_query_ref, grad_kv_ref = refs[4 + halo_count : 6 + halo_count]
    grad_halo_refs = refs[6 + halo_count :]
    rows = kv_ref.shape[0]
    kv_cols = kv_heads * HEAD_WIDTH
    scaling = 1.0 / math.sqrt(HEAD_WIDTH)
    bias = jnp.concatenate([bias_ref[...]] * group_width, axis=1)
    for group in range(kv_heads):
        heads = [group * group_width + member for member in range(group_width)]
        stacked = slice(heads[0] * rows, (heads[-1] + 1) * rows)
        query, grad = query_ref[stacked, :], grad_ref[stacked, :]
        key_cols = slice(group * HEAD_WIDTH, (group + 1) * HEAD_WIDTH)
        value_cols = slice(kv_cols + group * HEAD_WIDTH, kv_cols + (group + 1) * HEAD_WIDTH)
        blocks = [*halo_refs, kv_ref]
        key = jnp.concatenate([block[:, key_cols] for block in blocks], axis=0)
        value = jnp.concatenate([block[:, value_cols] for block in blocks], axis=0)
        scores = dot(key, query, 1, 1) * scaling + bias
        raised = jnp.exp(scores - jnp.max(scores, axis=0, keepdims=True))
        weights = raised * (1.0 / jnp.sum(raised, axis=0, keepdims=True))
        weights_half = weights.astype(jnp.bfloat16)
        grad_weights = dot(value, grad, 1, 1)
        delta = jnp.sum(weights_half.astype(jnp.float32) * grad_weights, axis=0, keepdims=True)
        grad_scores = (weights * (grad_weights - delta)).astype(jnp.bfloat16)
        grad_query = (dot(grad_scores, key, 0, 0) * scaling).astype(jnp.bfloat16)
        for member, h in enumerate(heads):
            grad_query_ref[:, h * HEAD_WIDTH : (h + 1) * HEAD_WIDTH] = grad_query[
                member * rows : (member + 1) * rows
            ]
        grad_key = dot(grad_scores, query, 1, 0) * scaling
        grad_value = dot(weights_half, grad, 1, 0)
        start = 0
        for size, out_ref in zip([*halo_rows, rows], [*grad_halo_refs, grad_kv_ref]):
            out_ref[:, key_cols] = grad_key[start : start + size].astype(out_ref.dtype)
            out_ref[:, value_cols] = grad_value[start : start + size].astype(out_ref.dtype)
            start += size


def attention_backward(query, grad, kv, bias, halos):
    rows, kv_cols = kv.shape[0], kv.shape[1] // 2
    kv_heads = kv_cols // HEAD_WIDTH
    group_width = query.shape[0] // (rows * kv_heads)
    query_cols = kv_heads * group_width * HEAD_WIDTH
    halo_rows = [halo.shape[0] for halo in halos]
    span = bias.shape[0]
    whole = pl.BlockSpec(memory_space=pltpu.VMEM)
    outs = [
        jax.ShapeDtypeStruct((rows, query_cols), jnp.bfloat16),
        jax.ShapeDtypeStruct((rows, 2 * kv_cols), jnp.float32),
        *[jax.ShapeDtypeStruct((size, 2 * kv_cols), jnp.bfloat16) for size in halo_rows],
    ]
    return pl.pallas_call(
        functools.partial(attention_kernel, kv_heads, group_width, halo_rows),
        out_shape=outs,
        in_specs=[whole] * (4 + len(halos)),
        out_specs=[whole] * len(outs),
        compiler_params=pltpu.CompilerParams(vmem_limit_bytes=8 * 1024 * 1024),
        cost_estimate=pl.CostEstimate(
            flops=12 * rows * span * query_cols,
            bytes_accessed=4 * rows * query_cols * 2,
            transcendentals=rows * span * kv_heads * group_width,
        ),
    )(query, grad, kv, bias, *halos)


def join_kernel(query_ref, kv_ref, *refs):
    *part_refs, joined_ref = refs
    rows = kv_ref.shape[0]
    query_cols = query_ref.shape[1]
    joined_ref[:, :query_cols] = query_ref[...]
    total = kv_ref[...]
    for part_ref in part_refs:
        size = part_ref.shape[0]
        part = part_ref[...].astype(jnp.float32)
        if size < rows:
            part = jnp.concatenate(
                [jnp.zeros((rows - size, part.shape[1]), jnp.float32), part], axis=0
            )
        total = total + part
    joined_ref[:, query_cols:] = total.astype(jnp.bfloat16)


def join(query_part, kv_part, returned):
    rows, query_cols = query_part.shape
    kv_cols = kv_part.shape[1]
    whole = pl.BlockSpec(memory_space=pltpu.VMEM)
    return pl.pallas_call(
        join_kernel,
        out_shape=jax.ShapeDtypeStruct((rows, query_cols + kv_cols), jnp.bfloat16),
        in_specs=[whole] * (2 + len(returned)),
        out_specs=whole,
        compiler_params=pltpu.CompilerParams(vmem_limit_bytes=8 * 1024 * 1024),
        cost_estimate=pl.CostEstimate(flops=1, bytes_accessed=1, transcendentals=0),
    )(query_part, kv_part, *returned)


def project_kernel(pieces, tile, core_ref, *refs):
    count = len(pieces)
    flat_refs, (query_weight, key_weight, value_weight) = refs[: sum(pieces)], refs[sum(pieces) :][:3]
    keep_refs, give_refs = refs[-2 * count - 2 : -count - 2], refs[-count - 2 : -2]
    full_ref, block_ref = refs[-2:]
    row, at = 0, 0
    for count in pieces:
        column = 0
        for ref in flat_refs[at : at + count]:
            block_ref[row : row + ref.shape[0], column : column + ref.shape[1]] = ref[...]
            column += ref.shape[1]
        at += count
        row += flat_refs[at - 1].shape[0]
    query_cols, kv_cols = query_weight.shape[1], key_weight.shape[1]

    def step(i, carry):
        at = pl.ds(pl.multiple_of(i * tile, 16), tile)
        full_ref[at, :] = (
            dot(query_weight[at, :], block_ref[:, :query_cols], 1, 1)
            + dot(key_weight[at, :], block_ref[:, query_cols : query_cols + kv_cols], 1, 1)
            + dot(value_weight[at, :], block_ref[:, query_cols + kv_cols :], 1, 1)
        )
        return carry

    lax.fori_loop(0, full_ref.shape[0] // tile, step, 0)
    half, rows = give_refs[0].shape
    own = pl.ds(pl.multiple_of(core_ref[0] * half, 8), half)
    other = pl.ds(pl.multiple_of((1 - core_ref[0]) * half, 8), half)
    for i, (keep_ref, give_ref) in enumerate(zip(keep_refs, give_refs)):
        cols = slice(i * rows, (i + 1) * rows)
        keep_ref[...] = full_ref[own, cols].astype(jnp.bfloat16)
        give_ref[...] = full_ref[other, cols].astype(jnp.bfloat16)


def project(blocks, weights, core, light):
    width = weights[0].shape[0]
    rows = sum(block[0].shape[0] for block in blocks)
    half = (width // 2, rows // len(blocks))
    cols = sum(weight.shape[1] for weight in weights)
    tile = max(t for t in range(16, 449, 16) if width % t == 0)
    flat = [piece for block in blocks for piece in block]
    whole = pl.BlockSpec(memory_space=pltpu.VMEM)
    return pl.pallas_call(
        functools.partial(project_kernel, [len(block) for block in blocks], tile),
        out_shape=[jax.ShapeDtypeStruct(half, jnp.bfloat16)] * (2 * len(blocks)),
        in_specs=[pl.BlockSpec(memory_space=pltpu.SMEM)] + [whole] * (len(flat) + 3),
        out_specs=[whole] * (2 * len(blocks)),
        scratch_shapes=[
            pltpu.VMEM((width, rows), jnp.float32),
            pltpu.VMEM((rows, cols), jnp.bfloat16),
        ],
        compiler_params=pltpu.CompilerParams(vmem_limit_bytes=8 * 1024 * 1024),
        cost_estimate=pl.CostEstimate(
            flops=1 if light else 2 * rows * width * cols,
            bytes_accessed=1 if light else 2 * width * cols + 6 * width * rows,
            transcendentals=0,
        ),
    )(core, *flat, *weights)


def moved(block, axis, by):
    size = lax.axis_size(axis)
    return lax.ppermute(block, axis, [(i, i + by) for i in range(size) if 0 <= i + by < size])


def swapped(block, axis, first):
    pairs = []
    for i in range(first, lax.axis_size(axis) - 1, 2):
        pairs += [(i, i + 1), (i + 1, i)]
    return lax.ppermute(block, axis, pairs)


def after(arrays, *others):
    return lax.optimization_barrier((*arrays, *others))[: len(arrays)]


def passed_along(block, axis, distance):
    devices = range(lax.axis_size(axis))
    return lax.ppermute(block, axis, [((i - distance) % len(devices), i) for i in devices])


def per_device(
    query_rows,
    key_row_matrix,
    value_row_matrix,
    out_grad,
    w_query,
    key_weight,
    value_weight,
    doc_ids,
):
    documents = doc_ids[0]
    tokens = documents.shape[0]
    rows = query_rows.shape[1]
    kv_cols = key_row_matrix.shape[2]
    shards = lax.axis_size("seq")
    place = lax.axis_index("seq")
    back = min(WINDOW, tokens // 3) - 1
    halo_rows = []
    while sum(halo_rows) < back and len(halo_rows) < shards - 1:
        halo_rows.append(min(rows, -(-(back - sum(halo_rows)) // 16) * 16))
    kv = lax.optimization_barrier(
        jnp.concatenate([key_row_matrix[0], value_row_matrix[0]], axis=1)
    )
    halos = [moved(kv[rows - size :], "seq", d) for d, size in enumerate(halo_rows, 1)]
    reach = sum(halo_rows)
    first_row = place * rows
    key_docs = lax.dynamic_slice_in_dim(
        jnp.concatenate([jnp.full((reach,), -1, jnp.int32), documents]), first_row, reach + rows, 0
    )
    query_docs = lax.dynamic_slice_in_dim(documents, first_row, rows, 0)
    offset = (
        jnp.arange(rows, dtype=jnp.int32)[None, :]
        + reach
        - jnp.arange(reach + rows, dtype=jnp.int32)[:, None]
    )
    allowed = (query_docs[None, :] == key_docs[:, None]) & (offset >= 0) & (offset < WINDOW)
    bias = jnp.where(allowed, 0.0, MASKED).astype(jnp.float32)
    kv_heads = kv_cols // HEAD_WIDTH
    query_stack, grad_stack = stack(
        *after((query_rows[0], out_grad[0]), kv), kv_heads, query_rows.shape[2] // kv_cols
    )
    grad_query, grad_kv, *grad_halos = attention_backward(
        query_stack, grad_stack, kv, bias, halos[::-1]
    )
    returned = [moved(part, "seq", -d) for d, part in enumerate(grad_halos[::-1], 1)]
    own = join(grad_query, grad_kv, returned)
    weights = (w_query[0], key_weight[0], value_weight[0])
    core = lax.axis_index("mp").astype(jnp.int32)

    def halves_summed(blocks, late, before=(), light=False):
        halves = project([(block,) for block in blocks], weights, core[None], light)
        sums = []
        for keep, give in zip(halves[: len(blocks)], halves[len(blocks) :]):
            if before:
                (give,) = after((give,), *before)
            got = passed_along(give, "mp", 1)
            if late:
                (got,) = after((got,), *late)
            sums.append((keep.astype(jnp.float32) + got.astype(jnp.float32)).astype(jnp.bfloat16))
        return sums

    even = place % 2 == 0
    results, waiting, hops = [], [own], []

    def hop(blocks):
        came = passed_along(jnp.concatenate(blocks, axis=1), "section", -1)
        hops.append([came])
        return [came[:, i * rows : (i + 1) * rows] for i in range(len(blocks))]

    by_first, by_second = own, own
    for step in range(1, shards):
        came_first = swapped(by_first, "seq", 0)
        last = step == shards - 1 and shards % 2 == 0
        came_second = came_first if last else swapped(by_second, "seq", 1)
        if step > 1:
            waiting = after(waiting, *sums, *(hops[-2] if step > 2 else ()))
        late = (came_first, came_second) if step > 1 else ()
        if step > 2 and last:
            late = hops[-1]
        sums = halves_summed(waiting, late, light=step > 2 and last)
        results.append(hop(sums))
        by_first, by_second = came_second, came_first
        if last:
            waiting = [came_first]
        elif 2 * step < shards:
            waiting = [came_first, came_second]
        else:
            waiting = [jnp.where(even == (place >= step), came_second, came_first)]
    sums = halves_summed(waiting, (), sum(hops[-2:], []))
    results.append(hop(sums))
    for step, blocks in enumerate(results):
        if len(blocks) > 1:
            first, second = blocks
            results[step] = [jnp.where(even, second, first), jnp.where(even, first, second)]
    upstream = jnp.zeros((results[0][0].shape[0], tokens), jnp.bfloat16)
    for s in range(shards):
        behind = results[s][0]
        ahead = results[(shards - s) % shards][-1]
        block = jnp.where(place >= s, behind, ahead)
        upstream = lax.dynamic_update_slice_in_dim(
            upstream, block, ((place - s) % shards) * rows, 1
        )
    return upstream.T[None]


def solution(mesh):
    placed = P("section", "seq", "mp")
    return jax.shard_map(
        per_device,
        mesh=mesh,
        in_specs=(placed,) * 7 + (P("section", None),),
        out_specs=P("section", None, ("seq", "mp")),
        check_vma=False,
    )
```
